32 devices in a mesh: req: 8 (over z, y), mp: 4 (over x, core).
Axes of the slice: x: 2, y: 2, z: 4, core: 2. Of those that a mesh axis runs over, the one named last changes fastest.
Arguments:
- q_pre: bfloat16 [4096, 3072], P('req', 'mp'), may hold values from -64 to 64
- k_pre: bfloat16 [4096, 1024], P('req', 'mp'), may hold values from -64 to 64
- v_pre: bfloat16 [4096, 1024], P('req', 'mp'), may hold values from -12 to 12
- q_bias: float32 [3072], P('mp'), may hold values from -3 to 3
- k_bias: float32 [1024], P('mp'), may hold values from -3 to 3
- v_bias: float32 [1024], P('mp'), may hold values from -3 to 3
- segment_ids: int32 [4096], P('req'), may hold values from -1 to 31, as said below
- lengths: int32 [8, 4], replicated, may hold values from 64 to 128, as said below
- page_table: int32 [8, 4], replicated, may hold values from 0 to 31, as said below
- w_out: bfloat16 [3072, 5120], P('mp'), may hold values from -0.109375 to 0.109375
- residual: bfloat16 [4096, 5120], P('req'), may hold values from -4 to 4
- norm_gain: float32 [5120], replicated, may hold values from 0.1 to 1.9
- w_gate: bfloat16 [5120, 6912], P('req', 'mp'), may hold values from -0.078125 to 0.078125
- w_up: bfloat16 [5120, 6912], P('req', 'mp'), may hold values from -0.078125 to 0.078125
Outputs:
- hidden: bfloat16 [4096, 6912], P('req', 'mp')
- kv_cache: bfloat16 [32, 8, 128, 256], P('req', 'mp')
The draws below stay inside these ranges and needn't reach their ends.
Inputs may be any that keep to these rules, and one draw needn't show every extreme that they name: Requests of block r lie in order from the block's first token, request j taking lengths[r, j] tokens; in every block one request has exactly 128 tokens. `segment_ids`: token t of block r carries r * 4 + j inside request j's run of tokens given by lengths, and -1 after the last request of its block. `page_table`: every page is named once; page p is held by req index p // 4; the requests of one block have pages held by different req indices.
All inputs are finite; a program needn't handle non-finite values.
Results may differ from the reference program's by a relative error of at most 0.019.
Values may be sent and summed in bfloat16 or wider, within the bound.
No kernel may reach another device: no remote copies, remote signals or barrier semaphores. Data moves between devices by JAX's collectives and lax.ppermute only.
A program may use at most 128 MiB of HBM per device.

```python
import math
import jax
import jax.numpy as jnp
from jax import lax

D = 5120
KVH = 8
HD = 128
QH = 24
FF = 6912
PAGE = 128
REQS = 4
BLOCK = 512
TOKENS = 4096
PAGES = 32
N_REQ = 8
N_MP = 4


def layout(key):
    base = jax.random.fold_in(key, 5)
    key_len = jax.random.fold_in(base, 0)
    key_long = jax.random.fold_in(base, 1)
    key_owner = jax.random.fold_in(base, 3)
    key_slot = jax.random.fold_in(base, 4)
    length_table = jax.random.randint(key_len, (N_REQ, REQS), PAGE // 2, PAGE + 1)
    longest = jax.random.randint(key_long, (N_REQ, 1), 0, REQS)
    length_table = jnp.where(jnp.arange(REQS)[None, :] == longest, PAGE, length_table).astype(jnp.int32)
    owner_order = jax.random.permutation(key_owner, N_REQ)
    owner_ids = owner_order[(jnp.arange(N_REQ)[:, None] + jnp.arange(REQS)[None, :]) % N_REQ]
    rotation = jax.random.randint(key_slot, (N_REQ,), 0, REQS)
    slot_ids = (jnp.arange(REQS)[None, :] + rotation[owner_ids]) % REQS
    page_ids = (owner_ids * REQS + slot_ids).astype(jnp.int32)
    return (length_table, page_ids)


def draw_lengths(key, part):
    return layout(key)[0]


def draw_page_table(key, part):
    return layout(key)[1]


def draw_segment_ids(key, part):
    length_table = layout(key)[0]
    starts = jnp.cumsum(length_table, axis=1) - length_table
    row_ids = jnp.arange(BLOCK)[None, :, None]
    inside = (row_ids >= starts[:, None, :]) & (row_ids < (starts + length_table)[:, None, :])
    request_ids = jnp.arange(N_REQ)[:, None, None] * REQS + jnp.arange(REQS)[None, None, :]
    segment = jnp.max(jnp.where(inside, request_ids, -1), axis=2)
    return segment.reshape(TOKENS).astype(jnp.int32)


def fields(key):
    base = jax.random.fold_in(key, 9)
    key_query, key_key = jax.random.split(base, 2)
    queries = jax.random.normal(key_query, (TOKENS, QH * HD), jnp.float32)
    keys = jax.random.normal(key_key, (TOKENS, KVH * HD), jnp.float32)
    return (queries, keys)


def draw_q_pre(key, part):
    return fields(key)[0].astype(jnp.bfloat16)


def draw_k_pre(key, part):
    return fields(key)[1].astype(jnp.bfloat16)


def steps_of(key, shape, shards, least, largest):
    def one(dim, shards_of):
        heights = jax.random.uniform(jax.random.fold_in(jax.random.fold_in(key, 6), dim), (shards_of,), jnp.float32, least / len(shards), largest / len(shards))
        return jnp.repeat(jnp.exp(heights), shape[dim] // shards_of).reshape((-1,) + (1,) * (len(shape) - dim - 1))

    gain = one(*shards[0])
    for cut in shards[1:]:
        gain = gain * one(*cut)
    return gain


def centred(rng, extent, deviation, reach, shards=(), kind=jnp.bfloat16):
    entries = deviation * jax.random.normal(rng, extent, jnp.float32)
    if shards:
        entries = entries * steps_of(rng, extent, shards, -0.22, 0.18)
    return jnp.clip(entries, -reach, reach).astype(kind)


def setup_inputs(seed: int = 0) -> dict:
    splits = jax.random.split(jax.random.key(seed), 15)
    q_pre = draw_q_pre(jax.random.fold_in(splits[14], 71), 0)
    k_pre = draw_k_pre(jax.random.fold_in(splits[14], 71), 0)
    v_pre = centred(splits[2], (TOKENS, KVH * HD), 2.0, 12.0, ((0, 8), (1, 4)))
    q_bias = centred(splits[3], (QH * HD,), 0.5, 3.0, ((0, 4),), jnp.float32)
    k_bias = centred(splits[4], (KVH * HD,), 0.5, 3.0, ((0, 4),), jnp.float32)
    v_bias = centred(splits[5], (KVH * HD,), 0.5, 3.0, ((0, 4),), jnp.float32)
    segment_ids = draw_segment_ids(jax.random.fold_in(splits[14], 71), 0)
    lengths = draw_lengths(jax.random.fold_in(splits[14], 71), 0)
    page_table = draw_page_table(jax.random.fold_in(splits[14], 71), 0)
    w_out = centred(splits[9], (QH * HD, D), (QH * HD) ** -0.5, 0.109375, ((0, 4),))
    residual = centred(splits[10], (TOKENS, D), 0.5, 4.0, ((0, 8),))
    norm_gain = jnp.clip(1.0 + 0.18 * jax.random.normal(splits[11], (D,), jnp.float32), 0.1, 1.9)
    w_gate = centred(splits[12], (D, FF), D ** -0.5, 0.078125, ((0, 8), (1, 4)))
    w_up = centred(splits[13], (D, FF), D ** -0.5, 0.078125, ((0, 8), (1, 4)))
    return {"q_pre": q_pre, "k_pre": k_pre, "v_pre": v_pre, "q_bias": q_bias, "k_bias": k_bias, "v_bias": v_bias, "segment_ids": segment_ids, "lengths": lengths, "page_table": page_table, "w_out": w_out, "residual": residual, "norm_gain": norm_gain, "w_gate": w_gate, "w_up": w_up}


THETA = 1000000.0
EPS = 1e-06

def rotate(values, positions):
    half_dim = values.shape[-1] // 2
    frequencies = THETA ** (-jnp.arange(half_dim, dtype=jnp.float32) * (2.0 / values.shape[-1]))
    angles = positions[:, None] * frequencies[None, :]
    cosine = jnp.cos(angles)[:, None, :]
    sine_part = jnp.sin(angles)[:, None, :]
    first_half = values[..., :half_dim]
    second = values[..., half_dim:]
    return jnp.concatenate([first_half * cosine - second * sine_part, second * cosine + first_half * sine_part], axis=-1)

def reference(q_pre, k_pre, v_pre, q_bias, k_bias, v_bias, segment_ids, lengths, page_table, w_out, residual, norm_gain, w_gate, w_up):
    group_size = QH // KVH
    head_cols = QH * HD // N_MP
    scale_factor = 1.0 / math.sqrt(HD)

    def one_block(inputs):
        block_idx, q_rows, k_rows, v_rows, seg_rows, lens_row, resid_rows = inputs
        starts = jnp.cumsum(lens_row) - lens_row
        alive_rows = seg_rows >= 0
        req_idx = jnp.clip(seg_rows - block_idx * REQS, 0, REQS - 1).astype(jnp.int32)
        positions = (jnp.arange(BLOCK, dtype=jnp.int32) - jnp.take(starts, req_idx)).astype(jnp.float32)
        queries = rotate((q_rows.astype(jnp.float32) + q_bias).reshape(BLOCK, QH, HD), positions)
        queries = jnp.where(alive_rows[:, None, None], queries, 0.0).astype(jnp.bfloat16)
        keyrot = rotate((k_rows.astype(jnp.float32) + k_bias).reshape(BLOCK, KVH, HD), positions)
        keyrot = jnp.where(alive_rows[:, None, None], keyrot, 0.0).astype(jnp.bfloat16)
        valrows = (v_rows.astype(jnp.float32) + v_bias).reshape(BLOCK, KVH, HD)
        valrows = jnp.where(alive_rows[:, None, None], valrows, 0.0).astype(jnp.bfloat16)
        scores = jnp.einsum('qhge,khe->hgqk', queries.reshape(BLOCK, KVH, group_size, HD).astype(jnp.float32), keyrot.astype(jnp.float32)) * scale_factor
        allowed = (seg_rows[:, None] == seg_rows[None, :]) & alive_rows[None, :] & (positions[None, :] <= positions[:, None])
        allowed = allowed[None, None]
        row_max = lax.optimization_barrier(jnp.max(jnp.where(allowed, scores, -1e+30), axis=-1, keepdims=True))
        weights = jnp.where(allowed, jnp.exp(scores - row_max), 0.0)
        row_sum = lax.optimization_barrier(jnp.sum(weights, axis=-1, keepdims=True))
        present = alive_rows[None, None, :, None]
        row_probs = jnp.where(present, weights / jnp.where(present, row_sum, 1.0), 0.0).astype(jnp.bfloat16)
        attended = jnp.einsum('hgqk,khe->qhge', row_probs.astype(jnp.float32), valrows.astype(jnp.float32)).astype(jnp.bfloat16).reshape(BLOCK, QH * HD)
        summed = jnp.zeros((BLOCK, D), jnp.float32)
        for member in range(N_MP):
            product = jnp.dot(attended[:, member * head_cols:(member + 1) * head_cols], w_out[member * head_cols:(member + 1) * head_cols], preferred_element_type=jnp.float32)
            summed = summed + lax.optimization_barrier(product.astype(jnp.bfloat16)).astype(jnp.float32)
        state = resid_rows.astype(jnp.float32) + summed
        normed = (state * lax.rsqrt(lax.optimization_barrier(jnp.mean(state * state, axis=-1, keepdims=True)) + EPS) * norm_gain).astype(jnp.bfloat16)
        gate_acc = jnp.dot(normed, w_gate, preferred_element_type=jnp.float32)
        up_acc = jnp.dot(normed, w_up, preferred_element_type=jnp.float32)
        hidden_rows = (jax.nn.silu(gate_acc) * up_acc).astype(jnp.bfloat16)
        row_index = jnp.clip(starts[:, None] + jnp.arange(PAGE, dtype=jnp.int32)[None, :], 0, BLOCK - 1).astype(jnp.int32)
        inside = (jnp.arange(PAGE, dtype=jnp.int32)[None, :] < lens_row[:, None])[:, :, None, None]
        page_keys = jnp.where(inside, keyrot[row_index], jnp.zeros((), jnp.bfloat16))
        page_vals = jnp.where(inside, valrows[row_index], jnp.zeros((), jnp.bfloat16))
        page_rows = jnp.concatenate([page_keys, page_vals], axis=-1).transpose(0, 2, 1, 3)
        return (hidden_rows, page_rows)
    hidden_all, pages_all = lax.map(one_block, (jnp.arange(N_REQ, dtype=jnp.int32), q_pre.reshape(N_REQ, BLOCK, QH * HD), k_pre.reshape(N_REQ, BLOCK, KVH * HD), v_pre.reshape(N_REQ, BLOCK, KVH * HD), segment_ids.reshape(N_REQ, BLOCK), lengths, residual.reshape(N_REQ, BLOCK, D)))
    cache_all = jnp.zeros((PAGES, KVH, PAGE, 2 * HD), jnp.bfloat16)
    cache_all = cache_all.at[page_table.reshape(-1)].set(pages_all.reshape(PAGES, KVH, PAGE, 2 * HD))
    return (hidden_all.reshape(TOKENS, FF), cache_all)
```

```python
import math

import jax
import jax.numpy as jnp
from jax import lax
from jax.experimental import pallas as pl
from jax.experimental.pallas import tpu as pltpu
from jax.sharding import PartitionSpec as P

HD = 128
PAGE = 128
REQS = 4
CORES = 2
THETA = 1000000.0
EPS = 1e-06
NT = (((1,), (1,)), ((), ()))


def rope_tables(positions):
    half_dim = HD // 2
    frequencies = THETA ** (-jnp.arange(half_dim, dtype=jnp.float32) * (2.0 / HD))
    angles = positions[:, None] * frequencies[None, :]
    cosine = jnp.cos(angles)
    sine = jnp.sin(angles)
    return jnp.concatenate([cosine, cosine], axis=-1), jnp.concatenate([-sine, sine], axis=-1)


def attention_kernel(q_ref, k_ref, v_ref, qb_ref, kb_ref, vb_ref, cos_ref, sin_ref, segc_ref, segr_ref,
                     slot_ref, out_ref, send_ref, q_buf, k_buf, v_buf, kv_buf):
    rows = q_ref.shape[0]
    kv_heads = k_ref.shape[1] // HD
    q_heads = q_ref.shape[1] // HD
    group = q_heads // kv_heads
    live = segc_ref[...] >= 0
    cosine = cos_ref[...]
    sine = sin_ref[...]

    def turned(source, bias, head):
        cols = slice(head * HD, (head + 1) * HD)
        raw = source[:, cols].astype(jnp.float32) + bias[:, cols]
        return jnp.where(live, raw * cosine + pltpu.roll(raw, HD // 2, 1) * sine, 0.0).astype(jnp.bfloat16)

    for head in range(q_heads):
        q_buf[:, head * HD:(head + 1) * HD] = turned(q_ref, qb_ref, head)
    for head in range(kv_heads):
        cols = slice(head * HD, (head + 1) * HD)
        key = turned(k_ref, kb_ref, head)
        value = jnp.where(live, v_ref[:, cols].astype(jnp.float32) + vb_ref[:, cols], 0.0).astype(jnp.bfloat16)
        k_buf[:, cols] = key
        v_buf[:, cols] = value
        kv_buf[:, 2 * head * HD:(2 * head + 1) * HD] = key
        kv_buf[:, (2 * head + 1) * HD:(2 * head + 2) * HD] = value
    slots = slot_ref[...]
    for part in range(send_ref.shape[0] // rows):
        wanted = lax.broadcasted_iota(jnp.int32, (rows, rows), 0) + part * rows
        pick = jnp.where(wanted == slots, 1.0, 0.0).astype(jnp.bfloat16)
        send_ref[part * rows:(part + 1) * rows, :] = jnp.dot(
            pick, kv_buf[...], preferred_element_type=jnp.float32
        ).astype(jnp.bfloat16)
    scale = 1.0 / math.sqrt(HD)
    tile = PAGE
    for start in range(0, rows, tile):
        low = max(0, start - tile)
        high = start + tile
        seg_q = segc_ref[start:high, :]
        seg_k = segr_ref[:, low:high]
        row_at = lax.broadcasted_iota(jnp.int32, (tile, high - low), 0) + start
        col_at = lax.broadcasted_iota(jnp.int32, (tile, high - low), 1) + low
        allowed = (seg_q == seg_k) & (seg_k >= 0) & (col_at <= row_at)
        for head in range(q_heads):
            kv = head // group
            kv_cols = slice(kv * HD, (kv + 1) * HD)
            scores = lax.dot_general(
                q_buf[start:high, head * HD:(head + 1) * HD], k_buf[low:high, kv_cols], NT,
                preferred_element_type=jnp.float32,
            ) * scale
            row_max = jnp.max(jnp.where(allowed, scores, -1e30), axis=-1, keepdims=True)
            weights = jnp.where(allowed, jnp.exp(scores - row_max), 0.0)
            total = jnp.sum(weights, axis=-1, keepdims=True)
            probs = (weights / jnp.where(total > 0.0, total, 1.0)).astype(jnp.bfloat16)
            out_ref[start:high, head * HD:(head + 1) * HD] = jnp.dot(
                probs, v_buf[low:high, kv_cols], preferred_element_type=jnp.float32
            ).astype(jnp.bfloat16)


def attention(q_pre, k_pre, v_pre, q_bias, k_bias, v_bias, cosine, sine, segs, slots, slot_count):
    rows, q_cols = q_pre.shape
    kv_cols = k_pre.shape[1]
    vmem = pl.BlockSpec(memory_space=pltpu.VMEM)
    return pl.pallas_call(
        attention_kernel,
        out_shape=(
            jax.ShapeDtypeStruct((rows, q_cols), jnp.bfloat16),
            jax.ShapeDtypeStruct((slot_count, 2 * kv_cols), jnp.bfloat16),
        ),
        in_specs=[vmem] * 11,
        out_specs=(vmem, vmem),
        scratch_shapes=[
            pltpu.VMEM((rows, q_cols), jnp.bfloat16),
            pltpu.VMEM((rows, kv_cols), jnp.bfloat16),
            pltpu.VMEM((rows, kv_cols), jnp.bfloat16),
            pltpu.VMEM((rows, 2 * kv_cols), jnp.bfloat16),
        ],
        compiler_params=pltpu.CompilerParams(vmem_limit_bytes=32 * 2**20),
        cost_estimate=pl.CostEstimate(flops=2 * 10**9, bytes_accessed=4 * 2**20, transcendentals=10**6),
        name="attention",
    )(q_pre, k_pre, v_pre, q_bias[None], k_bias[None], v_bias[None], cosine, sine, segs[:, None], segs[None],
      slots[None])


def cache_kernel(source_ref, in_ref, out_ref):
    out_ref[0, 0] = in_ref[0]


def write_cache(sources, pages_in, kv_heads):
    grid_spec = pltpu.PrefetchScalarGridSpec(
        num_scalar_prefetch=1,
        grid=(REQS, kv_heads),
        in_specs=[pl.BlockSpec((1, PAGE, 2 * HD), lambda page, head, source: (source[page], 0, head))],
        out_specs=pl.BlockSpec((1, 1, PAGE, 2 * HD), lambda page, head, source: (page, head, 0, 0)),
    )
    return pl.pallas_call(
        cache_kernel,
        out_shape=jax.ShapeDtypeStruct((REQS, kv_heads, PAGE, 2 * HD), jnp.bfloat16),
        grid_spec=grid_spec,
        name="write_cache",
    )(sources, pages_in)


def mlp_kernel(count, pieces, ids_ref, *refs):
    weights = refs[:count]
    rows_in = refs[count:count + pieces]
    out_ref, gate_buf, up_buf, row_buf, weight_sems, row_sems = refs[count + pieces:]
    depth = weights[0].shape[2]
    piece = rows_in[0].shape[0]
    copies = []
    for index in range(pieces):
        at = pl.multiple_of(ids_ref[count + index] * piece, piece)
        copies.append(pltpu.make_async_copy(rows_in[index], row_buf.at[pl.ds(at, piece), :], row_sems.at[index]))
    for index in range(count):
        at = pl.multiple_of(ids_ref[index] * depth, depth)
        for which, buf in enumerate((gate_buf, up_buf)):
            copies.append(
                pltpu.make_async_copy(
                    weights[index].at[which], buf.at[:, pl.ds(at, depth)], weight_sems.at[which, index]
                )
            )
    for copy in copies:
        copy.start()
    for copy in copies:
        copy.wait()
    tile = min(256, out_ref.shape[1])
    for start in range(0, out_ref.shape[1], tile):
        block = row_buf[start:start + tile, :]
        gate = lax.dot_general(gate_buf[...], block, NT, preferred_element_type=jnp.float32)
        up = lax.dot_general(up_buf[...], block, NT, preferred_element_type=jnp.float32)
        out_ref[:, start:start + tile] = (gate / (1.0 + jnp.exp(-gate)) * up).astype(jnp.bfloat16)


def mlp_block(weights, weight_ids, rows_in, row_ids):
    count, pieces = len(weights), len(rows_in)
    units, depth = weights[0].shape[1:]
    piece, width = rows_in[0].shape
    tokens = piece * pieces
    if depth % 128 or units % 16 or piece % 16:
        both = jnp.zeros((2, units, width), jnp.bfloat16)
        for index in range(count):
            both = lax.dynamic_update_slice(both, weights[index], (0, 0, weight_ids[index] * depth))
        rows = jnp.zeros((tokens, width), jnp.bfloat16)
        for index in range(pieces):
            rows = lax.dynamic_update_slice(rows, rows_in[index], (row_ids[index] * piece, 0))
        gate = lax.dot_general(both[0], rows, NT, preferred_element_type=jnp.float32)
        up = lax.dot_general(both[1], rows, NT, preferred_element_type=jnp.float32)
        return (jax.nn.silu(gate) * up).astype(jnp.bfloat16)
    ids = jnp.stack([jnp.asarray(i, jnp.int32) for i in list(weight_ids) + list(row_ids)])
    anywhere = pl.BlockSpec(memory_space=pl.ANY)
    return pl.pallas_call(
        lambda *refs: mlp_kernel(count, pieces, *refs),
        out_shape=jax.ShapeDtypeStruct((units, tokens), jnp.bfloat16),
        in_specs=[pl.BlockSpec(memory_space=pltpu.SMEM)] + [anywhere] * (count + pieces),
        out_specs=pl.BlockSpec(memory_space=pltpu.VMEM),
        scratch_shapes=[
            pltpu.VMEM((units, width), jnp.bfloat16),
            pltpu.VMEM((units, width), jnp.bfloat16),
            pltpu.VMEM((tokens, width), jnp.bfloat16),
            pltpu.SemaphoreType.DMA((2, count)),
            pltpu.SemaphoreType.DMA((pieces,)),
        ],
        compiler_params=pltpu.CompilerParams(vmem_limit_bytes=48 * 2**20),
        cost_estimate=pl.CostEstimate(
            flops=4 * units * width * tokens,
            bytes_accessed=2 * (2 * units * width + tokens * width + units * tokens),
            transcendentals=units * tokens,
        ),
        name="mlp_block",
    )(ids, *weights, *rows_in)


def shards(q_pre, k_pre, v_pre, q_bias, k_bias, v_bias, segment_ids, lengths, page_table, w_out, residual,
           norm_gain, w_gate, w_up):
    me_req = lax.axis_index("req")
    me_mp = lax.axis_index("mp")
    n_req = lax.axis_size("req")
    n_mp = lax.axis_size("mp")
    n_z = 4 if n_req % 4 == 0 else 1
    n_y = n_req // n_z
    n_x = n_mp // CORES
    z = me_req // n_y
    y = me_req % n_y
    x = me_mp // CORES
    core = me_mp % CORES

    def along_z(value, shift):
        pairs = [(a * n_y + b, (a + shift) % n_z * n_y + b) for a in range(n_z) for b in range(n_y)]
        return lax.ppermute(value, "req", pairs)

    def along_y(value, shift):
        pairs = [(a * n_y + b, a * n_y + (b + shift) % n_y) for a in range(n_z) for b in range(n_y)]
        return lax.ppermute(value, "req", pairs)

    def along_x(value, shift):
        pairs = [(a * CORES + b, (a + shift) % n_x * CORES + b) for a in range(n_x) for b in range(CORES)]
        return lax.ppermute(value, "mp", pairs)

    def across_cores(value):
        pairs = [(a * CORES + b, a * CORES + 1 - b) for a in range(n_x) for b in range(CORES)]
        return lax.ppermute(value, "mp", pairs)

    units_all, depth = w_gate.shape[1], w_gate.shape[0]
    units = units_all // n_z
    gate_t, up_t = w_gate.T, w_up.T

    def share(target):
        at = (target * units, 0)
        return jnp.stack(
            [lax.dynamic_slice(gate_t, at, (units, depth)), lax.dynamic_slice(up_t, at, (units, depth))]
        )

    weights, weight_ids = [], []

    def arrived(chunk, shift):
        source_z = (z - shift) % n_z
        weights.append(chunk)
        weight_ids.append(source_z * n_y + y)
        for step in range(1, n_y):
            weights.append(along_y(chunk, step))
            weight_ids.append(source_z * n_y + (y - step) % n_y)

    arrived(share(z), 0)
    last = None
    shifts = [n_z // 2] + [s for s in range(1, n_z) if s != n_z // 2]
    for shift in shifts if n_z > 1 else []:
        chunk = share((z + shift) % n_z)
        if last is not None:
            chunk, last = lax.optimization_barrier((chunk, last))
        last = along_z(chunk, shift)
        arrived(last, shift)

    rows = q_pre.shape[0]
    kv_heads = k_pre.shape[1] // HD
    own_lens = lax.dynamic_index_in_dim(lengths, me_req, 0, keepdims=False)
    own_pages = lax.dynamic_index_in_dim(page_table, me_req, 0, keepdims=False)
    own_owner = own_pages // REQS
    starts = jnp.cumsum(own_lens) - own_lens
    alive = segment_ids >= 0
    req_idx = jnp.clip(segment_ids - me_req * REQS, 0, REQS - 1)
    hit = req_idx[:, None] == jnp.arange(REQS)[None, :]
    row_start = jnp.sum(jnp.where(hit, starts[None, :], 0), axis=1)
    row_owner = jnp.sum(jnp.where(hit, own_owner[None, :], 0), axis=1)
    row_pos = jnp.arange(rows, dtype=jnp.int32) - row_start
    slots = jnp.where(alive, row_owner * PAGE + row_pos, -1)
    cosine, sine = rope_tables(row_pos.astype(jnp.float32))
    attended, kv_send = attention(
        q_pre, k_pre, v_pre, q_bias, k_bias, v_bias, cosine, sine, segment_ids, slots, n_req * PAGE
    )
    partial = jnp.dot(attended, w_out, preferred_element_type=jnp.float32).astype(jnp.bfloat16)
    width = partial.shape[1]
    piece = rows // n_mp
    parts = lax.all_to_all(partial.reshape(n_mp, piece, width), "mp", split_axis=0, concat_axis=0, tiled=True)
    summed = jnp.sum(parts.astype(jnp.float32), axis=0)
    state = lax.dynamic_slice(residual, (me_mp * piece, 0), (piece, width)).astype(jnp.float32) + summed
    scale = lax.rsqrt(jnp.mean(state * state, axis=-1, keepdims=True) + EPS)
    normed = (state * scale * norm_gain).astype(jnp.bfloat16)

    kv_in = lax.all_to_all(
        kv_send.reshape(n_req, PAGE, 2 * kv_heads * HD), "req", split_axis=0, concat_axis=0, tiled=True
    )
    mine = page_table[None] == (me_req * REQS + jnp.arange(REQS, dtype=jnp.int32))[:, None, None]
    sources = jnp.sum(jnp.where(mine, jnp.arange(n_req, dtype=jnp.int32)[None, :, None], 0), axis=(1, 2))
    cache_out = write_cache(sources.astype(jnp.int32), kv_in, kv_heads)

    def spread(own):
        across = [(own, x)] + [(along_x(own, step), (x - step) % n_x) for step in range(1, n_x)]
        pieces = [(value, at * CORES + core) for value, at in across]
        pieces += [(across_cores(value), at * CORES + 1 - core) for value, at in across]
        return [p[0] for p in pieces], [p[1] for p in pieces]

    normed, last = lax.optimization_barrier((normed, last)) if last is not None else (normed, None)
    hidden_t = jnp.zeros((units_all, rows), jnp.bfloat16)
    block = normed
    for step in range(n_z):
        if step:
            block = along_z(block, 1)
        values, at = spread(block)
        done = mlp_block(weights, weight_ids, values, at)
        if step:
            done = along_z(done, -step)
        hidden_t = lax.dynamic_update_slice(hidden_t, done, ((z + step) % n_z * units, 0))
    return hidden_t.T, cache_out


def solution(mesh):
    in_specs = (
        P("req", "mp"),
        P("req", "mp"),
        P("req", "mp"),
        P("mp"),
        P("mp"),
        P("mp"),
        P("req"),
        P(),
        P(),
        P("mp", None),
        P("req", None),
        P(),
        P("req", "mp"),
        P("req", "mp"),
    )
    out_specs = (P("req", "mp"), P("req", "mp", None, None))
    return jax.shard_map(shards, mesh=mesh, in_specs=in_specs, out_specs=out_specs, check_vma=False)
```

```python
import math

import jax
import jax.numpy as jnp
from jax import lax
from jax.experimental import pallas as pl
from jax.experimental.pallas import tpu as pltpu
from jax.sharding import PartitionSpec as P

HD = 128
PAGE = 128
REQS = 4
CORES = 2
N_Z = 4
THETA = 1000000.0
EPS = 1e-06
NT = (((1,), (1,)), ((), ()))


def rope_tables(positions):
    half_dim = HD // 2
    frequencies = THETA ** (-jnp.arange(half_dim, dtype=jnp.float32) * (2.0 / HD))
    angles = positions[:, None] * frequencies[None, :]
    cosine = jnp.cos(angles)
    sine = jnp.sin(angles)
    return jnp.concatenate([cosine, cosine], axis=-1), jnp.concatenate([-sine, sine], axis=-1)


def attention_kernel(order, q_ref, k_ref, v_ref, qb_ref, kb_ref, vb_ref, cos_ref, sin_ref, segc_ref, segr_ref,
                     slot_ref, out_ref, send_ref, q_buf, k_buf, v_buf, kv_buf):
    rows = q_ref.shape[0]
    kv_heads = k_ref.shape[1] // HD
    q_heads = q_ref.shape[1] // HD
    group = q_heads // kv_heads
    live = segc_ref[...] >= 0
    cosine = cos_ref[...]
    sine = sin_ref[...]

    def turned(source, bias, head):
        cols = slice(head * HD, (head + 1) * HD)
        raw = source[:, cols].astype(jnp.float32) + bias[:, cols]
        return jnp.where(live, raw * cosine + pltpu.roll(raw, HD // 2, 1) * sine, 0.0).astype(jnp.bfloat16)

    for head in range(q_heads):
        q_buf[:, head * HD:(head + 1) * HD] = turned(q_ref, qb_ref, head)
    for head in range(kv_heads):
        cols = slice(head * HD, (head + 1) * HD)
        key = turned(k_ref, kb_ref, head)
        value = jnp.where(live, v_ref[:, cols].astype(jnp.float32) + vb_ref[:, cols], 0.0).astype(jnp.bfloat16)
        k_buf[:, cols] = key
        v_buf[:, cols] = value
        kv_buf[:, 2 * head * HD:(2 * head + 1) * HD] = key
        kv_buf[:, (2 * head + 1) * HD:(2 * head + 2) * HD] = value
    slots = slot_ref[...]
    for part in range(send_ref.shape[0] // rows):
        wanted = lax.broadcasted_iota(jnp.int32, (rows, rows), 0) + part * rows
        pick = jnp.where(wanted == slots, 1.0, 0.0).astype(jnp.bfloat16)
        send_ref[part * rows:(part + 1) * rows, :] = jnp.dot(
            pick, kv_buf[...], preferred_element_type=jnp.float32
        ).astype(jnp.bfloat16)
    scale = 1.0 / math.sqrt(HD)
    tile = PAGE
    for start in range(0, rows, tile):
        low = max(0, start - tile)
        high = start + tile
        seg_q = segc_ref[start:high, :]
        seg_k = segr_ref[:, low:high]
        row_at = lax.broadcasted_iota(jnp.int32, (tile, high - low), 0) + start
        col_at = lax.broadcasted_iota(jnp.int32, (tile, high - low), 1) + low
        allowed = (seg_q == seg_k) & (seg_k >= 0) & (col_at <= row_at)
        for head in range(q_heads):
            kv = head // group
            kv_cols = slice(kv * HD, (kv + 1) * HD)
            scores = lax.dot_general(
                q_buf[start:high, head * HD:(head + 1) * HD], k_buf[low:high, kv_cols], NT,
                preferred_element_type=jnp.float32,
            ) * scale
            row_max = jnp.max(jnp.where(allowed, scores, -1e30), axis=-1, keepdims=True)
            weights = jnp.where(allowed, jnp.exp(scores - row_max), 0.0)
            total = jnp.sum(weights, axis=-1, keepdims=True)
            probs = (weights / jnp.where(total > 0.0, total, 1.0)).astype(jnp.bfloat16)
            mixed = jnp.dot(
                probs, v_buf[low:high, kv_cols], preferred_element_type=jnp.float32
            ).astype(jnp.bfloat16)
            size = rows // len(order)
            for at in range(0, tile, size):
                to = order[(start + at) // size] * size
                out_ref[to:to + size, head * HD:(head + 1) * HD] = mixed[at:at + size]


def attention(q_pre, k_pre, v_pre, q_bias, k_bias, v_bias, cosine, sine, segs, slots, slot_count, order):
    rows, q_cols = q_pre.shape
    kv_cols = k_pre.shape[1]
    vmem = pl.BlockSpec(memory_space=pltpu.VMEM)
    return pl.pallas_call(
        lambda *refs: attention_kernel(order, *refs),
        out_shape=(
            jax.ShapeDtypeStruct((rows, q_cols), jnp.bfloat16),
            jax.ShapeDtypeStruct((slot_count, 2 * kv_cols), jnp.bfloat16),
        ),
        in_specs=[vmem] * 11,
        out_specs=(vmem, vmem),
        scratch_shapes=[
            pltpu.VMEM((rows, q_cols), jnp.bfloat16),
            pltpu.VMEM((rows, kv_cols), jnp.bfloat16),
            pltpu.VMEM((rows, kv_cols), jnp.bfloat16),
            pltpu.VMEM((rows, 2 * kv_cols), jnp.bfloat16),
        ],
        compiler_params=pltpu.CompilerParams(vmem_limit_bytes=32 * 2**20),
        cost_estimate=pl.CostEstimate(flops=3 * 10**10, bytes_accessed=4 * 2**20, transcendentals=10**6),
        name="attention",
    )(q_pre, k_pre, v_pre, q_bias[None], k_bias[None], v_bias[None], cosine, sine, segs[:, None], segs[None],
      slots[None])


def cache_kernel(source_ref, in_ref, out_ref):
    out_ref[0, 0] = in_ref[0]


def write_cache(sources, pages_in, kv_heads):
    grid_spec = pltpu.PrefetchScalarGridSpec(
        num_scalar_prefetch=1,
        grid=(REQS, kv_heads),
        in_specs=[pl.BlockSpec((1, PAGE, 2 * HD), lambda page, head, source: (source[page], 0, head))],
        out_specs=pl.BlockSpec((1, 1, PAGE, 2 * HD), lambda page, head, source: (page, head, 0, 0)),
    )
    return pl.pallas_call(
        cache_kernel,
        out_shape=jax.ShapeDtypeStruct((REQS, kv_heads, PAGE, 2 * HD), jnp.bfloat16),
        grid_spec=grid_spec,
        name="write_cache",
    )(sources, pages_in)


def mlp_kernel(count, pieces, halves, ids_ref, *refs):
    weights = refs[:count]
    rows_in = refs[count:count + pieces]
    out_ref, gate_buf, up_buf, row_buf, weight_sems, row_sems = refs[count + pieces:]
    depth = weights[0].shape[2]
    piece = rows_in[0].shape[0] // halves
    copies = []
    for index in range(pieces):
        for half in range(halves):
            at = pl.multiple_of((half * pieces + ids_ref[count + index]) * piece, piece)
            copies.append(
                pltpu.make_async_copy(
                    rows_in[index].at[pl.ds(half * piece, piece), :],
                    row_buf.at[pl.ds(at, piece), :],
                    row_sems.at[index, half],
                )
            )
    for index in range(count):
        at = pl.multiple_of(ids_ref[index] * depth, depth)
        for which, buf in enumerate((gate_buf, up_buf)):
            copies.append(
                pltpu.make_async_copy(
                    weights[index].at[which], buf.at[:, pl.ds(at, depth)], weight_sems.at[which, index]
                )
            )
    for copy in copies:
        copy.start()
    for copy in copies:
        copy.wait()
    tile = min(256, out_ref.shape[1])
    for start in range(0, out_ref.shape[1], tile):
        block = row_buf[start:start + tile, :]
        gate = lax.dot_general(gate_buf[...], block, NT, preferred_element_type=jnp.float32)
        up = lax.dot_general(up_buf[...], block, NT, preferred_element_type=jnp.float32)
        out_ref[:, start:start + tile] = (gate / (1.0 + jnp.exp(-gate)) * up).astype(jnp.bfloat16)


def mlp_block(weights, weight_ids, rows_in, row_ids, halves):
    count, pieces = len(weights), len(rows_in)
    units, depth = weights[0].shape[1:]
    width = rows_in[0].shape[1]
    piece = rows_in[0].shape[0] // halves
    tokens = piece * pieces * halves
    if depth % 128 or units % 16 or piece % 16:
        both = jnp.zeros((2, units, width), jnp.bfloat16)
        for index in range(count):
            both = lax.dynamic_update_slice(both, weights[index], (0, 0, weight_ids[index] * depth))
        rows = jnp.zeros((tokens, width), jnp.bfloat16)
        for index in range(pieces):
            for half in range(halves):
                at = (half * pieces + row_ids[index]) * piece
                rows = lax.dynamic_update_slice(rows, rows_in[index][half * piece:(half + 1) * piece], (at, 0))
        gate = lax.dot_general(both[0], rows, NT, preferred_element_type=jnp.float32)
        up = lax.dot_general(both[1], rows, NT, preferred_element_type=jnp.float32)
        return (jax.nn.silu(gate) * up).astype(jnp.bfloat16)
    ids = jnp.stack([jnp.asarray(i, jnp.int32) for i in list(weight_ids) + list(row_ids)])
    anywhere = pl.BlockSpec(memory_space=pl.ANY)
    return pl.pallas_call(
        lambda *refs: mlp_kernel(count, pieces, halves, *refs),
        out_shape=jax.ShapeDtypeStruct((units, tokens), jnp.bfloat16),
        in_specs=[pl.BlockSpec(memory_space=pltpu.SMEM)] + [anywhere] * (count + pieces),
        out_specs=pl.BlockSpec(memory_space=pltpu.VMEM),
        scratch_shapes=[
            pltpu.VMEM((units, width), jnp.bfloat16),
            pltpu.VMEM((units, width), jnp.bfloat16),
            pltpu.VMEM((tokens, width), jnp.bfloat16),
            pltpu.SemaphoreType.DMA((2, count)),
            pltpu.SemaphoreType.DMA((pieces, halves)),
        ],
        compiler_params=pltpu.CompilerParams(vmem_limit_bytes=32 * 2**20),
        cost_estimate=pl.CostEstimate(
            flops=4 * units * width * tokens,
            bytes_accessed=2 * (2 * units * width + tokens * width + units * tokens),
            transcendentals=units * tokens,
        ),
        name="mlp_block",
    )(ids, *weights, *rows_in)


def after(value, *before):
    return lax.optimization_barrier((value,) + before)[0]


def shards(q_pre, k_pre, v_pre, q_bias, k_bias, v_bias, segment_ids, lengths, page_table, w_out, residual,
           norm_gain, w_gate, w_up):
    me_req = lax.axis_index("req")
    me_mp = lax.axis_index("mp")
    n_req = lax.axis_size("req")
    n_mp = lax.axis_size("mp")
    n_y = n_req // N_Z
    n_x = n_mp // CORES
    z = me_req // n_y
    y = me_req % n_y
    x = me_mp // CORES
    core = me_mp % CORES

    def along_z(value, moves):
        return lax.ppermute(value, "req", [(a * n_y + c, b * n_y + c) for a, b in moves for c in range(n_y)])

    def turn_z(value, shift):
        return along_z(value, [(a, (a + shift) % N_Z) for a in range(N_Z)])

    def along_y(value):
        return [
            lax.ppermute(
                value, "req", [(a * n_y + b, a * n_y + (b + step) % n_y) for a in range(N_Z) for b in range(n_y)]
            )
            for step in range(1, n_y)
        ]

    def along_x(value):
        return [
            lax.ppermute(
                value,
                "mp",
                [(a * CORES + b, (a + step) % n_x * CORES + b) for a in range(n_x) for b in range(CORES)],
            )
            for step in range(1, n_x)
        ]

    def across_cores(value):
        return lax.ppermute(
            value, "mp", [(a * CORES + b, a * CORES + 1 - b) for a in range(n_x) for b in range(CORES)]
        )

    units_all, depth = w_gate.shape[1], w_gate.shape[0]
    units = units_all // N_Z

    def share(gate_t, up_t, target):
        at = (target * units, 0)
        return jnp.stack(
            [lax.dynamic_slice(gate_t, at, (units, depth)), lax.dynamic_slice(up_t, at, (units, depth))]
        )

    def source_ids(shift):
        source_z = (z - shift) % N_Z
        return [source_z * n_y + (y - step) % n_y for step in range(n_y)]

    gate_t, up_t = w_gate.T, w_up.T
    first = share(gate_t, up_t, (z + 2) % N_Z)
    gate_t, up_t, first, q_pre, segment_ids = lax.optimization_barrier((gate_t, up_t, first, q_pre, segment_ids))
    own = share(gate_t, up_t, z)
    from_2 = turn_z(first, 2)
    own_y = along_y(own)
    from_1 = turn_z(after(share(gate_t, up_t, (z + 1) % N_Z), from_2, *own_y), 1)
    from_2_y = along_y(from_2)
    from_3 = turn_z(after(share(gate_t, up_t, (z + 3) % N_Z), from_1, *from_2_y), 3)
    from_1_y = along_y(from_1)

    rows = q_pre.shape[0]
    kv_heads = k_pre.shape[1] // HD
    own_lens = lax.dynamic_index_in_dim(lengths, me_req, 0, keepdims=False)
    own_pages = lax.dynamic_index_in_dim(page_table, me_req, 0, keepdims=False)
    own_owner = own_pages // REQS
    starts = jnp.cumsum(own_lens) - own_lens
    alive = segment_ids >= 0
    req_idx = jnp.clip(segment_ids - me_req * REQS, 0, REQS - 1)
    hit = req_idx[:, None] == jnp.arange(REQS)[None, :]
    row_start = jnp.sum(jnp.where(hit, starts[None, :], 0), axis=1)
    row_owner = jnp.sum(jnp.where(hit, own_owner[None, :], 0), axis=1)
    row_pos = jnp.arange(rows, dtype=jnp.int32) - row_start
    slots = jnp.where(alive, row_owner * PAGE + row_pos, -1)
    cosine, sine = rope_tables(row_pos.astype(jnp.float32))
    order = [group % n_mp * 2 + group // n_mp for group in range(2 * n_mp)]
    attended, kv_send = attention(
        q_pre, k_pre, v_pre, q_bias, k_bias, v_bias, cosine, sine, segment_ids, slots, n_req * PAGE, order
    )
    partial = jnp.dot(attended, w_out, preferred_element_type=jnp.float32).astype(jnp.bfloat16)
    width = partial.shape[1]
    run = rows // n_mp // 2
    parts = lax.all_to_all(partial.reshape(n_mp, 2 * run, width), "mp", split_axis=0, concat_axis=0, tiled=True)
    summed = jnp.sum(parts.astype(jnp.float32), axis=0)
    residual_rows = jnp.concatenate(
        [
            lax.dynamic_slice(residual, (me_mp * run, 0), (run, width)),
            lax.dynamic_slice(residual, (rows // 2 + me_mp * run, 0), (run, width)),
        ]
    )
    state = residual_rows.astype(jnp.float32) + summed
    scale = lax.rsqrt(jnp.mean(state * state, axis=-1, keepdims=True) + EPS)
    normed = (state * scale * norm_gain).astype(jnp.bfloat16)

    row_ids = [(x - step) % n_x * CORES + core for step in range(n_x)]
    row_ids += [(x - step) % n_x * CORES + 1 - core for step in range(n_x)]
    normed_x = along_x(normed)
    normed = after(normed, from_3, *from_1_y)
    from_3_y = along_y(from_3)
    up_1 = along_z(normed, [(0, 1), (1, 2), (2, 3)])
    down_1 = along_z(normed, [(1, 0), (2, 1), (3, 2)])
    up_1, down_1, *_ = lax.optimization_barrier((up_1, down_1, *from_3_y, *normed_x))
    up_2 = along_z(up_1, [(1, 2), (2, 3)])
    down_2 = along_z(down_1, [(1, 0), (2, 1)])
    block_1 = jnp.where(z % 2 == 0, down_1, up_1)
    block_1_x = along_x(block_1)
    up_2, down_2, *_ = lax.optimization_barrier((up_2, down_2, *block_1_x))
    up_3a = along_z(up_2[:run], [(2, 3)])
    down_3a = along_z(down_2[:run], [(1, 0)])
    block_2 = jnp.where(z < 2, down_2, up_2)
    block_2_x = along_x(block_2)
    kv_send = after(kv_send, up_2, down_2)
    up_3a, down_3a = lax.optimization_barrier((up_3a, down_3a))
    up_3b = along_z(after(up_2[run:], up_3a, down_3a), [(2, 3)])
    down_3b = along_z(after(down_2[run:], up_3a, down_3a), [(1, 0)])

    def last_block(half, up, down):
        at = slice(half * run, (half + 1) * run)
        return jnp.where(z == 0, down, jnp.where(z == 3, up, jnp.where(z == 1, down_1[at], up_1[at])))

    block_3a = after(last_block(0, up_3a, down_3a), *block_2_x)
    block_3b = last_block(1, up_3b, down_3b)
    block_3a_x = along_x(block_3a)
    block_3b_x = along_x(after(block_3b, *block_3a_x))

    weights = [own, *own_y, from_2, *from_2_y, from_1, *from_1_y, from_3, *from_3_y]
    weight_ids = [i for shift in (0, 2, 1, 3) for i in source_ids(shift)]

    def work(block, block_x, halves):
        pieces = [block, *block_x]
        return mlp_block(weights, weight_ids, pieces + [across_cores(p) for p in pieces], row_ids, halves)

    hidden_t = jnp.zeros((units_all, rows), jnp.bfloat16)
    hidden_t = lax.dynamic_update_slice(hidden_t, work(normed, normed_x, 2), (z * units, 0))
    for flip, half, block, block_x in (
        (1, 0, block_1, block_1_x),
        (2, 0, block_2, block_2_x),
        (3, 0, block_3a, block_3a_x),
        (3, 1, block_3b, block_3b_x),
    ):
        done = work(block, block_x, block.shape[0] // run)
        done = along_z(done, [(a, a ^ flip) for a in range(N_Z)])
        hidden_t = lax.dynamic_update_slice(hidden_t, done, ((z ^ flip) * units, half * (rows // 2)))

    kv_in = lax.all_to_all(
        kv_send.reshape(n_req, PAGE, 2 * kv_heads * HD), "req", split_axis=0, concat_axis=0, tiled=True
    )
    mine = page_table[None] == (me_req * REQS + jnp.arange(REQS, dtype=jnp.int32))[:, None, None]
    sources = jnp.sum(jnp.where(mine, jnp.arange(n_req, dtype=jnp.int32)[None, :, None], 0), axis=(1, 2))
    cache_out = write_cache(sources.astype(jnp.int32), kv_in, kv_heads)
    return hidden_t.T, cache_out


def solution(mesh):
    in_specs = (
        P("req", "mp"),
        P("req", "mp"),
        P("req", "mp"),
        P("mp"),
        P("mp"),
        P("mp"),
        P("req"),
        P(),
        P(),
        P("mp", None),
        P("req", None),
        P(),
        P("req", "mp"),
        P("req", "mp"),
    )
    out_specs = (P("req", "mp"), P("req", "mp", None, None))
    return jax.shard_map(shards, mesh=mesh, in_specs=in_specs, out_specs=out_specs, check_vma=False)
```

```python
import math

import jax
import jax.numpy as jnp
from jax import lax
from jax.experimental import pallas as pl
from jax.experimental.pallas import tpu as pltpu
from jax.sharding import PartitionSpec as P

HD = 128
PAGE = 128
REQS = 4
CORES = 2
N_Z = 4
THETA = 1000000.0
EPS = 1e-06
NT = (((1,), (1,)), ((), ()))


def rope_tables(positions):
    half_dim = HD // 2
    frequencies = THETA ** (-jnp.arange(half_dim, dtype=jnp.float32) * (2.0 / HD))
    angles = positions[:, None] * frequencies[None, :]
    cosine = jnp.cos(angles)
    sine = jnp.sin(angles)
    return jnp.concatenate([cosine, cosine], axis=-1), jnp.concatenate([-sine, sine], axis=-1)


def attention_kernel(order, q_ref, k_ref, v_ref, qb_ref, kb_ref, vb_ref, cos_ref, sin_ref, segc_ref, segr_ref,
                     slot_ref, out_ref, send_ref, q_buf, k_buf, v_buf, kv_buf):
    rows = q_ref.shape[0]
    kv_heads = k_ref.shape[1] // HD
    q_heads = q_ref.shape[1] // HD
    group = q_heads // kv_heads
    live = segc_ref[...] >= 0
    cosine = cos_ref[...]
    sine = sin_ref[...]

    def turned(source, bias, head):
        cols = slice(head * HD, (head + 1) * HD)
        raw = source[:, cols].astype(jnp.float32) + bias[:, cols]
        return jnp.where(live, raw * cosine + pltpu.roll(raw, HD // 2, 1) * sine, 0.0).astype(jnp.bfloat16)

    for head in range(q_heads):
        q_buf[:, head * HD:(head + 1) * HD] = turned(q_ref, qb_ref, head)
    for head in range(kv_heads):
        cols = slice(head * HD, (head + 1) * HD)
        key = turned(k_ref, kb_ref, head)
        value = jnp.where(live, v_ref[:, cols].astype(jnp.float32) + vb_ref[:, cols], 0.0).astype(jnp.bfloat16)
        k_buf[:, cols] = key
        v_buf[:, cols] = value
        kv_buf[:, 2 * head * HD:(2 * head + 1) * HD] = key
        kv_buf[:, (2 * head + 1) * HD:(2 * head + 2) * HD] = value
    slots = slot_ref[...]
    for part in range(send_ref.shape[0] // rows):
        wanted = lax.broadcasted_iota(jnp.int32, (rows, rows), 0) + part * rows
        pick = jnp.where(wanted == slots, 1.0, 0.0).astype(jnp.bfloat16)
        send_ref[part * rows:(part + 1) * rows, :] = jnp.dot(
            pick, kv_buf[...], preferred_element_type=jnp.float32
        ).astype(jnp.bfloat16)
    scale = 1.0 / math.sqrt(HD)
    tile = PAGE
    for start in range(0, rows, tile):
        low = max(0, start - tile)
        high = start + tile
        seg_q = segc_ref[start:high, :]
        seg_k = segr_ref[:, low:high]
        row_at = lax.broadcasted_iota(jnp.int32, (tile, high - low), 0) + start
        col_at = lax.broadcasted_iota(jnp.int32, (tile, high - low), 1) + low
        allowed = (seg_q == seg_k) & (seg_k >= 0) & (col_at <= row_at)
        for head in range(q_heads):
            kv = head // group
            kv_cols = slice(kv * HD, (kv + 1) * HD)
            scores = lax.dot_general(
                q_buf[start:high, head * HD:(head + 1) * HD], k_buf[low:high, kv_cols], NT,
                preferred_element_type=jnp.float32,
            ) * scale
            row_max = jnp.max(jnp.where(allowed, scores, -1e30), axis=-1, keepdims=True)
            weights = jnp.where(allowed, jnp.exp(scores - row_max), 0.0)
            total = jnp.sum(weights, axis=-1, keepdims=True)
            probs = (weights / jnp.where(total > 0.0, total, 1.0)).astype(jnp.bfloat16)
            mixed = jnp.dot(
                probs, v_buf[low:high, kv_cols], preferred_element_type=jnp.float32
            ).astype(jnp.bfloat16)
            size = rows // len(order)
            for at in range(0, tile, size):
                to = order[(start + at) // size] * size
                out_ref[to:to + size, head * HD:(head + 1) * HD] = mixed[at:at + size]


def attention(q_pre, k_pre, v_pre, q_bias, k_bias, v_bias, cosine, sine, segs, slots, slot_count, order):
    rows, q_cols = q_pre.shape
    kv_cols = k_pre.shape[1]
    vmem = pl.BlockSpec(memory_space=pltpu.VMEM)
    return pl.pallas_call(
        lambda *refs: attention_kernel(order, *refs),
        out_shape=(
            jax.ShapeDtypeStruct((rows, q_cols), jnp.bfloat16),
            jax.ShapeDtypeStruct((slot_count, 2 * kv_cols), jnp.bfloat16),
        ),
        in_specs=[vmem] * 11,
        out_specs=(vmem, vmem),
        scratch_shapes=[
            pltpu.VMEM((rows, q_cols), jnp.bfloat16),
            pltpu.VMEM((rows, kv_cols), jnp.bfloat16),
            pltpu.VMEM((rows, kv_cols), jnp.bfloat16),
            pltpu.VMEM((rows, 2 * kv_cols), jnp.bfloat16),
        ],
        compiler_params=pltpu.CompilerParams(vmem_limit_bytes=32 * 2**20),
        cost_estimate=pl.CostEstimate(flops=10**8, bytes_accessed=2**16, transcendentals=0),
        name="attention",
    )(q_pre, k_pre, v_pre, q_bias[None], k_bias[None], v_bias[None], cosine, sine, segs[:, None], segs[None],
      slots[None])


def cache_kernel(source_ref, in_ref, out_ref):
    out_ref[0, 0] = in_ref[0]


def write_cache(sources, pages_in, kv_heads):
    grid_spec = pltpu.PrefetchScalarGridSpec(
        num_scalar_prefetch=1,
        grid=(REQS, kv_heads),
        in_specs=[pl.BlockSpec((1, PAGE, 2 * HD), lambda page, head, source: (source[page], 0, head))],
        out_specs=pl.BlockSpec((1, 1, PAGE, 2 * HD), lambda page, head, source: (page, head, 0, 0)),
    )
    return pl.pallas_call(
        cache_kernel,
        out_shape=jax.ShapeDtypeStruct((REQS, kv_heads, PAGE, 2 * HD), jnp.bfloat16),
        grid_spec=grid_spec,
        name="write_cache",
    )(sources, pages_in)


def mlp_kernel(count, pieces, halves, ids_ref, *refs):
    weights = (refs[:count], refs[count:2 * count])
    rows_in = refs[2 * count:2 * count + pieces * halves]
    out_ref, gate_buf, up_buf, row_buf, weight_sems, row_sems = refs[2 * count + pieces * halves:]
    depth = weights[0][0].shape[1]
    piece = rows_in[0].shape[0]
    copies = []
    for half in range(halves):
        for index in range(pieces):
            at = pl.multiple_of((half * pieces + ids_ref[count + index]) * piece, piece)
            copies.append(
                pltpu.make_async_copy(
                    rows_in[half * pieces + index], row_buf.at[pl.ds(at, piece), :], row_sems.at[half, index]
                )
            )
    for index in range(count):
        at = pl.multiple_of(ids_ref[index] * depth, depth)
        for which, buf in enumerate((gate_buf, up_buf)):
            copies.append(
                pltpu.make_async_copy(
                    weights[which][index], buf.at[:, pl.ds(at, depth)], weight_sems.at[which, index]
                )
            )
    for copy in copies:
        copy.start()
    for copy in copies:
        copy.wait()
    tile = min(256, out_ref.shape[1])
    for start in range(0, out_ref.shape[1], tile):
        block = row_buf[start:start + tile, :]
        gate = lax.dot_general(gate_buf[...], block, NT, preferred_element_type=jnp.float32)
        up = lax.dot_general(up_buf[...], block, NT, preferred_element_type=jnp.float32)
        out_ref[:, start:start + tile] = (gate / (1.0 + jnp.exp(-gate)) * up).astype(jnp.bfloat16)


def mlp_block(weights, weight_ids, rows_in, row_ids):
    count, halves, pieces = len(weight_ids), len(rows_in), len(row_ids)
    units, depth = weights[0].shape
    piece, width = rows_in[0][0].shape
    tokens = piece * pieces * halves
    if depth % 128 or units % 16 or piece % 16:
        both = jnp.zeros((2, units, width), jnp.bfloat16)
        for index in range(count):
            pair = jnp.stack([weights[index], weights[count + index]])
            both = lax.dynamic_update_slice(both, pair, (0, 0, weight_ids[index] * depth))
        rows = jnp.zeros((tokens, width), jnp.bfloat16)
        for half in range(halves):
            for index in range(pieces):
                at = (half * pieces + row_ids[index]) * piece
                rows = lax.dynamic_update_slice(rows, rows_in[half][index], (at, 0))
        gate = lax.dot_general(both[0], rows, NT, preferred_element_type=jnp.float32)
        up = lax.dot_general(both[1], rows, NT, preferred_element_type=jnp.float32)
        return (jax.nn.silu(gate) * up).astype(jnp.bfloat16)
    ids = jnp.stack([jnp.asarray(i, jnp.int32) for i in list(weight_ids) + list(row_ids)])
    anywhere = pl.BlockSpec(memory_space=pl.ANY)
    return pl.pallas_call(
        lambda *refs: mlp_kernel(count, pieces, halves, *refs),
        out_shape=jax.ShapeDtypeStruct((units, tokens), jnp.bfloat16),
        in_specs=[pl.BlockSpec(memory_space=pltpu.SMEM)] + [anywhere] * (2 * count + pieces * halves),
        out_specs=pl.BlockSpec(memory_space=pltpu.VMEM),
        scratch_shapes=[
            pltpu.VMEM((units, width), jnp.bfloat16),
            pltpu.VMEM((units, width), jnp.bfloat16),
            pltpu.VMEM((tokens, width), jnp.bfloat16),
            pltpu.SemaphoreType.DMA((2, count)),
            pltpu.SemaphoreType.DMA((halves, pieces)),
        ],
        compiler_params=pltpu.CompilerParams(vmem_limit_bytes=32 * 2**20),
        cost_estimate=pl.CostEstimate(flops=10**8, bytes_accessed=2**16, transcendentals=0),
        name="mlp_block",
    )(ids, *weights, *[value for half in rows_in for value in half])


def after(value, *before):
    return lax.optimization_barrier((value,) + before)[0]


def shards(q_pre, k_pre, v_pre, q_bias, k_bias, v_bias, segment_ids, lengths, page_table, w_out, residual,
           norm_gain, w_gate, w_up):
    me_req = lax.axis_index("req")
    me_mp = lax.axis_index("mp")
    n_req = lax.axis_size("req")
    n_mp = lax.axis_size("mp")
    n_y = n_req // N_Z
    n_x = n_mp // CORES
    z = me_req // n_y
    y = me_req % n_y
    x = me_mp // CORES
    core = me_mp % CORES

    def along_z(value, moves):
        return lax.ppermute(value, "req", [(a * n_y + c, b * n_y + c) for a, b in moves for c in range(n_y)])

    def turn_z(value, shift):
        return along_z(value, [(a, (a + shift) % N_Z) for a in range(N_Z)])

    def along_y(value):
        return [
            lax.ppermute(
                value, "req", [(a * n_y + b, a * n_y + (b + step) % n_y) for a in range(N_Z) for b in range(n_y)]
            )
            for step in range(1, n_y)
        ]

    def along_x(value):
        return [
            lax.ppermute(
                value,
                "mp",
                [(a * CORES + b, (a + step) % n_x * CORES + b) for a in range(n_x) for b in range(CORES)],
            )
            for step in range(1, n_x)
        ]

    def across_cores(value):
        return lax.ppermute(
            value, "mp", [(a * CORES + b, a * CORES + 1 - b) for a in range(n_x) for b in range(CORES)]
        )

    units_all, depth = w_gate.shape[1], w_gate.shape[0]
    units = units_all // N_Z

    def share(weight_t, shift):
        return lax.dynamic_slice(weight_t, ((z + shift) % N_Z * units, 0), (units, depth))

    def source_ids(shift):
        source_z = (z - shift) % N_Z
        return [source_z * n_y + (y - step) % n_y for step in range(n_y)]

    gate_t, up_t = w_gate.T, w_up.T
    gate_2 = share(gate_t, 2)
    gate_t, up_t, gate_2, q_pre, segment_ids = lax.optimization_barrier((gate_t, up_t, gate_2, q_pre, segment_ids))
    gate_0, up_0 = share(gate_t, 0), share(up_t, 0)
    gate_2 = turn_z(gate_2, 2)
    gate_0_y, up_0_y = along_y(gate_0), along_y(up_0)

    rows = q_pre.shape[0]
    kv_heads = k_pre.shape[1] // HD
    own_lens = lax.dynamic_index_in_dim(lengths, me_req, 0, keepdims=False)
    own_pages = lax.dynamic_index_in_dim(page_table, me_req, 0, keepdims=False)
    own_owner = own_pages // REQS
    starts = jnp.cumsum(own_lens) - own_lens
    alive = segment_ids >= 0
    req_idx = jnp.clip(segment_ids - me_req * REQS, 0, REQS - 1)
    hit = req_idx[:, None] == jnp.arange(REQS)[None, :]
    row_start = jnp.sum(jnp.where(hit, starts[None, :], 0), axis=1)
    row_owner = jnp.sum(jnp.where(hit, own_owner[None, :], 0), axis=1)
    row_pos = jnp.arange(rows, dtype=jnp.int32) - row_start
    slots = jnp.where(alive, row_owner * PAGE + row_pos, -1)
    cosine, sine = rope_tables(row_pos.astype(jnp.float32))
    run = rows // n_mp // 2
    order = []
    for group in range(2 * n_mp):
        half, device = divmod(group, n_mp)
        order.append((device % CORES * n_x + device // CORES) * 2 + half)
    attended, kv_send = attention(
        q_pre, k_pre, v_pre, q_bias, k_bias, v_bias, cosine, sine, segment_ids, slots, n_req * PAGE, order
    )
    attended = attended.reshape(CORES, n_x * 2 * run, attended.shape[1])

    def project(which):
        picked = lax.dynamic_index_in_dim(attended, which, 0, keepdims=False)
        return jnp.dot(picked, w_out, preferred_element_type=jnp.float32).astype(jnp.bfloat16)

    kept, given = project(core), project(1 - core)
    up_2, gate_2, gate_0_y, up_0_y, kept, given = lax.optimization_barrier(
        (share(up_t, 2), gate_2, gate_0_y, up_0_y, kept, given)
    )
    up_2 = turn_z(up_2, 2)
    gate_2_y = along_y(gate_2)
    sibling = across_cores(given)
    width = sibling.shape[1]
    gate_1, up_2, gate_2_y, sibling = lax.optimization_barrier((share(gate_t, 1), up_2, gate_2_y, sibling))
    gate_1 = turn_z(gate_1, 1)
    up_2_y = along_y(up_2)
    pair = (kept.astype(jnp.float32) + sibling.astype(jnp.float32)).reshape(n_x, 2 * run, width)
    summed = lax.dynamic_index_in_dim(pair, x, 0, keepdims=False)
    outgoing = [
        lax.dynamic_index_in_dim(pair, (x + step) % n_x, 0, keepdims=False).astype(jnp.bfloat16)
        for step in range(1, n_x)
    ]
    gate_3, up_3, gate_1, up_2_y, outgoing = lax.optimization_barrier(
        (share(gate_t, 3), share(up_t, 3), gate_1, up_2_y, outgoing)
    )
    gate_3, up_3 = turn_z(gate_3, 3), turn_z(up_3, 3)
    gate_1_y = along_y(gate_1)
    incoming = [
        lax.ppermute(
            outgoing[step - 1],
            "mp",
            [(a * CORES + b, (a + step) % n_x * CORES + b) for a in range(n_x) for b in range(CORES)],
        )
        for step in range(1, n_x)
    ]
    up_1, gate_3, up_3, gate_1_y, incoming = lax.optimization_barrier(
        (share(up_t, 1), gate_3, up_3, gate_1_y, incoming)
    )
    up_1 = turn_z(up_1, 1)
    gate_3_y = along_y(gate_3)
    residual_rows = jnp.concatenate(
        [
            lax.dynamic_slice(residual, (me_mp * run, 0), (run, width)),
            lax.dynamic_slice(residual, (rows // 2 + me_mp * run, 0), (run, width)),
        ]
    )
    for other in incoming:
        summed = summed + other.astype(jnp.float32)
    state = residual_rows.astype(jnp.float32) + summed
    scale = lax.rsqrt(jnp.mean(state * state, axis=-1, keepdims=True) + EPS)
    normed = (state * scale * norm_gain).astype(jnp.bfloat16)
    near = [normed[:run], normed[run:]]
    near, up_1, gate_3_y = lax.optimization_barrier((near, up_1, gate_3_y))

    row_ids = [(x - step) % n_x * CORES + core for step in range(n_x)]
    row_ids += [(x - step) % n_x * CORES + 1 - core for step in range(n_x)]
    flip = [[(a, a ^ by) for a in range(N_Z)] for by in range(N_Z)]
    middle = [(1, 2), (2, 1)]
    outward = [(1, 0), (2, 3)]
    at_end = (z == 0) | (z == N_Z - 1)
    up_1_y, up_3_y = along_y(up_1), along_y(up_3)
    near_x = [along_x(half) for half in near]
    next_1 = [along_z(half, flip[1]) for half in near]
    middle_1 = [along_z(half, middle) for half in near]
    next_1, middle_1, up_1_y, up_3_y, near_x = lax.optimization_barrier((next_1, middle_1, up_1_y, up_3_y, near_x))
    next_2e = [along_z(half, outward) for half in middle_1]
    next_2m = [along_z(half, middle) for half in next_1]
    next_1_x = [along_x(half) for half in next_1]

    gates = [gate_0, *gate_0_y, gate_2, *gate_2_y, gate_1, *gate_1_y, gate_3, *gate_3_y]
    ups = [up_0, *up_0_y, up_2, *up_2_y, up_1, *up_1_y, up_3, *up_3_y]
    weights = gates + ups
    weight_ids = [i for shift in (0, 2, 1, 3) for i in source_ids(shift)]

    def work(halves, halves_x):
        pieces = []
        for half, half_x in zip(halves, halves_x):
            shared = [half, *half_x]
            pieces.append(shared + [across_cores(p) for p in shared])
        return mlp_block(weights, weight_ids, pieces, row_ids)

    hidden_0 = work(near, near_x)
    next_2e, next_2m, next_1_x, hidden_0 = lax.optimization_barrier((next_2e, next_2m, next_1_x, hidden_0))
    next_3 = [along_z(half, outward) for half in next_2m]
    next_2 = [jnp.where(at_end, e, m) for e, m in zip(next_2e, next_2m)]
    next_2_x = [along_x(half) for half in next_2]
    hidden_1 = work(next_1, next_1_x)
    next_3, next_2_x, hidden_1, kv_send = lax.optimization_barrier((next_3, next_2_x, hidden_1, kv_send))
    kv_in = lax.all_to_all(
        kv_send.reshape(n_req, PAGE, 2 * kv_heads * HD), "req", split_axis=0, concat_axis=0, tiled=True
    )
    next_3 = [jnp.where(at_end, e, m) for e, m in zip(next_3, middle_1)]
    next_3a_x = along_x(next_3[0])
    back_1 = along_z(hidden_1, flip[1])
    hidden_2 = work(next_2, next_2_x)
    next_3b, next_3a_x, hidden_2, kv_in = lax.optimization_barrier((next_3[1], next_3a_x, hidden_2, kv_in))
    next_3b_x = along_x(next_3b)
    back_2 = along_z(hidden_2, flip[2])
    back_3a = along_z(work([next_3[0]], [next_3a_x]), flip[3])
    back_3b = along_z(work([next_3b], [next_3b_x]), flip[3])
    hidden_t = jnp.zeros((units_all, rows), jnp.bfloat16)
    for by, at, done in (
        (0, 0, hidden_0),
        (1, 0, back_1),
        (2, 0, back_2),
        (3, 0, back_3a),
        (3, rows // 2, back_3b),
    ):
        hidden_t = lax.dynamic_update_slice(hidden_t, done, ((z ^ by) * units, at))

    mine = page_table[None] == (me_req * REQS + jnp.arange(REQS, dtype=jnp.int32))[:, None, None]
    sources = jnp.sum(jnp.where(mine, jnp.arange(n_req, dtype=jnp.int32)[None, :, None], 0), axis=(1, 2))
    cache_out = write_cache(sources.astype(jnp.int32), kv_in, kv_heads)
    return hidden_t.T, cache_out


def solution(mesh):
    in_specs = (
        P("req", "mp"),
        P("req", "mp"),
        P("req", "mp"),
        P("mp"),
        P("mp"),
        P("mp"),
        P("req"),
        P(),
        P(),
        P("mp", None),
        P("req", None),
        P(),
        P("req", "mp"),
        P("req", "mp"),
    )
    out_specs = (P("req", "mp"), P("req", "mp", None, None))
    return jax.shard_map(shards, mesh=mesh, in_specs=in_specs, out_specs=out_specs, check_vma=False)
```

```python
import math

import jax
import jax.numpy as jnp
from jax import lax
from jax.experimental import pallas as pl
from jax.experimental.pallas import tpu as pltpu
from jax.sharding import PartitionSpec as P

HD = 128
PAGE = 128
REQS = 4
CORES = 2
N_Z = 4
THETA = 1000000.0
EPS = 1e-06
NT = (((1,), (1,)), ((), ()))


def rope_tables(positions):
    half_dim = HD // 2
    frequencies = THETA ** (-jnp.arange(half_dim, dtype=jnp.float32) * (2.0 / HD))
    angles = positions[:, None] * frequencies[None, :]
    cosine = jnp.cos(angles)
    sine = jnp.sin(angles)
    return jnp.concatenate([cosine, cosine], axis=-1), jnp.concatenate([-sine, sine], axis=-1)


def attention_kernel(order, q_ref, k_ref, v_ref, qb_ref, kb_ref, vb_ref, cos_ref, sin_ref, segc_ref, segr_ref,
                     slot_ref, out_ref, send_ref, q_buf, k_buf, v_buf, kv_buf):
    rows = q_ref.shape[0]
    kv_heads = k_ref.shape[1] // HD
    q_heads = q_ref.shape[1] // HD
    group = q_heads // kv_heads
    live = segc_ref[...] >= 0
    cosine = cos_ref[...]
    sine = sin_ref[...]

    def turned(source, bias, head):
        cols = slice(head * HD, (head + 1) * HD)
        raw = source[:, cols].astype(jnp.float32) + bias[:, cols]
        return jnp.where(live, raw * cosine + pltpu.roll(raw, HD // 2, 1) * sine, 0.0).astype(jnp.bfloat16)

    for head in range(q_heads):
        q_buf[:, head * HD:(head + 1) * HD] = turned(q_ref, qb_ref, head)
    for head in range(kv_heads):
        cols = slice(head * HD, (head + 1) * HD)
        key = turned(k_ref, kb_ref, head)
        value = jnp.where(live, v_ref[:, cols].astype(jnp.float32) + vb_ref[:, cols], 0.0).astype(jnp.bfloat16)
        k_buf[:, cols] = key
        v_buf[:, cols] = value
        kv_buf[:, 2 * head * HD:(2 * head + 1) * HD] = key
        kv_buf[:, (2 * head + 1) * HD:(2 * head + 2) * HD] = value
    slots = slot_ref[...]
    for part in range(send_ref.shape[0] // rows):
        wanted = lax.broadcasted_iota(jnp.int32, (rows, rows), 0) + part * rows
        pick = jnp.where(wanted == slots, 1.0, 0.0).astype(jnp.bfloat16)
        send_ref[part * rows:(part + 1) * rows, :] = jnp.dot(
            pick, kv_buf[...], preferred_element_type=jnp.float32
        ).astype(jnp.bfloat16)
    scale = 1.0 / math.sqrt(HD)
    tile = PAGE
    for start in range(0, rows, tile):
        low = max(0, start - tile)
        high = start + tile
        seg_q = segc_ref[start:high, :]
        seg_k = segr_ref[:, low:high]
        row_at = lax.broadcasted_iota(jnp.int32, (tile, high - low), 0) + start
        col_at = lax.broadcasted_iota(jnp.int32, (tile, high - low), 1) + low
        allowed = (seg_q == seg_k) & (seg_k >= 0) & (col_at <= row_at)
        for head in range(q_heads):
            kv = head // group
            kv_cols = slice(kv * HD, (kv + 1) * HD)
            scores = lax.dot_general(
                q_buf[start:high, head * HD:(head + 1) * HD], k_buf[low:high, kv_cols], NT,
                preferred_element_type=jnp.float32,
            ) * scale
            row_max = jnp.max(jnp.where(allowed, scores, -1e30), axis=-1, keepdims=True)
            weights = jnp.where(allowed, jnp.exp(scores - row_max), 0.0)
            total = jnp.sum(weights, axis=-1, keepdims=True)
            probs = (weights / jnp.where(total > 0.0, total, 1.0)).astype(jnp.bfloat16)
            mixed = jnp.dot(
                probs, v_buf[low:high, kv_cols], preferred_element_type=jnp.float32
            ).astype(jnp.bfloat16)
            size = rows // len(order)
            for at in range(0, tile, size):
                to = order[(start + at) // size] * size
                out_ref[to:to + size, head * HD:(head + 1) * HD] = mixed[at:at + size]


def attention(q_pre, k_pre, v_pre, q_bias, k_bias, v_bias, cosine, sine, segs, slots, slot_count, order):
    rows, q_cols = q_pre.shape
    kv_cols = k_pre.shape[1]
    vmem = pl.BlockSpec(memory_space=pltpu.VMEM)
    return pl.pallas_call(
        lambda *refs: attention_kernel(order, *refs),
        out_shape=(
            jax.ShapeDtypeStruct((rows, q_cols), jnp.bfloat16),
            jax.ShapeDtypeStruct((slot_count, 2 * kv_cols), jnp.bfloat16),
        ),
        in_specs=[vmem] * 11,
        out_specs=(vmem, vmem),
        scratch_shapes=[
            pltpu.VMEM((rows, q_cols), jnp.bfloat16),
            pltpu.VMEM((rows, kv_cols), jnp.bfloat16),
            pltpu.VMEM((rows, kv_cols), jnp.bfloat16),
            pltpu.VMEM((rows, 2 * kv_cols), jnp.bfloat16),
        ],
        compiler_params=pltpu.CompilerParams(vmem_limit_bytes=32 * 2**20),
        cost_estimate=pl.CostEstimate(flops=10**8, bytes_accessed=2**16, transcendentals=0),
        name="attention",
    )(q_pre, k_pre, v_pre, q_bias[None], k_bias[None], v_bias[None], cosine, sine, segs[:, None], segs[None],
      slots[None])


def cache_kernel(source_ref, in_ref, out_ref):
    out_ref[0, 0] = in_ref[0]


def write_cache(sources, pages_in, kv_heads):
    grid_spec = pltpu.PrefetchScalarGridSpec(
        num_scalar_prefetch=1,
        grid=(REQS, kv_heads),
        in_specs=[pl.BlockSpec((1, PAGE, 2 * HD), lambda page, head, source: (source[page], 0, head))],
        out_specs=pl.BlockSpec((1, 1, PAGE, 2 * HD), lambda page, head, source: (page, head, 0, 0)),
    )
    return pl.pallas_call(
        cache_kernel,
        out_shape=jax.ShapeDtypeStruct((REQS, kv_heads, PAGE, 2 * HD), jnp.bfloat16),
        grid_spec=grid_spec,
        name="write_cache",
    )(sources, pages_in)


def mlp_kernel(count, pieces, halves, ids_ref, *refs):
    weights = (refs[:count], refs[count:2 * count])
    rows_in = refs[2 * count:2 * count + pieces]
    out_ref, gate_buf, up_buf, row_buf, acc, weight_sems, row_sems = refs[2 * count + pieces:]
    depth = weights[0][0].shape[1]
    piece = rows_in[0].shape[0] // halves
    first, second = [], []
    for index in range(pieces):
        for half in range(halves):
            at = pl.multiple_of((half * pieces + ids_ref[count + index]) * piece, piece)
            first.append(
                pltpu.make_async_copy(
                    rows_in[index].at[pl.ds(half * piece, piece), :],
                    row_buf.at[pl.ds(at, piece), :],
                    row_sems.at[index, half],
                )
            )
    for which, buf, copies in ((0, gate_buf, first), (1, up_buf, second)):
        for index in range(count):
            at = pl.multiple_of(ids_ref[index] * depth, depth)
            copies.append(
                pltpu.make_async_copy(weights[which][index], buf.at[:, pl.ds(at, depth)], weight_sems.at[which, index])
            )
    for copy in first + second:
        copy.start()
    tile = min(256, out_ref.shape[1])
    for copy in first:
        copy.wait()
    for start in range(0, out_ref.shape[1], tile):
        acc[:, start:start + tile] = lax.dot_general(
            gate_buf[...], row_buf[start:start + tile, :], NT, preferred_element_type=jnp.float32
        )
    for copy in second:
        copy.wait()
    for start in range(0, out_ref.shape[1], tile):
        up = lax.dot_general(up_buf[...], row_buf[start:start + tile, :], NT, preferred_element_type=jnp.float32)
        gate = acc[:, start:start + tile]
        out_ref[:, start:start + tile] = (gate / (1.0 + jnp.exp(-gate)) * up).astype(jnp.bfloat16)


def mlp_block(weights, weight_ids, rows_in, row_ids, halves):
    count, pieces = len(weight_ids), len(row_ids)
    units, depth = weights[0].shape
    width = rows_in[0].shape[1]
    piece = rows_in[0].shape[0] // halves
    tokens = piece * pieces * halves
    if depth % 128 or units % 16 or piece % 16:
        both = jnp.zeros((2, units, width), jnp.bfloat16)
        for index in range(count):
            pair = jnp.stack([weights[index], weights[count + index]])
            both = lax.dynamic_update_slice(both, pair, (0, 0, weight_ids[index] * depth))
        rows = jnp.zeros((tokens, width), jnp.bfloat16)
        for index in range(pieces):
            for half in range(halves):
                at = (half * pieces + row_ids[index]) * piece
                rows = lax.dynamic_update_slice(rows, rows_in[index][half * piece:(half + 1) * piece], (at, 0))
        gate = lax.dot_general(both[0], rows, NT, preferred_element_type=jnp.float32)
        up = lax.dot_general(both[1], rows, NT, preferred_element_type=jnp.float32)
        return (jax.nn.silu(gate) * up).astype(jnp.bfloat16)
    ids = jnp.stack([jnp.asarray(i, jnp.int32) for i in list(weight_ids) + list(row_ids)])
    anywhere = pl.BlockSpec(memory_space=pl.ANY)
    return pl.pallas_call(
        lambda *refs: mlp_kernel(count, pieces, halves, *refs),
        out_shape=jax.ShapeDtypeStruct((units, tokens), jnp.bfloat16),
        in_specs=[pl.BlockSpec(memory_space=pltpu.SMEM)] + [anywhere] * (2 * count + pieces),
        out_specs=pl.BlockSpec(memory_space=pltpu.VMEM),
        scratch_shapes=[
            pltpu.VMEM((units, width), jnp.bfloat16),
            pltpu.VMEM((units, width), jnp.bfloat16),
            pltpu.VMEM((tokens, width), jnp.bfloat16),
            pltpu.VMEM((units, tokens), jnp.float32),
            pltpu.SemaphoreType.DMA((2, count)),
            pltpu.SemaphoreType.DMA((pieces, halves)),
        ],
        compiler_params=pltpu.CompilerParams(vmem_limit_bytes=60 * 2**20),
        cost_estimate=pl.CostEstimate(flops=10**8, bytes_accessed=2**16, transcendentals=0),
        name="mlp_block",
    )(ids, *weights, *rows_in)


def after(value, *before):
    return lax.optimization_barrier((value,) + before)[0]


def shards(q_pre, k_pre, v_pre, q_bias, k_bias, v_bias, segment_ids, lengths, page_table, w_out, residual,
           norm_gain, w_gate, w_up):
    me_req = lax.axis_index("req")
    me_mp = lax.axis_index("mp")
    n_req = lax.axis_size("req")
    n_mp = lax.axis_size("mp")
    n_y = n_req // N_Z
    n_x = n_mp // CORES
    z = me_req // n_y
    y = me_req % n_y
    x = me_mp // CORES
    core = me_mp % CORES

    def along_z(value, moves):
        return lax.ppermute(value, "req", [(a * n_y + c, b * n_y + c) for a, b in moves for c in range(n_y)])

    def turn_z(value, shift):
        return along_z(value, [(a, (a + shift) % N_Z) for a in range(N_Z)])

    def along_y(value):
        return [
            lax.ppermute(
                value, "req", [(a * n_y + b, a * n_y + (b + step) % n_y) for a in range(N_Z) for b in range(n_y)]
            )
            for step in range(1, n_y)
        ]

    def along_x(value):
        return [
            lax.ppermute(
                value,
                "mp",
                [(a * CORES + b, (a + step) % n_x * CORES + b) for a in range(n_x) for b in range(CORES)],
            )
            for step in range(1, n_x)
        ]

    def across_cores(value):
        return lax.ppermute(
            value, "mp", [(a * CORES + b, a * CORES + 1 - b) for a in range(n_x) for b in range(CORES)]
        )

    units_all, depth = w_gate.shape[1], w_gate.shape[0]
    units = units_all // N_Z

    def share(weight_t, shift):
        return lax.dynamic_slice(weight_t, ((z + shift) % N_Z * units, 0), (units, depth))

    def source_ids(shift):
        source_z = (z - shift) % N_Z
        return [source_z * n_y + (y - step) % n_y for step in range(n_y)]

    gate_t, up_t = w_gate.T, w_up.T
    gate_2 = share(gate_t, 2)
    gate_t, up_t, gate_2, q_pre, segment_ids = lax.optimization_barrier((gate_t, up_t, gate_2, q_pre, segment_ids))
    gate_0, up_0 = share(gate_t, 0), share(up_t, 0)
    gate_2 = turn_z(gate_2, 2)
    gate_0_y, up_0_y = along_y(gate_0), along_y(up_0)

    rows = q_pre.shape[0]
    kv_heads = k_pre.shape[1] // HD
    own_lens = lax.dynamic_index_in_dim(lengths, me_req, 0, keepdims=False)
    own_pages = lax.dynamic_index_in_dim(page_table, me_req, 0, keepdims=False)
    own_owner = own_pages // REQS
    starts = jnp.cumsum(own_lens) - own_lens
    alive = segment_ids >= 0
    req_idx = jnp.clip(segment_ids - me_req * REQS, 0, REQS - 1)
    hit = req_idx[:, None] == jnp.arange(REQS)[None, :]
    row_start = jnp.sum(jnp.where(hit, starts[None, :], 0), axis=1)
    row_owner = jnp.sum(jnp.where(hit, own_owner[None, :], 0), axis=1)
    row_pos = jnp.arange(rows, dtype=jnp.int32) - row_start
    slots = jnp.where(alive, row_owner * PAGE + row_pos, -1)
    cosine, sine = rope_tables(row_pos.astype(jnp.float32))
    run = rows // n_mp // 2
    order = []
    for group in range(2 * n_mp):
        half, device = divmod(group, n_mp)
        order.append((device % CORES * n_x + device // CORES) * 2 + half)
    attended, kv_send = attention(
        q_pre, k_pre, v_pre, q_bias, k_bias, v_bias, cosine, sine, segment_ids, slots, n_req * PAGE, order
    )
    attended = attended.reshape(CORES, n_x * 2 * run, attended.shape[1])

    def project(which):
        picked = lax.dynamic_index_in_dim(attended, which, 0, keepdims=False)
        return jnp.dot(picked, w_out, preferred_element_type=jnp.float32).astype(jnp.bfloat16)

    kept, given = project(core), project(1 - core)
    up_2, gate_2, gate_0_y, up_0_y, kept, given = lax.optimization_barrier(
        (share(up_t, 2), gate_2, gate_0_y, up_0_y, kept, given)
    )
    up_2 = turn_z(up_2, 2)
    gate_2_y = along_y(gate_2)
    sibling = across_cores(given)
    width = sibling.shape[1]
    gate_1, up_2, gate_2_y, sibling = lax.optimization_barrier((share(gate_t, 1), up_2, gate_2_y, sibling))
    gate_1 = turn_z(gate_1, 1)
    up_2_y = along_y(up_2)
    pair = (kept.astype(jnp.float32) + sibling.astype(jnp.float32)).reshape(n_x, 2 * run, width)
    summed = lax.dynamic_index_in_dim(pair, x, 0, keepdims=False)
    outgoing = [
        lax.dynamic_index_in_dim(pair, (x + step) % n_x, 0, keepdims=False).astype(jnp.bfloat16)
        for step in range(1, n_x)
    ]
    gate_3, up_3, gate_1, up_2_y, outgoing = lax.optimization_barrier(
        (share(gate_t, 3), share(up_t, 3), gate_1, up_2_y, outgoing)
    )
    gate_3, up_3 = turn_z(gate_3, 3), turn_z(up_3, 3)
    gate_1_y = along_y(gate_1)
    incoming = [
        lax.ppermute(
            outgoing[step - 1],
            "mp",
            [(a * CORES + b, (a + step) % n_x * CORES + b) for a in range(n_x) for b in range(CORES)],
        )
        for step in range(1, n_x)
    ]
    up_1, gate_3, up_3, gate_1_y, incoming = lax.optimization_barrier(
        (share(up_t, 1), gate_3, up_3, gate_1_y, incoming)
    )
    up_1 = turn_z(up_1, 1)
    gate_3_y = along_y(gate_3)
    residual_rows = jnp.concatenate(
        [
            lax.dynamic_slice(residual, (me_mp * run, 0), (run, width)),
            lax.dynamic_slice(residual, (rows // 2 + me_mp * run, 0), (run, width)),
        ]
    )
    for other in incoming:
        summed = summed + other.astype(jnp.float32)
    state = residual_rows.astype(jnp.float32) + summed
    scale = lax.rsqrt(jnp.mean(state * state, axis=-1, keepdims=True) + EPS)
    normed = (state * scale * norm_gain).astype(jnp.bfloat16)
    near, up_1, gate_3_y = lax.optimization_barrier((normed, up_1, gate_3_y))

    row_ids = [(x - step) % n_x * CORES + core for step in range(n_x)]
    row_ids += [(x - step) % n_x * CORES + 1 - core for step in range(n_x)]
    flip = [[(a, a ^ by) for a in range(N_Z)] for by in range(N_Z)]
    middle = [(1, 2), (2, 1)]
    outward = [(1, 0), (2, 3)]
    at_end = (z == 0) | (z == N_Z - 1)
    up_1_y, up_3_y = along_y(up_1), along_y(up_3)
    near_x = along_x(near)
    next_1, middle_1 = along_z(near, flip[1]), along_z(near, middle)
    next_1, middle_1, up_1_y, up_3_y, near_x = lax.optimization_barrier((next_1, middle_1, up_1_y, up_3_y, near_x))
    next_2e, next_2m = along_z(middle_1, outward), along_z(next_1, middle)
    next_1_x = along_x(next_1)

    gates = [gate_0, *gate_0_y, gate_2, *gate_2_y, gate_1, *gate_1_y, gate_3, *gate_3_y]
    ups = [up_0, *up_0_y, up_2, *up_2_y, up_1, *up_1_y, up_3, *up_3_y]
    weights = gates + ups
    weight_ids = [i for shift in (0, 2, 1, 3) for i in source_ids(shift)]

    def shared(block, block_x):
        return [block, *block_x, *[across_cores(p) for p in (block, *block_x)]]

    def work(pieces):
        return mlp_block(weights, weight_ids, pieces, row_ids, pieces[0].shape[0] // run)

    pieces_0 = shared(near, near_x)
    next_2e, next_2m, next_1_x, pieces_0 = lax.optimization_barrier((next_2e, next_2m, next_1_x, pieces_0))
    next_3 = along_z(next_2m, outward)
    next_2 = jnp.where(at_end, next_2e, next_2m)
    next_2_x = along_x(next_2)
    hidden_0 = work(pieces_0)
    hidden_1 = work(shared(next_1, next_1_x))
    next_3, next_2_x, hidden_0, hidden_1, kv_send = lax.optimization_barrier(
        (next_3, next_2_x, hidden_0, hidden_1, kv_send)
    )
    next_3a = jnp.where(at_end, next_3[:run], middle_1[:run])
    next_3b = jnp.where(at_end, next_3[run:], middle_1[run:])
    next_3a_x = along_x(next_3a)
    pieces_2 = shared(next_2, next_2_x)
    next_3b, next_3a_x, pieces_2 = lax.optimization_barrier((next_3b, next_3a_x, pieces_2))
    next_3b_x = along_x(next_3b)
    kv_in = lax.all_to_all(
        kv_send.reshape(n_req, PAGE, 2 * kv_heads * HD), "req", split_axis=0, concat_axis=0, tiled=True
    )
    back_1 = along_z(hidden_1, flip[1])
    hidden_2 = work(pieces_2)
    pieces_3a = shared(next_3a, next_3a_x)
    next_3b_x, hidden_2, pieces_3a, kv_in = lax.optimization_barrier((next_3b_x, hidden_2, pieces_3a, kv_in))
    back_2 = along_z(hidden_2, flip[2])
    back_3a = along_z(work(pieces_3a), flip[3])
    back_3b = along_z(work(shared(next_3b, next_3b_x)), flip[3])
    hidden_t = jnp.zeros((units_all, rows), jnp.bfloat16)
    for by, at, done in (
        (0, 0, hidden_0),
        (1, 0, back_1),
        (2, 0, back_2),
        (3, 0, back_3a),
        (3, rows // 2, back_3b),
    ):
        hidden_t = lax.dynamic_update_slice(hidden_t, done, ((z ^ by) * units, at))

    mine = page_table[None] == (me_req * REQS + jnp.arange(REQS, dtype=jnp.int32))[:, None, None]
    sources = jnp.sum(jnp.where(mine, jnp.arange(n_req, dtype=jnp.int32)[None, :, None], 0), axis=(1, 2))
    cache_out = write_cache(sources.astype(jnp.int32), kv_in, kv_heads)
    return hidden_t.T, cache_out


def solution(mesh):
    in_specs = (
        P("req", "mp"),
        P("req", "mp"),
        P("req", "mp"),
        P("mp"),
        P("mp"),
        P("mp"),
        P("req"),
        P(),
        P(),
        P("mp", None),
        P("req", None),
        P(),
        P("req", "mp"),
        P("req", "mp"),
    )
    out_specs = (P("req", "mp"), P("req", "mp", None, None))
    return jax.shard_map(shards, mesh=mesh, in_specs=in_specs, out_specs=out_specs, check_vma=False)
```

```python
import math

import jax
import jax.numpy as jnp
from jax import lax
from jax.experimental import pallas as pl
from jax.experimental.pallas import tpu as pltpu
from jax.sharding import PartitionSpec as P

HD = 128
PAGE = 128
REQS = 4
CORES = 2
N_Z = 4
THETA = 1000000.0
EPS = 1e-06
NT = (((1,), (1,)), ((), ()))


def rope_tables(positions):
    half_dim = HD // 2
    frequencies = THETA ** (-jnp.arange(half_dim, dtype=jnp.float32) * (2.0 / HD))
    angles = positions[:, None] * frequencies[None, :]
    cosine = jnp.cos(angles)
    sine = jnp.sin(angles)
    return jnp.concatenate([cosine, cosine], axis=-1), jnp.concatenate([-sine, sine], axis=-1)


def attention_kernel(order, q_ref, k_ref, v_ref, qb_ref, kb_ref, vb_ref, cos_ref, sin_ref, segc_ref, segr_ref,
                     slot_ref, out_ref, send_ref, q_buf, k_buf, v_buf, kv_buf):
    rows = q_ref.shape[0]
    kv_heads = k_ref.shape[1] // HD
    q_heads = q_ref.shape[1] // HD
    group = q_heads // kv_heads
    live = segc_ref[...] >= 0
    cosine = cos_ref[...]
    sine = sin_ref[...]

    def turned(source, bias, head):
        cols = slice(head * HD, (head + 1) * HD)
        raw = source[:, cols].astype(jnp.float32) + bias[:, cols]
        return jnp.where(live, raw * cosine + pltpu.roll(raw, HD // 2, 1) * sine, 0.0).astype(jnp.bfloat16)

    for head in range(q_heads):
        q_buf[:, head * HD:(head + 1) * HD] = turned(q_ref, qb_ref, head)
    for head in range(kv_heads):
        cols = slice(head * HD, (head + 1) * HD)
        key = turned(k_ref, kb_ref, head)
        value = jnp.where(live, v_ref[:, cols].astype(jnp.float32) + vb_ref[:, cols], 0.0).astype(jnp.bfloat16)
        k_buf[:, cols] = key
        v_buf[:, cols] = value
        kv_buf[:, 2 * head * HD:(2 * head + 1) * HD] = key
        kv_buf[:, (2 * head + 1) * HD:(2 * head + 2) * HD] = value
    slots = slot_ref[...]
    for part in range(send_ref.shape[0] // rows):
        wanted = lax.broadcasted_iota(jnp.int32, (rows, rows), 0) + part * rows
        pick = jnp.where(wanted == slots, 1.0, 0.0).astype(jnp.bfloat16)
        send_ref[part * rows:(part + 1) * rows, :] = jnp.dot(
            pick, kv_buf[...], preferred_element_type=jnp.float32
        ).astype(jnp.bfloat16)
    scale = 1.0 / math.sqrt(HD)
    tile = PAGE
    for start in range(0, rows, tile):
        low = max(0, start - tile)
        high = start + tile
        seg_q = segc_ref[start:high, :]
        seg_k = segr_ref[:, low:high]
        row_at = lax.broadcasted_iota(jnp.int32, (tile, high - low), 0) + start
        col_at = lax.broadcasted_iota(jnp.int32, (tile, high - low), 1) + low
        allowed = (seg_q == seg_k) & (seg_k >= 0) & (col_at <= row_at)
        for head in range(q_heads):
            kv = head // group
            kv_cols = slice(kv * HD, (kv + 1) * HD)
            scores = lax.dot_general(
                q_buf[start:high, head * HD:(head + 1) * HD], k_buf[low:high, kv_cols], NT,
                preferred_element_type=jnp.float32,
            ) * scale
            row_max = jnp.max(jnp.where(allowed, scores, -1e30), axis=-1, keepdims=True)
            weights = jnp.where(allowed, jnp.exp(scores - row_max), 0.0)
            total = jnp.sum(weights, axis=-1, keepdims=True)
            probs = (weights / jnp.where(total > 0.0, total, 1.0)).astype(jnp.bfloat16)
            mixed = jnp.dot(
                probs, v_buf[low:high, kv_cols], preferred_element_type=jnp.float32
            ).astype(jnp.bfloat16)
            size = rows // len(order)
            for at in range(0, tile, size):
                to = order[(start + at) // size] * size
                out_ref[to:to + size, head * HD:(head + 1) * HD] = mixed[at:at + size]


def attention(q_pre, k_pre, v_pre, q_bias, k_bias, v_bias, cosine, sine, segs, slots, slot_count, order):
    rows, q_cols = q_pre.shape
    kv_cols = k_pre.shape[1]
    vmem = pl.BlockSpec(memory_space=pltpu.VMEM)
    return pl.pallas_call(
        lambda *refs: attention_kernel(order, *refs),
        out_shape=(
            jax.ShapeDtypeStruct((rows, q_cols), jnp.bfloat16),
            jax.ShapeDtypeStruct((slot_count, 2 * kv_cols), jnp.bfloat16),
        ),
        in_specs=[vmem] * 11,
        out_specs=(vmem, vmem),
        scratch_shapes=[
            pltpu.VMEM((rows, q_cols), jnp.bfloat16),
            pltpu.VMEM((rows, kv_cols), jnp.bfloat16),
            pltpu.VMEM((rows, kv_cols), jnp.bfloat16),
            pltpu.VMEM((rows, 2 * kv_cols), jnp.bfloat16),
        ],
        compiler_params=pltpu.CompilerParams(vmem_limit_bytes=32 * 2**20),
        cost_estimate=pl.CostEstimate(flops=10**8, bytes_accessed=2**16, transcendentals=0),
        name="attention",
    )(q_pre, k_pre, v_pre, q_bias[None], k_bias[None], v_bias[None], cosine, sine, segs[:, None], segs[None],
      slots[None])


def cache_kernel(source_ref, in_ref, out_ref, sems):
    copies = []
    for page in range(out_ref.shape[0]):
        for head in range(out_ref.shape[1]):
            copies.append(
                pltpu.make_async_copy(
                    in_ref.at[source_ref[page], :, pl.ds(head * 2 * HD, 2 * HD)],
                    out_ref.at[page, head],
                    sems.at[page, head],
                )
            )
    for copy in copies:
        copy.start()
    for copy in copies:
        copy.wait()


def write_cache(sources, pages_in, kv_heads):
    anywhere = pl.BlockSpec(memory_space=pl.ANY)
    return pl.pallas_call(
        cache_kernel,
        out_shape=jax.ShapeDtypeStruct((REQS, kv_heads, PAGE, 2 * HD), jnp.bfloat16),
        in_specs=[pl.BlockSpec(memory_space=pltpu.SMEM), anywhere],
        out_specs=anywhere,
        scratch_shapes=[pltpu.SemaphoreType.DMA((REQS, kv_heads))],
        name="write_cache",
    )(sources, pages_in)


def mlp_kernel(count, pieces, halves, ids_ref, *refs):
    weights = (refs[:count], refs[count:2 * count])
    rows_in = refs[2 * count:2 * count + pieces]
    out_ref, gate_buf, up_buf, row_buf, acc, weight_sems, row_sems = refs[2 * count + pieces:]
    depth = weights[0][0].shape[1]
    piece = rows_in[0].shape[0] // halves
    first, second = [], []
    for index in range(pieces):
        for half in range(halves):
            at = pl.multiple_of((half * pieces + ids_ref[count + index]) * piece, piece)
            first.append(
                pltpu.make_async_copy(
                    rows_in[index].at[pl.ds(half * piece, piece), :],
                    row_buf.at[pl.ds(at, piece), :],
                    row_sems.at[index, half],
                )
            )
    for index in range(count):
        for which, buf in ((0, gate_buf), (1, up_buf)):
            second.append(
                pltpu.make_async_copy(weights[which][index], buf.at[index], weight_sems.at[which, index])
            )
    for copy in first + second:
        copy.start()
    for copy in first:
        copy.wait()
    tokens = out_ref.shape[1]
    tile = min(256, tokens)
    for index in range(count):
        second[2 * index].wait()
        second[2 * index + 1].wait()
        at = pl.multiple_of(ids_ref[index] * depth, depth)
        for start in range(0, tokens, tile):
            block = row_buf[start:start + tile, pl.ds(at, depth)]
            for which, buf in ((0, gate_buf), (1, up_buf)):
                term = lax.dot_general(buf[index], block, NT, preferred_element_type=jnp.float32)
                if index:
                    term = acc[which, :, start:start + tile] + term
                acc[which, :, start:start + tile] = term
    for start in range(0, tokens, tile):
        gate = acc[0, :, start:start + tile]
        up = acc[1, :, start:start + tile]
        out_ref[:, start:start + tile] = (gate / (1.0 + jnp.exp(-gate)) * up).astype(jnp.bfloat16)


def mlp_block(weights, weight_ids, rows_in, row_ids, halves):
    count, pieces = len(weight_ids), len(row_ids)
    units, depth = weights[0].shape
    width = rows_in[0].shape[1]
    piece = rows_in[0].shape[0] // halves
    tokens = piece * pieces * halves
    if depth % 128 or units % 16 or piece % 16:
        both = jnp.zeros((2, units, width), jnp.bfloat16)
        for index in range(count):
            pair = jnp.stack([weights[index], weights[count + index]])
            both = lax.dynamic_update_slice(both, pair, (0, 0, weight_ids[index] * depth))
        rows = jnp.zeros((tokens, width), jnp.bfloat16)
        for index in range(pieces):
            for half in range(halves):
                at = (half * pieces + row_ids[index]) * piece
                rows = lax.dynamic_update_slice(rows, rows_in[index][half * piece:(half + 1) * piece], (at, 0))
        gate = lax.dot_general(both[0], rows, NT, preferred_element_type=jnp.float32)
        up = lax.dot_general(both[1], rows, NT, preferred_element_type=jnp.float32)
        return (jax.nn.silu(gate) * up).astype(jnp.bfloat16)
    ids = jnp.stack([jnp.asarray(i, jnp.int32) for i in list(weight_ids) + list(row_ids)])
    anywhere = pl.BlockSpec(memory_space=pl.ANY)
    return pl.pallas_call(
        lambda *refs: mlp_kernel(count, pieces, halves, *refs),
        out_shape=jax.ShapeDtypeStruct((units, tokens), jnp.bfloat16),
        in_specs=[pl.BlockSpec(memory_space=pltpu.SMEM)] + [anywhere] * (2 * count + pieces),
        out_specs=pl.BlockSpec(memory_space=pltpu.VMEM),
        scratch_shapes=[
            pltpu.VMEM((count, units, depth), jnp.bfloat16),
            pltpu.VMEM((count, units, depth), jnp.bfloat16),
            pltpu.VMEM((tokens, width), jnp.bfloat16),
            pltpu.VMEM((2, units, tokens), jnp.float32),
            pltpu.SemaphoreType.DMA((2, count)),
            pltpu.SemaphoreType.DMA((pieces, halves)),
        ],
        compiler_params=pltpu.CompilerParams(vmem_limit_bytes=60 * 2**20),
        cost_estimate=pl.CostEstimate(flops=10**8, bytes_accessed=2**16, transcendentals=0),
        name="mlp_block",
    )(ids, *weights, *rows_in)


def after(value, *before):
    return lax.optimization_barrier((value,) + before)[0]


def shards(q_pre, k_pre, v_pre, q_bias, k_bias, v_bias, segment_ids, lengths, page_table, w_out, residual,
           norm_gain, w_gate, w_up):
    me_req = lax.axis_index("req")
    me_mp = lax.axis_index("mp")
    n_req = lax.axis_size("req")
    n_mp = lax.axis_size("mp")
    n_y = n_req // N_Z
    n_x = n_mp // CORES
    z = me_req // n_y
    y = me_req % n_y
    x = me_mp // CORES
    core = me_mp % CORES

    def along_z(value, moves):
        return lax.ppermute(value, "req", [(a * n_y + c, b * n_y + c) for a, b in moves for c in range(n_y)])

    def turn_z(value, shift):
        return along_z(value, [(a, (a + shift) % N_Z) for a in range(N_Z)])

    def along_y(value):
        return [
            lax.ppermute(
                value, "req", [(a * n_y + b, a * n_y + (b + step) % n_y) for a in range(N_Z) for b in range(n_y)]
            )
            for step in range(1, n_y)
        ]

    def along_x(value):
        return [
            lax.ppermute(
                value,
                "mp",
                [(a * CORES + b, (a + step) % n_x * CORES + b) for a in range(n_x) for b in range(CORES)],
            )
            for step in range(1, n_x)
        ]

    def across_cores(value):
        return lax.ppermute(
            value, "mp", [(a * CORES + b, a * CORES + 1 - b) for a in range(n_x) for b in range(CORES)]
        )

    units_all, depth = w_gate.shape[1], w_gate.shape[0]
    units = units_all // N_Z

    def share(weight_t, shift):
        return lax.dynamic_slice(weight_t, ((z + shift) % N_Z * units, 0), (units, depth))

    def source_ids(shift):
        source_z = (z - shift) % N_Z
        return [source_z * n_y + (y - step) % n_y for step in range(n_y)]

    gate_t, up_t = w_gate.T, w_up.T
    gate_2 = share(gate_t, 2)
    gate_t, up_t, gate_2, q_pre, segment_ids = lax.optimization_barrier((gate_t, up_t, gate_2, q_pre, segment_ids))
    gate_0, up_0 = share(gate_t, 0), share(up_t, 0)
    gate_2 = turn_z(gate_2, 2)
    gate_0_y = along_y(gate_0)

    rows = q_pre.shape[0]
    kv_heads = k_pre.shape[1] // HD
    own_lens = lax.dynamic_index_in_dim(lengths, me_req, 0, keepdims=False)
    own_pages = lax.dynamic_index_in_dim(page_table, me_req, 0, keepdims=False)
    own_owner = own_pages // REQS
    starts = jnp.cumsum(own_lens) - own_lens
    alive = segment_ids >= 0
    req_idx = jnp.clip(segment_ids - me_req * REQS, 0, REQS - 1)
    hit = req_idx[:, None] == jnp.arange(REQS)[None, :]
    row_start = jnp.sum(jnp.where(hit, starts[None, :], 0), axis=1)
    row_owner = jnp.sum(jnp.where(hit, own_owner[None, :], 0), axis=1)
    row_pos = jnp.arange(rows, dtype=jnp.int32) - row_start
    slots = jnp.where(alive, row_owner * PAGE + row_pos, -1)
    cosine, sine = rope_tables(row_pos.astype(jnp.float32))
    run = rows // n_mp // 2
    order = []
    for group in range(2 * n_mp):
        half, device = divmod(group, n_mp)
        order.append((device % CORES * n_x + device // CORES) * 2 + half)
    attended, kv_send = attention(
        q_pre, k_pre, v_pre, q_bias, k_bias, v_bias, cosine, sine, segment_ids, slots, n_req * PAGE, order
    )
    attended = attended.reshape(CORES, n_x * 2 * run, attended.shape[1])

    def project(which):
        picked = lax.dynamic_index_in_dim(attended, which, 0, keepdims=False)
        return jnp.dot(picked, w_out, preferred_element_type=jnp.float32).astype(jnp.bfloat16)

    kept, given = project(core), project(1 - core)
    up_2, up_0, gate_2, gate_0_y, kept, given = lax.optimization_barrier(
        (share(up_t, 2), up_0, gate_2, gate_0_y, kept, given)
    )
    up_2 = turn_z(up_2, 2)
    up_0_y = along_y(up_0)
    gate_2_y = along_y(gate_2)
    sibling = across_cores(given)
    width = sibling.shape[1]
    gate_1, up_2, up_0_y, gate_2_y, sibling = lax.optimization_barrier(
        (share(gate_t, 1), up_2, up_0_y, gate_2_y, sibling)
    )
    gate_1 = turn_z(gate_1, 1)
    up_2_y = along_y(up_2)
    pair = (kept.astype(jnp.float32) + sibling.astype(jnp.float32)).reshape(n_x, 2 * run, width)
    summed = lax.dynamic_index_in_dim(pair, x, 0, keepdims=False)
    outgoing = [
        lax.dynamic_index_in_dim(pair, (x + step) % n_x, 0, keepdims=False).astype(jnp.bfloat16)
        for step in range(1, n_x)
    ]
    gate_3, up_3, gate_1, up_2_y, outgoing = lax.optimization_barrier(
        (share(gate_t, 3), share(up_t, 3), gate_1, up_2_y, outgoing)
    )
    gate_3, up_3 = turn_z(gate_3, 3), turn_z(up_3, 3)
    gate_1_y = along_y(gate_1)
    incoming = [
        lax.ppermute(
            outgoing[step - 1],
            "mp",
            [(a * CORES + b, (a + step) % n_x * CORES + b) for a in range(n_x) for b in range(CORES)],
        )
        for step in range(1, n_x)
    ]
    up_1, gate_3, up_3, gate_1_y, incoming = lax.optimization_barrier(
        (share(up_t, 1), gate_3, up_3, gate_1_y, incoming)
    )
    up_1 = turn_z(up_1, 1)
    gate_3_y = along_y(gate_3)
    residual_rows = jnp.concatenate(
        [
            lax.dynamic_slice(residual, (me_mp * run, 0), (run, width)),
            lax.dynamic_slice(residual, (rows // 2 + me_mp * run, 0), (run, width)),
        ]
    )
    for other in incoming:
        summed = summed + other.astype(jnp.float32)
    state = residual_rows.astype(jnp.float32) + summed
    scale = lax.rsqrt(jnp.mean(state * state, axis=-1, keepdims=True) + EPS)
    normed = (state * scale * norm_gain).astype(jnp.bfloat16)
    near, up_1, gate_3_y = lax.optimization_barrier((normed, up_1, gate_3_y))

    row_ids = [(x - step) % n_x * CORES + core for step in range(n_x)]
    row_ids += [(x - step) % n_x * CORES + 1 - core for step in range(n_x)]
    flip = [[(a, a ^ by) for a in range(N_Z)] for by in range(N_Z)]
    middle = [(1, 2), (2, 1)]
    outward = [(1, 0), (2, 3)]
    at_end = (z == 0) | (z == N_Z - 1)
    up_1_y, up_3_y = along_y(up_1), along_y(up_3)
    near_x = along_x(near)
    next_1, middle_1 = along_z(near, flip[1]), along_z(near, middle)
    next_1, middle_1, up_1_y, up_3_y, near_x = lax.optimization_barrier((next_1, middle_1, up_1_y, up_3_y, near_x))
    next_2e, next_2m = along_z(middle_1, outward), along_z(next_1, middle)
    next_1_x = along_x(next_1)

    gates = [gate_0, *gate_0_y, gate_2, *gate_2_y, gate_1, *gate_1_y, gate_3, *gate_3_y]
    ups = [up_0, *up_0_y, up_2, *up_2_y, up_1, *up_1_y, up_3, *up_3_y]
    weights = gates + ups
    weight_ids = [i for shift in (0, 2, 1, 3) for i in source_ids(shift)]

    def shared(block, block_x):
        return [block, *block_x, *[across_cores(p) for p in (block, *block_x)]]

    def work(pieces):
        return mlp_block(weights, weight_ids, pieces, row_ids, pieces[0].shape[0] // run)

    pieces_0 = shared(near, near_x)
    next_2e, next_2m, next_1_x, pieces_0 = lax.optimization_barrier((next_2e, next_2m, next_1_x, pieces_0))
    next_3 = along_z(next_2m, outward)
    next_2 = jnp.where(at_end, next_2e, next_2m)
    next_2_x = along_x(next_2)
    hidden_0 = work(pieces_0)
    hidden_1 = work(shared(next_1, next_1_x))
    next_3, next_2_x, hidden_0, hidden_1, kv_send = lax.optimization_barrier(
        (next_3, next_2_x, hidden_0, hidden_1, kv_send)
    )
    next_3a = jnp.where(at_end, next_3[:run], middle_1[:run])
    next_3b = jnp.where(at_end, next_3[run:], middle_1[run:])
    next_3a_x = along_x(next_3a)
    hidden_2 = work(shared(next_2, next_2_x))
    back_1 = along_z(hidden_1, flip[1])
    kv_in = lax.all_to_all(
        kv_send.reshape(n_req, PAGE, 2 * kv_heads * HD), "req", split_axis=0, concat_axis=0, tiled=True
    )
    next_3b, next_3a_x, hidden_2, back_1, kv_in = lax.optimization_barrier(
        (next_3b, next_3a_x, hidden_2, back_1, kv_in)
    )
    next_3b_x = along_x(next_3b)
    back_2 = along_z(hidden_2, flip[2])
    hidden_3a = work(shared(next_3a, next_3a_x))
    mine = page_table[None] == (me_req * REQS + jnp.arange(REQS, dtype=jnp.int32))[:, None, None]
    sources = jnp.sum(jnp.where(mine, jnp.arange(n_req, dtype=jnp.int32)[None, :, None], 0), axis=(1, 2))
    cache_out = write_cache(sources.astype(jnp.int32), kv_in, kv_heads)
    next_3b_x, hidden_3a, back_2, cache_out = lax.optimization_barrier((next_3b_x, hidden_3a, back_2, cache_out))
    back_3a = along_z(hidden_3a, flip[3])
    back_3b = along_z(work(shared(next_3b, next_3b_x)), flip[3])
    hidden_t = jnp.zeros((units_all, rows), jnp.bfloat16)
    for by, at, done in (
        (0, 0, hidden_0),
        (1, 0, back_1),
        (2, 0, back_2),
        (3, 0, back_3a),
        (3, rows // 2, back_3b),
    ):
        hidden_t = lax.dynamic_update_slice(hidden_t, done, ((z ^ by) * units, at))
    return hidden_t.T, cache_out


def solution(mesh):
    in_specs = (
        P("req", "mp"),
        P("req", "mp"),
        P("req", "mp"),
        P("mp"),
        P("mp"),
        P("mp"),
        P("req"),
        P(),
        P(),
        P("mp", None),
        P("req", None),
        P(),
        P("req", "mp"),
        P("req", "mp"),
    )
    out_specs = (P("req", "mp"), P("req", "mp", None, None))
    return jax.shard_map(shards, mesh=mesh, in_specs=in_specs, out_specs=out_specs, check_vma=False)
```

```python
import math

import jax
import jax.numpy as jnp
from jax import lax
from jax.experimental import pallas as pl
from jax.experimental.pallas import tpu as pltpu
from jax.sharding import PartitionSpec as P

HD = 128
PAGE = 128
REQS = 4
CORES = 2
N_Z = 4
THETA = 1000000.0
EPS = 1e-06
NT = (((1,), (1,)), ((), ()))


def rope_tables(positions):
    half_dim = HD // 2
    frequencies = THETA ** (-jnp.arange(half_dim, dtype=jnp.float32) * (2.0 / HD))
    angles = positions[:, None] * frequencies[None, :]
    cosine = jnp.cos(angles)
    sine = jnp.sin(angles)
    return jnp.concatenate([cosine, cosine], axis=-1), jnp.concatenate([-sine, sine], axis=-1)


def attention_kernel(order, q_ref, k_ref, v_ref, qb_ref, kb_ref, vb_ref, cos_ref, sin_ref, segc_ref, segr_ref,
                     slot_ref, out_ref, send_ref, q_buf, k_buf, v_buf, kv_buf):
    rows = q_ref.shape[0]
    kv_heads = k_ref.shape[1] // HD
    q_heads = q_ref.shape[1] // HD
    group = q_heads // kv_heads
    live = segc_ref[...] >= 0
    cosine = cos_ref[...]
    sine = sin_ref[...]

    def turned(source, bias, head):
        cols = slice(head * HD, (head + 1) * HD)
        raw = source[:, cols].astype(jnp.float32) + bias[:, cols]
        return jnp.where(live, raw * cosine + pltpu.roll(raw, HD // 2, 1) * sine, 0.0).astype(jnp.bfloat16)

    for head in range(q_heads):
        q_buf[:, head * HD:(head + 1) * HD] = turned(q_ref, qb_ref, head)
    for head in range(kv_heads):
        cols = slice(head * HD, (head + 1) * HD)
        key = turned(k_ref, kb_ref, head)
        value = jnp.where(live, v_ref[:, cols].astype(jnp.float32) + vb_ref[:, cols], 0.0).astype(jnp.bfloat16)
        k_buf[:, cols] = key
        v_buf[:, cols] = value
        kv_buf[:, 2 * head * HD:(2 * head + 1) * HD] = key
        kv_buf[:, (2 * head + 1) * HD:(2 * head + 2) * HD] = value
    slots = slot_ref[...]
    for part in range(send_ref.shape[0] // rows):
        wanted = lax.broadcasted_iota(jnp.int32, (rows, rows), 0) + part * rows
        pick = jnp.where(wanted == slots, 1.0, 0.0).astype(jnp.bfloat16)
        send_ref[part * rows:(part + 1) * rows, :] = jnp.dot(
            pick, kv_buf[...], preferred_element_type=jnp.float32
        ).astype(jnp.bfloat16)
    scale = 1.0 / math.sqrt(HD)
    tile = PAGE
    for start in range(0, rows, tile):
        low = max(0, start - tile)
        high = start + tile
        seg_q = segc_ref[start:high, :]
        seg_k = segr_ref[:, low:high]
        row_at = lax.broadcasted_iota(jnp.int32, (tile, high - low), 0) + start
        col_at = lax.broadcasted_iota(jnp.int32, (tile, high - low), 1) + low
        allowed = (seg_q == seg_k) & (seg_k >= 0) & (col_at <= row_at)
        for head in range(q_heads):
            kv = head // group
            kv_cols = slice(kv * HD, (kv + 1) * HD)
            scores = lax.dot_general(
                q_buf[start:high, head * HD:(head + 1) * HD], k_buf[low:high, kv_cols], NT,
                preferred_element_type=jnp.float32,
            ) * scale
            row_max = jnp.max(jnp.where(allowed, scores, -1e30), axis=-1, keepdims=True)
            weights = jnp.where(allowed, jnp.exp(scores - row_max), 0.0)
            total = jnp.sum(weights, axis=-1, keepdims=True)
            probs = (weights / jnp.where(total > 0.0, total, 1.0)).astype(jnp.bfloat16)
            mixed = jnp.dot(
                probs, v_buf[low:high, kv_cols], preferred_element_type=jnp.float32
            ).astype(jnp.bfloat16)
            size = rows // len(order)
            for at in range(0, tile, size):
                to = order[(start + at) // size] * size
                out_ref[to:to + size, head * HD:(head + 1) * HD] = mixed[at:at + size]


def attention(q_pre, k_pre, v_pre, q_bias, k_bias, v_bias, cosine, sine, segs, slots, slot_count, order):
    rows, q_cols = q_pre.shape
    kv_cols = k_pre.shape[1]
    vmem = pl.BlockSpec(memory_space=pltpu.VMEM)
    return pl.pallas_call(
        lambda *refs: attention_kernel(order, *refs),
        out_shape=(
            jax.ShapeDtypeStruct((rows, q_cols), jnp.bfloat16),
            jax.ShapeDtypeStruct((slot_count, 2 * kv_cols), jnp.bfloat16),
        ),
        in_specs=[vmem] * 11,
        out_specs=(vmem, vmem),
        scratch_shapes=[
            pltpu.VMEM((rows, q_cols), jnp.bfloat16),
            pltpu.VMEM((rows, kv_cols), jnp.bfloat16),
            pltpu.VMEM((rows, kv_cols), jnp.bfloat16),
            pltpu.VMEM((rows, 2 * kv_cols), jnp.bfloat16),
        ],
        compiler_params=pltpu.CompilerParams(vmem_limit_bytes=32 * 2**20),
        cost_estimate=pl.CostEstimate(flops=10**8, bytes_accessed=2**16, transcendentals=0),
        name="attention",
    )(q_pre, k_pre, v_pre, q_bias[None], k_bias[None], v_bias[None], cosine, sine, segs[:, None], segs[None],
      slots[None])


def cache_kernel(source_ref, in_ref, out_ref):
    for page in range(out_ref.shape[0]):
        for head in range(out_ref.shape[1]):
            out_ref[page, head] = in_ref[source_ref[page], :, head * 2 * HD:(head + 1) * 2 * HD]


def write_cache(sources, pages_in, kv_heads):
    vmem = pl.BlockSpec(memory_space=pltpu.VMEM)
    return pl.pallas_call(
        cache_kernel,
        out_shape=jax.ShapeDtypeStruct((REQS, kv_heads, PAGE, 2 * HD), jnp.bfloat16),
        in_specs=[pl.BlockSpec(memory_space=pltpu.SMEM), vmem],
        out_specs=vmem,
        cost_estimate=pl.CostEstimate(flops=0, bytes_accessed=2**16, transcendentals=0),
        name="write_cache",
    )(sources, pages_in)


def mlp_kernel(count, pieces, halves, ids_ref, *refs):
    weights = (refs[:count], refs[count:2 * count])
    rows_in = refs[2 * count:2 * count + pieces]
    out_ref, gate_buf, up_buf, row_buf, acc, weight_sems, row_sems = refs[2 * count + pieces:]
    units, depth = weights[0][0].shape
    parts = weight_sems.shape[2]
    piece = rows_in[0].shape[0] // halves
    first, second = [], []
    for index in range(pieces):
        for half in range(halves):
            at = pl.multiple_of((half * pieces + ids_ref[count + index]) * piece, piece)
            first.append(
                pltpu.make_async_copy(
                    rows_in[index].at[pl.ds(half * piece, piece), :],
                    row_buf.at[pl.ds(at, piece), :],
                    row_sems.at[index, half],
                )
            )
    for index in range(count):
        for which, buf in ((0, gate_buf), (1, up_buf)):
            for part in range(parts):
                some = pl.ds(part * (units // parts), units // parts)
                second.append(
                    pltpu.make_async_copy(
                        weights[which][index].at[some, :], buf.at[index, some, :], weight_sems.at[which, index, part]
                    )
                )
    for copy in first + second:
        copy.start()
    for copy in first:
        copy.wait()
    tokens = out_ref.shape[1]
    tile = min(256, tokens)
    for index in range(count):
        for copy in second[2 * parts * index:2 * parts * (index + 1)]:
            copy.wait()
        at = pl.multiple_of(ids_ref[index] * depth, depth)
        for start in range(0, tokens, tile):
            block = row_buf[start:start + tile, pl.ds(at, depth)]
            for which, buf in ((0, gate_buf), (1, up_buf)):
                term = lax.dot_general(buf[index], block, NT, preferred_element_type=jnp.float32)
                if index:
                    term = acc[which, :, start:start + tile] + term
                acc[which, :, start:start + tile] = term
    for start in range(0, tokens, tile):
        gate = acc[0, :, start:start + tile]
        up = acc[1, :, start:start + tile]
        out_ref[:, start:start + tile] = (gate / (1.0 + jnp.exp(-gate)) * up).astype(jnp.bfloat16)


def mlp_block(weights, weight_ids, rows_in, row_ids, halves):
    count, pieces = len(weight_ids), len(row_ids)
    units, depth = weights[0].shape
    width = rows_in[0].shape[1]
    piece = rows_in[0].shape[0] // halves
    tokens = piece * pieces * halves
    if depth % 128 or units % 16 or piece % 16:
        both = jnp.zeros((2, units, width), jnp.bfloat16)
        for index in range(count):
            pair = jnp.stack([weights[index], weights[count + index]])
            both = lax.dynamic_update_slice(both, pair, (0, 0, weight_ids[index] * depth))
        rows = jnp.zeros((tokens, width), jnp.bfloat16)
        for index in range(pieces):
            for half in range(halves):
                at = (half * pieces + row_ids[index]) * piece
                rows = lax.dynamic_update_slice(rows, rows_in[index][half * piece:(half + 1) * piece], (at, 0))
        gate = lax.dot_general(both[0], rows, NT, preferred_element_type=jnp.float32)
        up = lax.dot_general(both[1], rows, NT, preferred_element_type=jnp.float32)
        return (jax.nn.silu(gate) * up).astype(jnp.bfloat16)
    ids = jnp.stack([jnp.asarray(i, jnp.int32) for i in list(weight_ids) + list(row_ids)])
    anywhere = pl.BlockSpec(memory_space=pl.ANY)
    return pl.pallas_call(
        lambda *refs: mlp_kernel(count, pieces, halves, *refs),
        out_shape=jax.ShapeDtypeStruct((units, tokens), jnp.bfloat16),
        in_specs=[pl.BlockSpec(memory_space=pltpu.SMEM)] + [anywhere] * (2 * count + pieces),
        out_specs=pl.BlockSpec(memory_space=pltpu.VMEM),
        scratch_shapes=[
            pltpu.VMEM((count, units, depth), jnp.bfloat16),
            pltpu.VMEM((count, units, depth), jnp.bfloat16),
            pltpu.VMEM((tokens, width), jnp.bfloat16),
            pltpu.VMEM((2, units, tokens), jnp.float32),
            pltpu.SemaphoreType.DMA((2, count, 3 if units % 48 == 0 else 1)),
            pltpu.SemaphoreType.DMA((pieces, halves)),
        ],
        compiler_params=pltpu.CompilerParams(vmem_limit_bytes=60 * 2**20),
        cost_estimate=pl.CostEstimate(flops=10**8, bytes_accessed=2**16, transcendentals=0),
        name="mlp_block",
    )(ids, *weights, *rows_in)


def after(value, *before):
    return lax.optimization_barrier((value,) + before)[0]


def shards(q_pre, k_pre, v_pre, q_bias, k_bias, v_bias, segment_ids, lengths, page_table, w_out, residual,
           norm_gain, w_gate, w_up):
    me_req = lax.axis_index("req")
    me_mp = lax.axis_index("mp")
    n_req = lax.axis_size("req")
    n_mp = lax.axis_size("mp")
    n_y = n_req // N_Z
    n_x = n_mp // CORES
    z = me_req // n_y
    y = me_req % n_y
    x = me_mp // CORES
    core = me_mp % CORES

    def along_z(value, moves):
        return lax.ppermute(value, "req", [(a * n_y + c, b * n_y + c) for a, b in moves for c in range(n_y)])

    def turn_z(value, shift):
        return along_z(value, [(a, (a + shift) % N_Z) for a in range(N_Z)])

    def along_y(value):
        return [
            lax.ppermute(
                value, "req", [(a * n_y + b, a * n_y + (b + step) % n_y) for a in range(N_Z) for b in range(n_y)]
            )
            for step in range(1, n_y)
        ]

    def along_x(value):
        return [
            lax.ppermute(
                value,
                "mp",
                [(a * CORES + b, (a + step) % n_x * CORES + b) for a in range(n_x) for b in range(CORES)],
            )
            for step in range(1, n_x)
        ]

    def across_cores(value):
        return lax.ppermute(
            value, "mp", [(a * CORES + b, a * CORES + 1 - b) for a in range(n_x) for b in range(CORES)]
        )

    units_all, depth = w_gate.shape[1], w_gate.shape[0]
    units = units_all // N_Z

    def share(weight_t, shift):
        return lax.dynamic_slice(weight_t, ((z + shift) % N_Z * units, 0), (units, depth))

    def source_ids(shift):
        source_z = (z - shift) % N_Z
        return [source_z * n_y + (y - step) % n_y for step in range(n_y)]

    gate_t, up_t = w_gate.T, w_up.T
    gate_2 = share(gate_t, 2)
    gate_t, up_t, gate_2, q_pre, segment_ids = lax.optimization_barrier((gate_t, up_t, gate_2, q_pre, segment_ids))
    gate_0, up_0 = share(gate_t, 0), share(up_t, 0)
    gate_2 = turn_z(gate_2, 2)
    gate_0_y = along_y(gate_0)

    rows = q_pre.shape[0]
    kv_heads = k_pre.shape[1] // HD
    own_lens = lax.dynamic_index_in_dim(lengths, me_req, 0, keepdims=False)
    own_pages = lax.dynamic_index_in_dim(page_table, me_req, 0, keepdims=False)
    own_owner = own_pages // REQS
    starts = jnp.cumsum(own_lens) - own_lens
    alive = segment_ids >= 0
    req_idx = jnp.clip(segment_ids - me_req * REQS, 0, REQS - 1)
    hit = req_idx[:, None] == jnp.arange(REQS)[None, :]
    row_start = jnp.sum(jnp.where(hit, starts[None, :], 0), axis=1)
    row_owner = jnp.sum(jnp.where(hit, own_owner[None, :], 0), axis=1)
    row_pos = jnp.arange(rows, dtype=jnp.int32) - row_start
    slots = jnp.where(alive, row_owner * PAGE + row_pos, -1)
    cosine, sine = rope_tables(row_pos.astype(jnp.float32))
    run = rows // n_mp // 2
    order = []
    for group in range(2 * n_mp):
        half, device = divmod(group, n_mp)
        order.append((device % CORES * n_x + device // CORES) * 2 + half)
    attended, kv_send = attention(
        q_pre, k_pre, v_pre, q_bias, k_bias, v_bias, cosine, sine, segment_ids, slots, n_req * PAGE, order
    )
    attended = attended.reshape(CORES, n_x * 2 * run, attended.shape[1])

    def project(which):
        picked = lax.dynamic_index_in_dim(attended, which, 0, keepdims=False)
        return jnp.dot(picked, w_out, preferred_element_type=jnp.float32).astype(jnp.bfloat16)

    kept, given = project(core), project(1 - core)
    up_2, up_0, gate_2, gate_0_y, kept, given = lax.optimization_barrier(
        (share(up_t, 2), up_0, gate_2, gate_0_y, kept, given)
    )
    up_2 = turn_z(up_2, 2)
    up_0_y = along_y(up_0)
    gate_2_y = along_y(gate_2)
    sibling = across_cores(given)
    width = sibling.shape[1]
    gate_1, up_2, up_0_y, gate_2_y, sibling = lax.optimization_barrier(
        (share(gate_t, 1), up_2, up_0_y, gate_2_y, sibling)
    )
    gate_1 = turn_z(gate_1, 1)
    up_2_y = along_y(up_2)
    pair = (kept.astype(jnp.float32) + sibling.astype(jnp.float32)).reshape(n_x, 2 * run, width)
    summed = lax.dynamic_index_in_dim(pair, x, 0, keepdims=False)
    outgoing = [
        lax.dynamic_index_in_dim(pair, (x + step) % n_x, 0, keepdims=False).astype(jnp.bfloat16)
        for step in range(1, n_x)
    ]
    gate_3, up_3, gate_1, up_2_y, outgoing = lax.optimization_barrier(
        (share(gate_t, 3), share(up_t, 3), gate_1, up_2_y, outgoing)
    )
    gate_3, up_3 = turn_z(gate_3, 3), turn_z(up_3, 3)
    gate_1_y = along_y(gate_1)
    incoming = [
        lax.ppermute(
            outgoing[step - 1],
            "mp",
            [(a * CORES + b, (a + step) % n_x * CORES + b) for a in range(n_x) for b in range(CORES)],
        )
        for step in range(1, n_x)
    ]
    up_1, gate_3, up_3, gate_1_y, incoming = lax.optimization_barrier(
        (share(up_t, 1), gate_3, up_3, gate_1_y, incoming)
    )
    up_1 = turn_z(up_1, 1)
    gate_3_y = along_y(gate_3)
    residual_rows = jnp.concatenate(
        [
            lax.dynamic_slice(residual, (me_mp * run, 0), (run, width)),
            lax.dynamic_slice(residual, (rows // 2 + me_mp * run, 0), (run, width)),
        ]
    )
    for other in incoming:
        summed = summed + other.astype(jnp.float32)
    state = residual_rows.astype(jnp.float32) + summed
    scale = lax.rsqrt(jnp.mean(state * state, axis=-1, keepdims=True) + EPS)
    normed = (state * scale * norm_gain).astype(jnp.bfloat16)
    near, up_1, gate_3_y = lax.optimization_barrier((normed, up_1, gate_3_y))

    row_ids = [(x - step) % n_x * CORES + core for step in range(n_x)]
    row_ids += [(x - step) % n_x * CORES + 1 - core for step in range(n_x)]
    flip = [[(a, a ^ by) for a in range(N_Z)] for by in range(N_Z)]
    middle = [(1, 2), (2, 1)]
    outward = [(1, 0), (2, 3)]
    at_end = (z == 0) | (z == N_Z - 1)
    up_1_y, up_3_y = along_y(up_1), along_y(up_3)
    near_x = along_x(near)
    next_1, middle_1 = along_z(near, flip[1]), along_z(near, middle)
    next_1, middle_1, up_1_y, up_3_y, near_x = lax.optimization_barrier((next_1, middle_1, up_1_y, up_3_y, near_x))
    next_2e, next_2m = along_z(middle_1, outward), along_z(next_1, middle)
    next_1_x = along_x(next_1)

    gates = [gate_0, *gate_0_y, gate_2, *gate_2_y, gate_1, *gate_1_y, gate_3, *gate_3_y]
    ups = [up_0, *up_0_y, up_2, *up_2_y, up_1, *up_1_y, up_3, *up_3_y]
    weights = gates + ups
    weight_ids = [i for shift in (0, 2, 1, 3) for i in source_ids(shift)]

    def shared(block, block_x):
        return [block, *block_x, *[across_cores(p) for p in (block, *block_x)]]

    def work(pieces):
        return mlp_block(weights, weight_ids, pieces, row_ids, pieces[0].shape[0] // run)

    pieces_0 = shared(near, near_x)
    next_2e, next_2m, next_1_x, pieces_0 = lax.optimization_barrier((next_2e, next_2m, next_1_x, pieces_0))
    kv_send = after(kv_send, next_2e, next_2m)
    kv_in = lax.all_to_all(
        kv_send.reshape(n_req, PAGE, 2 * kv_heads * HD), "req", split_axis=0, concat_axis=0, tiled=True
    )
    next_3 = along_z(next_2m, outward)
    next_2 = jnp.where(at_end, next_2e, next_2m)
    next_2_x = along_x(next_2)
    hidden_0 = work(pieces_0)
    hidden_1 = work(shared(next_1, next_1_x))
    next_3, next_2_x, hidden_0, hidden_1, kv_in = lax.optimization_barrier(
        (next_3, next_2_x, hidden_0, hidden_1, kv_in)
    )
    next_3a = jnp.where(at_end, next_3[:run], middle_1[:run])
    next_3b = jnp.where(at_end, next_3[run:], middle_1[run:])
    next_3a_x = along_x(next_3a)
    hidden_2 = work(shared(next_2, next_2_x))
    back_1 = along_z(hidden_1, flip[1])
    mine = page_table[None] == (me_req * REQS + jnp.arange(REQS, dtype=jnp.int32))[:, None, None]
    sources = jnp.sum(jnp.where(mine, jnp.arange(n_req, dtype=jnp.int32)[None, :, None], 0), axis=(1, 2))
    cache_out = write_cache(sources.astype(jnp.int32), kv_in, kv_heads)
    next_3b, next_3a_x, hidden_2, back_1, cache_out = lax.optimization_barrier(
        (next_3b, next_3a_x, hidden_2, back_1, cache_out)
    )
    next_3b_x = along_x(next_3b)
    back_2 = along_z(hidden_2, flip[2])
    hidden_3a = work(shared(next_3a, next_3a_x))
    next_3b_x, hidden_3a = lax.optimization_barrier((next_3b_x, hidden_3a))
    back_3a = along_z(hidden_3a, flip[3])
    back_3b = along_z(work(shared(next_3b, next_3b_x)), flip[3])
    hidden_t = jnp.zeros((units_all, rows), jnp.bfloat16)
    for by, at, done in (
        (0, 0, hidden_0),
        (1, 0, back_1),
        (2, 0, back_2),
        (3, 0, back_3a),
        (3, rows // 2, back_3b),
    ):
        hidden_t = lax.dynamic_update_slice(hidden_t, done, ((z ^ by) * units, at))
    return hidden_t.T, cache_out


def solution(mesh):
    in_specs = (
        P("req", "mp"),
        P("req", "mp"),
        P("req", "mp"),
        P("mp"),
        P("mp"),
        P("mp"),
        P("req"),
        P(),
        P(),
        P("mp", None),
        P("req", None),
        P(),
        P("req", "mp"),
        P("req", "mp"),
    )
    out_specs = (P("req", "mp"), P("req", "mp", None, None))
    return jax.shard_map(shards, mesh=mesh, in_specs=in_specs, out_specs=out_specs, check_vma=False)
```

```python
import math

import jax
import jax.numpy as jnp
from jax import lax
from jax.experimental import pallas as pl
from jax.experimental.pallas import tpu as pltpu
from jax.sharding import PartitionSpec as P

HD = 128
PAGE = 128
REQS = 4
CORES = 2
N_Z = 4
THETA = 1000000.0
EPS = 1e-06
NT = (((1,), (1,)), ((), ()))


def rope_tables(positions):
    half_dim = HD // 2
    frequencies = THETA ** (-jnp.arange(half_dim, dtype=jnp.float32) * (2.0 / HD))
    angles = positions[:, None] * frequencies[None, :]
    cosine = jnp.cos(angles)
    sine = jnp.sin(angles)
    return jnp.concatenate([cosine, cosine], axis=-1), jnp.concatenate([-sine, sine], axis=-1)


def attention_kernel(order, q_ref, k_ref, v_ref, qb_ref, kb_ref, vb_ref, cos_ref, sin_ref, segc_ref, segr_ref,
                     slot_ref, out_ref, send_ref, q_buf, k_buf, v_buf, kv_buf):
    rows = q_ref.shape[0]
    kv_heads = k_ref.shape[1] // HD
    q_heads = q_ref.shape[1] // HD
    group = q_heads // kv_heads
    live = segc_ref[...] >= 0
    cosine = cos_ref[...]
    sine = sin_ref[...]

    def turned(source, bias, head):
        cols = slice(head * HD, (head + 1) * HD)
        raw = source[:, cols].astype(jnp.float32) + bias[:, cols]
        return jnp.where(live, raw * cosine + pltpu.roll(raw, HD // 2, 1) * sine, 0.0).astype(jnp.bfloat16)

    for head in range(q_heads):
        q_buf[:, head * HD:(head + 1) * HD] = turned(q_ref, qb_ref, head)
    for head in range(kv_heads):
        cols = slice(head * HD, (head + 1) * HD)
        key = turned(k_ref, kb_ref, head)
        value = jnp.where(live, v_ref[:, cols].astype(jnp.float32) + vb_ref[:, cols], 0.0).astype(jnp.bfloat16)
        k_buf[:, cols] = key
        v_buf[:, cols] = value
        kv_buf[:, 2 * head * HD:(2 * head + 1) * HD] = key
        kv_buf[:, (2 * head + 1) * HD:(2 * head + 2) * HD] = value
    slots = slot_ref[...]
    for part in range(send_ref.shape[0] // rows):
        wanted = lax.broadcasted_iota(jnp.int32, (rows, rows), 0) + part * rows
        pick = jnp.where(wanted == slots, 1.0, 0.0).astype(jnp.bfloat16)
        send_ref[part * rows:(part + 1) * rows, :] = jnp.dot(
            pick, kv_buf[...], preferred_element_type=jnp.float32
        ).astype(jnp.bfloat16)
    scale = 1.0 / math.sqrt(HD)
    tile = PAGE
    for start in range(0, rows, tile):
        low = max(0, start - tile)
        high = start + tile
        seg_q = segc_ref[start:high, :]
        seg_k = segr_ref[:, low:high]
        row_at = lax.broadcasted_iota(jnp.int32, (tile, high - low), 0) + start
        col_at = lax.broadcasted_iota(jnp.int32, (tile, high - low), 1) + low
        allowed = (seg_q == seg_k) & (seg_k >= 0) & (col_at <= row_at)
        for head in range(q_heads):
            kv = head // group
            kv_cols = slice(kv * HD, (kv + 1) * HD)
            scores = lax.dot_general(
                q_buf[start:high, head * HD:(head + 1) * HD], k_buf[low:high, kv_cols], NT,
                preferred_element_type=jnp.float32,
            ) * scale
            row_max = jnp.max(jnp.where(allowed, scores, -1e30), axis=-1, keepdims=True)
            weights = jnp.where(allowed, jnp.exp(scores - row_max), 0.0)
            total = jnp.sum(weights, axis=-1, keepdims=True)
            probs = (weights / jnp.where(total > 0.0, total, 1.0)).astype(jnp.bfloat16)
            mixed = jnp.dot(
                probs, v_buf[low:high, kv_cols], preferred_element_type=jnp.float32
            ).astype(jnp.bfloat16)
            size = rows // len(order)
            for at in range(0, tile, size):
                to = order[(start + at) // size] * size
                out_ref[to:to + size, head * HD:(head + 1) * HD] = mixed[at:at + size]


def attention(q_pre, k_pre, v_pre, q_bias, k_bias, v_bias, cosine, sine, segs, slots, slot_count, order):
    rows, q_cols = q_pre.shape
    kv_cols = k_pre.shape[1]
    vmem = pl.BlockSpec(memory_space=pltpu.VMEM)
    return pl.pallas_call(
        lambda *refs: attention_kernel(order, *refs),
        out_shape=(
            jax.ShapeDtypeStruct((rows, q_cols), jnp.bfloat16),
            jax.ShapeDtypeStruct((slot_count, 2 * kv_cols), jnp.bfloat16),
        ),
        in_specs=[vmem] * 11,
        out_specs=(vmem, vmem),
        scratch_shapes=[
            pltpu.VMEM((rows, q_cols), jnp.bfloat16),
            pltpu.VMEM((rows, kv_cols), jnp.bfloat16),
            pltpu.VMEM((rows, kv_cols), jnp.bfloat16),
            pltpu.VMEM((rows, 2 * kv_cols), jnp.bfloat16),
        ],
        compiler_params=pltpu.CompilerParams(vmem_limit_bytes=32 * 2**20),
        cost_estimate=pl.CostEstimate(flops=10**8, bytes_accessed=2**16, transcendentals=0),
        name="attention",
    )(q_pre, k_pre, v_pre, q_bias[None], k_bias[None], v_bias[None], cosine, sine, segs[:, None], segs[None],
      slots[None])


def cache_kernel(source_ref, in_ref, out_ref):
    for page in range(out_ref.shape[0]):
        for head in range(out_ref.shape[1]):
            out_ref[page, head] = in_ref[source_ref[page], :, head * 2 * HD:(head + 1) * 2 * HD]


def write_cache(sources, pages_in, kv_heads):
    vmem = pl.BlockSpec(memory_space=pltpu.VMEM)
    return pl.pallas_call(
        cache_kernel,
        out_shape=jax.ShapeDtypeStruct((REQS, kv_heads, PAGE, 2 * HD), jnp.bfloat16),
        in_specs=[pl.BlockSpec(memory_space=pltpu.SMEM), vmem],
        out_specs=vmem,
        cost_estimate=pl.CostEstimate(flops=0, bytes_accessed=2**16, transcendentals=0),
        name="write_cache",
    )(sources, pages_in)


def mlp_kernel(count, pieces, halves, ids_ref, *refs):
    weights = (refs[:count], refs[count:2 * count])
    rows_in = refs[2 * count:2 * count + pieces]
    out_ref, gate_buf, up_buf, row_buf, acc, weight_sems, row_sems = refs[2 * count + pieces:]
    units, depth = weights[0][0].shape
    parts = weight_sems.shape[2]
    piece = rows_in[0].shape[0] // halves
    first, second = [], []
    for index in range(pieces):
        for half in range(halves):
            at = pl.multiple_of((half * pieces + ids_ref[count + index]) * piece, piece)
            first.append(
                pltpu.make_async_copy(
                    rows_in[index].at[pl.ds(half * piece, piece), :],
                    row_buf.at[pl.ds(at, piece), :],
                    row_sems.at[index, half],
                )
            )
    for index in range(count):
        for which, buf in ((0, gate_buf), (1, up_buf)):
            for part in range(parts):
                some = pl.ds(part * (units // parts), units // parts)
                second.append(
                    pltpu.make_async_copy(
                        weights[which][index].at[some, :], buf.at[index, some, :], weight_sems.at[which, index, part]
                    )
                )
    for copy in first + second:
        copy.start()
    for copy in first:
        copy.wait()
    tokens = out_ref.shape[1]
    tile = min(256, tokens)
    for index in range(count):
        for copy in second[2 * parts * index:2 * parts * (index + 1)]:
            copy.wait()
        at = pl.multiple_of(ids_ref[index] * depth, depth)
        for start in range(0, tokens, tile):
            block = row_buf[start:start + tile, pl.ds(at, depth)]
            for which, buf in ((0, gate_buf), (1, up_buf)):
                term = lax.dot_general(buf[index], block, NT, preferred_element_type=jnp.float32)
                if index:
                    term = acc[which, :, start:start + tile] + term
                acc[which, :, start:start + tile] = term
    for start in range(0, tokens, tile):
        gate = acc[0, :, start:start + tile]
        up = acc[1, :, start:start + tile]
        out_ref[:, start:start + tile] = (gate / (1.0 + jnp.exp(-gate)) * up).astype(jnp.bfloat16)


def mlp_block(weights, weight_ids, rows_in, row_ids, halves):
    count, pieces = len(weight_ids), len(row_ids)
    units, depth = weights[0].shape
    width = rows_in[0].shape[1]
    piece = rows_in[0].shape[0] // halves
    tokens = piece * pieces * halves
    if depth % 128 or units % 16 or piece % 16:
        both = jnp.zeros((2, units, width), jnp.bfloat16)
        for index in range(count):
            pair = jnp.stack([weights[index], weights[count + index]])
            both = lax.dynamic_update_slice(both, pair, (0, 0, weight_ids[index] * depth))
        rows = jnp.zeros((tokens, width), jnp.bfloat16)
        for index in range(pieces):
            for half in range(halves):
                at = (half * pieces + row_ids[index]) * piece
                rows = lax.dynamic_update_slice(rows, rows_in[index][half * piece:(half + 1) * piece], (at, 0))
        gate = lax.dot_general(both[0], rows, NT, preferred_element_type=jnp.float32)
        up = lax.dot_general(both[1], rows, NT, preferred_element_type=jnp.float32)
        return (jax.nn.silu(gate) * up).astype(jnp.bfloat16)
    ids = jnp.stack([jnp.asarray(i, jnp.int32) for i in list(weight_ids) + list(row_ids)])
    anywhere = pl.BlockSpec(memory_space=pl.ANY)
    return pl.pallas_call(
        lambda *refs: mlp_kernel(count, pieces, halves, *refs),
        out_shape=jax.ShapeDtypeStruct((units, tokens), jnp.bfloat16),
        in_specs=[pl.BlockSpec(memory_space=pltpu.SMEM)] + [anywhere] * (2 * count + pieces),
        out_specs=pl.BlockSpec(memory_space=pltpu.VMEM),
        scratch_shapes=[
            pltpu.VMEM((count, units, depth), jnp.bfloat16),
            pltpu.VMEM((count, units, depth), jnp.bfloat16),
            pltpu.VMEM((tokens, width), jnp.bfloat16),
            pltpu.VMEM((2, units, tokens), jnp.float32),
            pltpu.SemaphoreType.DMA((2, count, 3 if units % 48 == 0 else 1)),
            pltpu.SemaphoreType.DMA((pieces, halves)),
        ],
        compiler_params=pltpu.CompilerParams(vmem_limit_bytes=60 * 2**20),
        cost_estimate=pl.CostEstimate(flops=10**8, bytes_accessed=2**16, transcendentals=0),
        name="mlp_block",
    )(ids, *weights, *rows_in)


def after(value, *before):
    return lax.optimization_barrier((value,) + before)[0]


def shards(q_pre, k_pre, v_pre, q_bias, k_bias, v_bias, segment_ids, lengths, page_table, w_out, residual,
           norm_gain, w_gate, w_up):
    me_req = lax.axis_index("req")
    me_mp = lax.axis_index("mp")
    n_req = lax.axis_size("req")
    n_mp = lax.axis_size("mp")
    n_y = n_req // N_Z
    n_x = n_mp // CORES
    z = me_req // n_y
    y = me_req % n_y
    x = me_mp // CORES
    core = me_mp % CORES

    def along_z(value, moves):
        return lax.ppermute(value, "req", [(a * n_y + c, b * n_y + c) for a, b in moves for c in range(n_y)])

    def turn_z(value, shift):
        return along_z(value, [(a, (a + shift) % N_Z) for a in range(N_Z)])

    def along_y(value):
        return [
            lax.ppermute(
                value, "req", [(a * n_y + b, a * n_y + (b + step) % n_y) for a in range(N_Z) for b in range(n_y)]
            )
            for step in range(1, n_y)
        ]

    def along_x(value):
        return [
            lax.ppermute(
                value,
                "mp",
                [(a * CORES + b, (a + step) % n_x * CORES + b) for a in range(n_x) for b in range(CORES)],
            )
            for step in range(1, n_x)
        ]

    def across_cores(value):
        return lax.ppermute(
            value, "mp", [(a * CORES + b, a * CORES + 1 - b) for a in range(n_x) for b in range(CORES)]
        )

    units_all, depth = w_gate.shape[1], w_gate.shape[0]
    units = units_all // N_Z

    def share(weight_t, shift):
        return lax.dynamic_slice(weight_t, ((z + shift) % N_Z * units, 0), (units, depth))

    def source_ids(shift):
        source_z = (z - shift) % N_Z
        return [source_z * n_y + (y - step) % n_y for step in range(n_y)]

    gate_t, up_t = w_gate.T, w_up.T
    gate_2 = share(gate_t, 2)
    gate_t, up_t, gate_2, q_pre, segment_ids = lax.optimization_barrier((gate_t, up_t, gate_2, q_pre, segment_ids))
    gate_0, up_0 = share(gate_t, 0), share(up_t, 0)
    gate_2 = turn_z(gate_2, 2)
    gate_0_y = along_y(gate_0)

    rows = q_pre.shape[0]
    kv_heads = k_pre.shape[1] // HD
    own_lens = lax.dynamic_index_in_dim(lengths, me_req, 0, keepdims=False)
    own_pages = lax.dynamic_index_in_dim(page_table, me_req, 0, keepdims=False)
    own_owner = own_pages // REQS
    starts = jnp.cumsum(own_lens) - own_lens
    alive = segment_ids >= 0
    req_idx = jnp.clip(segment_ids - me_req * REQS, 0, REQS - 1)
    hit = req_idx[:, None] == jnp.arange(REQS)[None, :]
    row_start = jnp.sum(jnp.where(hit, starts[None, :], 0), axis=1)
    row_owner = jnp.sum(jnp.where(hit, own_owner[None, :], 0), axis=1)
    row_pos = jnp.arange(rows, dtype=jnp.int32) - row_start
    slots = jnp.where(alive, row_owner * PAGE + row_pos, -1)
    cosine, sine = rope_tables(row_pos.astype(jnp.float32))
    run = rows // n_mp // 2
    order = []
    for group in range(2 * n_mp):
        half, device = divmod(group, n_mp)
        order.append((device % CORES * n_x + device // CORES) * 2 + half)
    attended, kv_send = attention(
        q_pre, k_pre, v_pre, q_bias, k_bias, v_bias, cosine, sine, segment_ids, slots, n_req * PAGE, order
    )
    attended = attended.reshape(CORES, n_x * 2 * run, attended.shape[1])

    def project(which):
        picked = lax.dynamic_index_in_dim(attended, which, 0, keepdims=False)
        return jnp.dot(picked, w_out, preferred_element_type=jnp.float32).astype(jnp.bfloat16)

    kept, given = project(core), project(1 - core)
    up_2, up_0, gate_2, gate_0_y, kept, given = lax.optimization_barrier(
        (share(up_t, 2), up_0, gate_2, gate_0_y, kept, given)
    )
    up_2 = turn_z(up_2, 2)
    up_0_y = along_y(up_0)
    gate_2_y = along_y(gate_2)
    sibling = across_cores(given)
    width = sibling.shape[1]
    gate_1, up_2, up_0_y, gate_2_y, sibling = lax.optimization_barrier(
        (share(gate_t, 1), up_2, up_0_y, gate_2_y, sibling)
    )
    gate_1 = turn_z(gate_1, 1)
    up_2_y = along_y(up_2)
    pair = (kept.astype(jnp.float32) + sibling.astype(jnp.float32)).reshape(n_x, 2 * run, width)
    summed = lax.dynamic_index_in_dim(pair, x, 0, keepdims=False)
    outgoing = [
        lax.dynamic_index_in_dim(pair, (x + step) % n_x, 0, keepdims=False).astype(jnp.bfloat16)
        for step in range(1, n_x)
    ]
    gate_3, up_3, gate_1, up_2_y, outgoing = lax.optimization_barrier(
        (share(gate_t, 3), share(up_t, 3), gate_1, up_2_y, outgoing)
    )
    gate_3, up_3 = turn_z(gate_3, 3), turn_z(up_3, 3)
    gate_1_y = along_y(gate_1)
    incoming = [
        lax.ppermute(
            outgoing[step - 1],
            "mp",
            [(a * CORES + b, (a + step) % n_x * CORES + b) for a in range(n_x) for b in range(CORES)],
        )
        for step in range(1, n_x)
    ]
    up_1, gate_3, up_3, gate_1_y, incoming = lax.optimization_barrier(
        (share(up_t, 1), gate_3, up_3, gate_1_y, incoming)
    )
    up_1 = turn_z(up_1, 1)
    gate_3_y = along_y(gate_3)
    residual_rows = jnp.concatenate(
        [
            lax.dynamic_slice(residual, (me_mp * run, 0), (run, width)),
            lax.dynamic_slice(residual, (rows // 2 + me_mp * run, 0), (run, width)),
        ]
    )
    for other in incoming:
        summed = summed + other.astype(jnp.float32)
    state = residual_rows.astype(jnp.float32) + summed
    scale = lax.rsqrt(jnp.mean(state * state, axis=-1, keepdims=True) + EPS)
    normed = (state * scale * norm_gain).astype(jnp.bfloat16)
    near, up_1, gate_3_y = lax.optimization_barrier((normed, up_1, gate_3_y))

    row_ids = [(x - step) % n_x * CORES + core for step in range(n_x)]
    row_ids += [(x - step) % n_x * CORES + 1 - core for step in range(n_x)]
    flip = [[(a, a ^ by) for a in range(N_Z)] for by in range(N_Z)]
    middle = [(1, 2), (2, 1)]
    outward = [(1, 0), (2, 3)]
    at_end = (z == 0) | (z == N_Z - 1)
    up_1_y, up_3_y = along_y(up_1), along_y(up_3)
    near_x = along_x(near)
    next_1, middle_1 = along_z(near, flip[1]), along_z(near, middle)
    next_1, middle_1, up_1_y, up_3_y, near_x = lax.optimization_barrier((next_1, middle_1, up_1_y, up_3_y, near_x))
    next_2e, next_2m = along_z(middle_1, outward), along_z(next_1, middle)
    next_1_x = along_x(next_1)

    gates = [gate_0, *gate_0_y, gate_2, *gate_2_y, gate_1, *gate_1_y, gate_3, *gate_3_y]
    ups = [up_0, *up_0_y, up_2, *up_2_y, up_1, *up_1_y, up_3, *up_3_y]
    weights = gates + ups
    weight_ids = [i for shift in (0, 2, 1, 3) for i in source_ids(shift)]

    def shared(block, block_x):
        return [block, *block_x, *[across_cores(p) for p in (block, *block_x)]]

    def work(pieces):
        return mlp_block(weights, weight_ids, pieces, row_ids, pieces[0].shape[0] // run)

    pieces_0 = shared(near, near_x)
    next_2e, next_2m, next_1_x, pieces_0 = lax.optimization_barrier((next_2e, next_2m, next_1_x, pieces_0))
    next_3 = along_z(next_2m, outward)
    next_2 = jnp.where(at_end, next_2e, next_2m)
    next_2_x = along_x(next_2)
    hidden_0 = work(pieces_0)
    hidden_0, kv_send = lax.optimization_barrier((hidden_0, kv_send))
    kv_in = lax.all_to_all(
        kv_send.reshape(n_req, PAGE, 2 * kv_heads * HD), "req", split_axis=0, concat_axis=0, tiled=True
    )
    hidden_1 = work(shared(next_1, next_1_x))
    next_3, next_2_x, hidden_0, hidden_1 = lax.optimization_barrier((next_3, next_2_x, hidden_0, hidden_1))
    next_3a = jnp.where(at_end, next_3[:run], middle_1[:run])
    next_3b = jnp.where(at_end, next_3[run:], middle_1[run:])
    next_3a_x = along_x(next_3a)
    hidden_2 = work(shared(next_2, next_2_x))
    back_1 = along_z(hidden_1, flip[1])
    next_3b, next_3a_x, hidden_2, back_1, kv_in = lax.optimization_barrier(
        (next_3b, next_3a_x, hidden_2, back_1, kv_in)
    )
    next_3b_x = along_x(next_3b)
    back_2 = along_z(hidden_2, flip[2])
    hidden_3a = work(shared(next_3a, next_3a_x))
    mine = page_table[None] == (me_req * REQS + jnp.arange(REQS, dtype=jnp.int32))[:, None, None]
    sources = jnp.sum(jnp.where(mine, jnp.arange(n_req, dtype=jnp.int32)[None, :, None], 0), axis=(1, 2))
    cache_out = write_cache(sources.astype(jnp.int32), kv_in, kv_heads)
    next_3b_x, hidden_3a, back_2, cache_out = lax.optimization_barrier((next_3b_x, hidden_3a, back_2, cache_out))
    back_3a = along_z(hidden_3a, flip[3])
    back_3b = along_z(work(shared(next_3b, next_3b_x)), flip[3])
    hidden_t = jnp.zeros((units_all, rows), jnp.bfloat16)
    for by, at, done in (
        (0, 0, hidden_0),
        (1, 0, back_1),
        (2, 0, back_2),
        (3, 0, back_3a),
        (3, rows // 2, back_3b),
    ):
        hidden_t = lax.dynamic_update_slice(hidden_t, done, ((z ^ by) * units, at))
    return hidden_t.T, cache_out


def solution(mesh):
    in_specs = (
        P("req", "mp"),
        P("req", "mp"),
        P("req", "mp"),
        P("mp"),
        P("mp"),
        P("mp"),
        P("req"),
        P(),
        P(),
        P("mp", None),
        P("req", None),
        P(),
        P("req", "mp"),
        P("req", "mp"),
    )
    out_specs = (P("req", "mp"), P("req", "mp", None, None))
    return jax.shard_map(shards, mesh=mesh, in_specs=in_specs, out_specs=out_specs, check_vma=False)
```

```python
import math

import jax
import jax.numpy as jnp
from jax import lax
from jax.experimental import pallas as pl
from jax.experimental.pallas import tpu as pltpu
from jax.sharding import PartitionSpec as P

HD = 128
PAGE = 128
REQS = 4
CORES = 2
N_Z = 4
THETA = 1000000.0
EPS = 1e-06
NT = (((1,), (1,)), ((), ()))


def rope_tables(positions):
    half_dim = HD // 2
    frequencies = THETA ** (-jnp.arange(half_dim, dtype=jnp.float32) * (2.0 / HD))
    angles = positions[:, None] * frequencies[None, :]
    cosine = jnp.cos(angles)
    sine = jnp.sin(angles)
    return jnp.concatenate([cosine, cosine], axis=-1), jnp.concatenate([-sine, sine], axis=-1)


def attention_kernel(order, q_ref, k_ref, v_ref, qb_ref, kb_ref, vb_ref, cos_ref, sin_ref, segc_ref, segr_ref,
                     slot_ref, out_ref, send_ref, q_buf, k_buf, v_buf, kv_buf):
    rows = q_ref.shape[0]
    kv_heads = k_ref.shape[1] // HD
    q_heads = q_ref.shape[1] // HD
    group = q_heads // kv_heads
    live = segc_ref[...] >= 0
    cosine = cos_ref[...]
    sine = sin_ref[...]

    def turned(source, bias, head):
        cols = slice(head * HD, (head + 1) * HD)
        raw = source[:, cols].astype(jnp.float32) + bias[:, cols]
        return jnp.where(live, raw * cosine + pltpu.roll(raw, HD // 2, 1) * sine, 0.0).astype(jnp.bfloat16)

    for head in range(q_heads):
        q_buf[:, head * HD:(head + 1) * HD] = turned(q_ref, qb_ref, head)
    for head in range(kv_heads):
        cols = slice(head * HD, (head + 1) * HD)
        key = turned(k_ref, kb_ref, head)
        value = jnp.where(live, v_ref[:, cols].astype(jnp.float32) + vb_ref[:, cols], 0.0).astype(jnp.bfloat16)
        k_buf[:, cols] = key
        v_buf[:, cols] = value
        kv_buf[:, 2 * head * HD:(2 * head + 1) * HD] = key
        kv_buf[:, (2 * head + 1) * HD:(2 * head + 2) * HD] = value
    slots = slot_ref[...]
    for part in range(send_ref.shape[0] // rows):
        wanted = lax.broadcasted_iota(jnp.int32, (rows, rows), 0) + part * rows
        pick = jnp.where(wanted == slots, 1.0, 0.0).astype(jnp.bfloat16)
        send_ref[part * rows:(part + 1) * rows, :] = jnp.dot(
            pick, kv_buf[...], preferred_element_type=jnp.float32
        ).astype(jnp.bfloat16)
    scale = 1.0 / math.sqrt(HD)
    tile = PAGE
    for start in range(0, rows, tile):
        low = max(0, start - tile)
        high = start + tile
        seg_q = segc_ref[start:high, :]
        seg_k = segr_ref[:, low:high]
        row_at = lax.broadcasted_iota(jnp.int32, (tile, high - low), 0) + start
        col_at = lax.broadcasted_iota(jnp.int32, (tile, high - low), 1) + low
        allowed = (seg_q == seg_k) & (seg_k >= 0) & (col_at <= row_at)
        for head in range(q_heads):
            kv = head // group
            kv_cols = slice(kv * HD, (kv + 1) * HD)
            scores = lax.dot_general(
                q_buf[start:high, head * HD:(head + 1) * HD], k_buf[low:high, kv_cols], NT,
                preferred_element_type=jnp.float32,
            ) * scale
            row_max = jnp.max(jnp.where(allowed, scores, -1e30), axis=-1, keepdims=True)
            weights = jnp.where(allowed, jnp.exp(scores - row_max), 0.0)
            total = jnp.sum(weights, axis=-1, keepdims=True)
            probs = (weights / jnp.where(total > 0.0, total, 1.0)).astype(jnp.bfloat16)
            mixed = jnp.dot(
                probs, v_buf[low:high, kv_cols], preferred_element_type=jnp.float32
            ).astype(jnp.bfloat16)
            size = rows // len(order)
            for at in range(0, tile, size):
                to = order[(start + at) // size] * size
                out_ref[to:to + size, head * HD:(head + 1) * HD] = mixed[at:at + size]


def attention(q_pre, k_pre, v_pre, q_bias, k_bias, v_bias, cosine, sine, segs, slots, slot_count, order):
    rows, q_cols = q_pre.shape
    kv_cols = k_pre.shape[1]
    vmem = pl.BlockSpec(memory_space=pltpu.VMEM)
    return pl.pallas_call(
        lambda *refs: attention_kernel(order, *refs),
        out_shape=(
            jax.ShapeDtypeStruct((rows, q_cols), jnp.bfloat16),
            jax.ShapeDtypeStruct((slot_count, 2 * kv_cols), jnp.bfloat16),
        ),
        in_specs=[vmem] * 11,
        out_specs=(vmem, vmem),
        scratch_shapes=[
            pltpu.VMEM((rows, q_cols), jnp.bfloat16),
            pltpu.VMEM((rows, kv_cols), jnp.bfloat16),
            pltpu.VMEM((rows, kv_cols), jnp.bfloat16),
            pltpu.VMEM((rows, 2 * kv_cols), jnp.bfloat16),
        ],
        compiler_params=pltpu.CompilerParams(vmem_limit_bytes=32 * 2**20),
        cost_estimate=pl.CostEstimate(flops=10**8, bytes_accessed=2**16, transcendentals=0),
        name="attention",
    )(q_pre, k_pre, v_pre, q_bias[None], k_bias[None], v_bias[None], cosine, sine, segs[:, None], segs[None],
      slots[None])


def cache_kernel(source_ref, in_ref, out_ref):
    for page in range(out_ref.shape[0]):
        for head in range(out_ref.shape[1]):
            out_ref[page, head] = in_ref[source_ref[page], :, head * 2 * HD:(head + 1) * 2 * HD]


def write_cache(sources, pages_in, kv_heads):
    vmem = pl.BlockSpec(memory_space=pltpu.VMEM)
    return pl.pallas_call(
        cache_kernel,
        out_shape=jax.ShapeDtypeStruct((REQS, kv_heads, PAGE, 2 * HD), jnp.bfloat16),
        in_specs=[pl.BlockSpec(memory_space=pltpu.SMEM), vmem],
        out_specs=vmem,
        cost_estimate=pl.CostEstimate(flops=0, bytes_accessed=2**16, transcendentals=0),
        name="write_cache",
    )(sources, pages_in)


def mlp_kernel(count, pieces, halves, ids_ref, *refs):
    weights = (refs[:count], refs[count:2 * count])
    rows_in = refs[2 * count:2 * count + pieces]
    out_ref, gate_buf, up_buf, row_buf, acc, weight_sems, row_sems = refs[2 * count + pieces:]
    units, depth = weights[0][0].shape
    parts = weight_sems.shape[2]
    piece = rows_in[0].shape[0] // halves
    first, second = [], []
    for index in range(pieces):
        for half in range(halves):
            at = pl.multiple_of((half * pieces + ids_ref[count + index]) * piece, piece)
            first.append(
                pltpu.make_async_copy(
                    rows_in[index].at[pl.ds(half * piece, piece), :],
                    row_buf.at[pl.ds(at, piece), :],
                    row_sems.at[index, half],
                )
            )
    for index in range(count):
        for which, buf in ((0, gate_buf), (1, up_buf)):
            for part in range(parts):
                some = pl.ds(part * (units // parts), units // parts)
                second.append(
                    pltpu.make_async_copy(
                        weights[which][index].at[some, :], buf.at[index, some, :], weight_sems.at[which, index, part]
                    )
                )
    for copy in first + second:
        copy.start()
    for copy in first:
        copy.wait()
    tokens = out_ref.shape[1]
    tile = min(256, tokens)
    for index in range(count):
        for copy in second[2 * parts * index:2 * parts * (index + 1)]:
            copy.wait()
        at = pl.multiple_of(ids_ref[index] * depth, depth)
        for start in range(0, tokens, tile):
            block = row_buf[start:start + tile, pl.ds(at, depth)]
            for which, buf in ((0, gate_buf), (1, up_buf)):
                term = lax.dot_general(buf[index], block, NT, preferred_element_type=jnp.float32)
                if index:
                    term = acc[which, :, start:start + tile] + term
                acc[which, :, start:start + tile] = term
    for start in range(0, tokens, tile):
        gate = acc[0, :, start:start + tile]
        up = acc[1, :, start:start + tile]
        out_ref[:, start:start + tile] = (gate / (1.0 + jnp.exp(-gate)) * up).astype(jnp.bfloat16)


def mlp_block(weights, weight_ids, rows_in, row_ids, halves):
    count, pieces = len(weight_ids), len(row_ids)
    units, depth = weights[0].shape
    width = rows_in[0].shape[1]
    piece = rows_in[0].shape[0] // halves
    tokens = piece * pieces * halves
    if depth % 128 or units % 16 or piece % 16:
        both = jnp.zeros((2, units, width), jnp.bfloat16)
        for index in range(count):
            pair = jnp.stack([weights[index], weights[count + index]])
            both = lax.dynamic_update_slice(both, pair, (0, 0, weight_ids[index] * depth))
        rows = jnp.zeros((tokens, width), jnp.bfloat16)
        for index in range(pieces):
            for half in range(halves):
                at = (half * pieces + row_ids[index]) * piece
                rows = lax.dynamic_update_slice(rows, rows_in[index][half * piece:(half + 1) * piece], (at, 0))
        gate = lax.dot_general(both[0], rows, NT, preferred_element_type=jnp.float32)
        up = lax.dot_general(both[1], rows, NT, preferred_element_type=jnp.float32)
        return (jax.nn.silu(gate) * up).astype(jnp.bfloat16)
    ids = jnp.stack([jnp.asarray(i, jnp.int32) for i in list(weight_ids) + list(row_ids)])
    anywhere = pl.BlockSpec(memory_space=pl.ANY)
    return pl.pallas_call(
        lambda *refs: mlp_kernel(count, pieces, halves, *refs),
        out_shape=jax.ShapeDtypeStruct((units, tokens), jnp.bfloat16),
        in_specs=[pl.BlockSpec(memory_space=pltpu.SMEM)] + [anywhere] * (2 * count + pieces),
        out_specs=pl.BlockSpec(memory_space=pltpu.VMEM),
        scratch_shapes=[
            pltpu.VMEM((count, units, depth), jnp.bfloat16),
            pltpu.VMEM((count, units, depth), jnp.bfloat16),
            pltpu.VMEM((tokens, width), jnp.bfloat16),
            pltpu.VMEM((2, units, tokens), jnp.float32),
            pltpu.SemaphoreType.DMA((2, count, 3 if units % 48 == 0 else 1)),
            pltpu.SemaphoreType.DMA((pieces, halves)),
        ],
        compiler_params=pltpu.CompilerParams(vmem_limit_bytes=60 * 2**20),
        cost_estimate=pl.CostEstimate(flops=10**8, bytes_accessed=2**16, transcendentals=0),
        name="mlp_block",
    )(ids, *weights, *rows_in)


def after(value, *before):
    return lax.optimization_barrier((value,) + before)[0]


def shards(q_pre, k_pre, v_pre, q_bias, k_bias, v_bias, segment_ids, lengths, page_table, w_out, residual,
           norm_gain, w_gate, w_up):
    me_req = lax.axis_index("req")
    me_mp = lax.axis_index("mp")
    n_req = lax.axis_size("req")
    n_mp = lax.axis_size("mp")
    n_y = n_req // N_Z
    n_x = n_mp // CORES
    z = me_req // n_y
    y = me_req % n_y
    x = me_mp // CORES
    core = me_mp % CORES

    def along_z(value, moves):
        return lax.ppermute(value, "req", [(a * n_y + c, b * n_y + c) for a, b in moves for c in range(n_y)])

    def turn_z(value, shift):
        return along_z(value, [(a, (a + shift) % N_Z) for a in range(N_Z)])

    def along_y(value):
        return [
            lax.ppermute(
                value, "req", [(a * n_y + b, a * n_y + (b + step) % n_y) for a in range(N_Z) for b in range(n_y)]
            )
            for step in range(1, n_y)
        ]

    def along_x(value):
        return [
            lax.ppermute(
                value,
                "mp",
                [(a * CORES + b, (a + step) % n_x * CORES + b) for a in range(n_x) for b in range(CORES)],
            )
            for step in range(1, n_x)
        ]

    def across_cores(value):
        return lax.ppermute(
            value, "mp", [(a * CORES + b, a * CORES + 1 - b) for a in range(n_x) for b in range(CORES)]
        )

    units_all, depth = w_gate.shape[1], w_gate.shape[0]
    units = units_all // N_Z

    def share(weight_t, shift):
        return lax.dynamic_slice(weight_t, ((z + shift) % N_Z * units, 0), (units, depth))

    def source_ids(shift):
        source_z = (z - shift) % N_Z
        return [source_z * n_y + (y - step) % n_y for step in range(n_y)]

    gate_t, up_t = w_gate.T, w_up.T
    gate_2 = share(gate_t, 2)
    gate_t, up_t, gate_2, q_pre, segment_ids = lax.optimization_barrier((gate_t, up_t, gate_2, q_pre, segment_ids))
    gate_2 = turn_z(gate_2, 2)

    rows = q_pre.shape[0]
    kv_heads = k_pre.shape[1] // HD
    own_lens = lax.dynamic_index_in_dim(lengths, me_req, 0, keepdims=False)
    own_pages = lax.dynamic_index_in_dim(page_table, me_req, 0, keepdims=False)
    own_owner = own_pages // REQS
    starts = jnp.cumsum(own_lens) - own_lens
    alive = segment_ids >= 0
    req_idx = jnp.clip(segment_ids - me_req * REQS, 0, REQS - 1)
    hit = req_idx[:, None] == jnp.arange(REQS)[None, :]
    row_start = jnp.sum(jnp.where(hit, starts[None, :], 0), axis=1)
    row_owner = jnp.sum(jnp.where(hit, own_owner[None, :], 0), axis=1)
    row_pos = jnp.arange(rows, dtype=jnp.int32) - row_start
    slots = jnp.where(alive, row_owner * PAGE + row_pos, -1)
    cosine, sine = rope_tables(row_pos.astype(jnp.float32))
    run = rows // n_mp // 2
    order = []
    for group in range(2 * n_mp):
        half, device = divmod(group, n_mp)
        order.append((device % CORES * n_x + device // CORES) * 2 + half)
    attended, kv_send = attention(
        q_pre, k_pre, v_pre, q_bias, k_bias, v_bias, cosine, sine, segment_ids, slots, n_req * PAGE, order
    )
    attended = attended.reshape(CORES, n_x * 2 * run, attended.shape[1])

    def project(which):
        picked = lax.dynamic_index_in_dim(attended, which, 0, keepdims=False)
        return jnp.dot(picked, w_out, preferred_element_type=jnp.float32).astype(jnp.bfloat16)

    kept, given = project(core), project(1 - core)
    up_2, gate_0, up_0, gate_2, kept, given = lax.optimization_barrier(
        (share(up_t, 2), share(gate_t, 0), share(up_t, 0), gate_2, kept, given)
    )
    up_2 = turn_z(up_2, 2)
    gate_0_y, up_0_y = along_y(gate_0), along_y(up_0)
    sibling = across_cores(given)
    width = sibling.shape[1]
    gate_1, up_2, gate_0_y, up_0_y, gate_2, sibling = lax.optimization_barrier(
        (share(gate_t, 1), up_2, gate_0_y, up_0_y, gate_2, sibling)
    )
    gate_1 = turn_z(gate_1, 1)
    gate_2_y = along_y(gate_2)
    pair = (kept.astype(jnp.float32) + sibling.astype(jnp.float32)).reshape(n_x, 2 * run, width)
    summed = lax.dynamic_index_in_dim(pair, x, 0, keepdims=False)
    outgoing = [
        lax.dynamic_index_in_dim(pair, (x + step) % n_x, 0, keepdims=False).astype(jnp.bfloat16)
        for step in range(1, n_x)
    ]
    gate_3, up_3, gate_1, up_2, gate_2_y, outgoing = lax.optimization_barrier(
        (share(gate_t, 3), share(up_t, 3), gate_1, up_2, gate_2_y, outgoing)
    )
    gate_3, up_3 = turn_z(gate_3, 3), turn_z(up_3, 3)
    up_2_y = along_y(up_2)
    gate_1_y = along_y(gate_1)
    incoming = [
        lax.ppermute(
            outgoing[step - 1],
            "mp",
            [(a * CORES + b, (a + step) % n_x * CORES + b) for a in range(n_x) for b in range(CORES)],
        )
        for step in range(1, n_x)
    ]
    up_1, gate_3, up_3, gate_1_y, up_2_y, incoming = lax.optimization_barrier(
        (share(up_t, 1), gate_3, up_3, gate_1_y, up_2_y, incoming)
    )
    up_1 = turn_z(up_1, 1)
    gate_3_y = along_y(gate_3)
    residual_rows = jnp.concatenate(
        [
            lax.dynamic_slice(residual, (me_mp * run, 0), (run, width)),
            lax.dynamic_slice(residual, (rows // 2 + me_mp * run, 0), (run, width)),
        ]
    )
    for other in incoming:
        summed = summed + other.astype(jnp.float32)
    state = residual_rows.astype(jnp.float32) + summed
    scale = lax.rsqrt(jnp.mean(state * state, axis=-1, keepdims=True) + EPS)
    normed = (state * scale * norm_gain).astype(jnp.bfloat16)
    near, up_1, gate_3_y = lax.optimization_barrier((normed, up_1, gate_3_y))

    row_ids = [(x - step) % n_x * CORES + core for step in range(n_x)]
    row_ids += [(x - step) % n_x * CORES + 1 - core for step in range(n_x)]
    flip = [[(a, a ^ by) for a in range(N_Z)] for by in range(N_Z)]
    middle = [(1, 2), (2, 1)]
    outward = [(1, 0), (2, 3)]
    at_end = (z == 0) | (z == N_Z - 1)
    up_1_y, up_3_y = along_y(up_1), along_y(up_3)
    near_x = along_x(near)
    next_1, middle_1 = along_z(near, flip[1]), along_z(near, middle)
    next_1, middle_1, up_1_y, up_3_y, near_x = lax.optimization_barrier((next_1, middle_1, up_1_y, up_3_y, near_x))
    next_2e, next_2m = along_z(middle_1, outward), along_z(next_1, middle)
    next_1_x = along_x(next_1)

    gates = [gate_0, *gate_0_y, gate_2, *gate_2_y, gate_1, *gate_1_y, gate_3, *gate_3_y]
    ups = [up_0, *up_0_y, up_2, *up_2_y, up_1, *up_1_y, up_3, *up_3_y]
    weights = gates + ups
    weight_ids = [i for shift in (0, 2, 1, 3) for i in source_ids(shift)]

    def shared(block, block_x):
        return [block, *block_x, *[across_cores(p) for p in (block, *block_x)]]

    def work(pieces):
        return mlp_block(weights, weight_ids, pieces, row_ids, pieces[0].shape[0] // run)

    pieces_0 = shared(near, near_x)
    next_2e, next_2m, next_1_x, pieces_0 = lax.optimization_barrier((next_2e, next_2m, next_1_x, pieces_0))
    next_3 = along_z(next_2m, outward)
    next_2 = jnp.where(at_end, next_2e, next_2m)
    next_2_x = along_x(next_2)
    hidden_0 = work(pieces_0)
    hidden_0, kv_send = lax.optimization_barrier((hidden_0, kv_send))
    kv_in = lax.all_to_all(
        kv_send.reshape(n_req, PAGE, 2 * kv_heads * HD), "req", split_axis=0, concat_axis=0, tiled=True
    )
    hidden_1 = work(shared(next_1, next_1_x))
    next_3, next_2_x, hidden_0, hidden_1 = lax.optimization_barrier((next_3, next_2_x, hidden_0, hidden_1))
    next_3a = jnp.where(at_end, next_3[:run], middle_1[:run])
    next_3b = jnp.where(at_end, next_3[run:], middle_1[run:])
    next_3a_x = along_x(next_3a)
    hidden_2 = work(shared(next_2, next_2_x))
    back_1 = along_z(hidden_1, flip[1])
    next_3b, next_3a_x, hidden_2, back_1, kv_in = lax.optimization_barrier(
        (next_3b, next_3a_x, hidden_2, back_1, kv_in)
    )
    next_3b_x = along_x(next_3b)
    back_2 = [along_z(hidden_2[:, :rows // 2], flip[2]), along_z(hidden_2[:, rows // 2:], flip[2])]
    hidden_3a = work(shared(next_3a, next_3a_x))
    mine = page_table[None] == (me_req * REQS + jnp.arange(REQS, dtype=jnp.int32))[:, None, None]
    sources = jnp.sum(jnp.where(mine, jnp.arange(n_req, dtype=jnp.int32)[None, :, None], 0), axis=(1, 2))
    cache_out = write_cache(sources.astype(jnp.int32), kv_in, kv_heads)
    next_3b_x, hidden_3a, back_2[0], cache_out = lax.optimization_barrier(
        (next_3b_x, hidden_3a, back_2[0], cache_out)
    )
    back_3a = along_z(hidden_3a, flip[3])
    hidden_3b, back_2[1] = lax.optimization_barrier((work(shared(next_3b, next_3b_x)), back_2[1]))
    back_3b = along_z(hidden_3b, flip[3])
    hidden_t = jnp.zeros((units_all, rows), jnp.bfloat16)
    for by, at, done in (
        (0, 0, hidden_0),
        (1, 0, back_1),
        (2, 0, back_2[0]),
        (2, rows // 2, back_2[1]),
        (3, 0, back_3a),
        (3, rows // 2, back_3b),
    ):
        hidden_t = lax.dynamic_update_slice(hidden_t, done, ((z ^ by) * units, at))
    return hidden_t.T, cache_out


def solution(mesh):
    in_specs = (
        P("req", "mp"),
        P("req", "mp"),
        P("req", "mp"),
        P("mp"),
        P("mp"),
        P("mp"),
        P("req"),
        P(),
        P(),
        P("mp", None),
        P("req", None),
        P(),
        P("req", "mp"),
        P("req", "mp"),
    )
    out_specs = (P("req", "mp"), P("req", "mp", None, None))
    return jax.shard_map(shards, mesh=mesh, in_specs=in_specs, out_specs=out_specs, check_vma=False)
```

```python
import math

import jax
import jax.numpy as jnp
from jax import lax
from jax.experimental import pallas as pl
from jax.experimental.pallas import tpu as pltpu
from jax.sharding import PartitionSpec as P

HD = 128
PAGE = 128
REQS = 4
CORES = 2
N_Z = 4
THETA = 1000000.0
EPS = 1e-06
NT = (((1,), (1,)), ((), ()))


def rope_tables(positions):
    half_dim = HD // 2
    frequencies = THETA ** (-jnp.arange(half_dim, dtype=jnp.float32) * (2.0 / HD))
    angles = positions[:, None] * frequencies[None, :]
    cosine = jnp.cos(angles)
    sine = jnp.sin(angles)
    return jnp.concatenate([cosine, cosine], axis=-1), jnp.concatenate([-sine, sine], axis=-1)


def attention_kernel(order, q_ref, k_ref, v_ref, qb_ref, kb_ref, vb_ref, cos_ref, sin_ref, segc_ref, segr_ref,
                     slot_ref, out_ref, send_ref, q_buf, k_buf, v_buf, kv_buf):
    rows = q_ref.shape[0]
    kv_heads = k_ref.shape[1] // HD
    q_heads = q_ref.shape[1] // HD
    group = q_heads // kv_heads
    live = segc_ref[...] >= 0
    cosine = cos_ref[...]
    sine = sin_ref[...]

    def turned(source, bias, head):
        cols = slice(head * HD, (head + 1) * HD)
        raw = source[:, cols].astype(jnp.float32) + bias[:, cols]
        return jnp.where(live, raw * cosine + pltpu.roll(raw, HD // 2, 1) * sine, 0.0).astype(jnp.bfloat16)

    for head in range(q_heads):
        q_buf[:, head * HD:(head + 1) * HD] = turned(q_ref, qb_ref, head)
    for head in range(kv_heads):
        cols = slice(head * HD, (head + 1) * HD)
        key = turned(k_ref, kb_ref, head)
        value = jnp.where(live, v_ref[:, cols].astype(jnp.float32) + vb_ref[:, cols], 0.0).astype(jnp.bfloat16)
        k_buf[:, cols] = key
        v_buf[:, cols] = value
        kv_buf[:, 2 * head * HD:(2 * head + 1) * HD] = key
        kv_buf[:, (2 * head + 1) * HD:(2 * head + 2) * HD] = value
    slots = slot_ref[...]
    for part in range(send_ref.shape[0] // rows):
        wanted = lax.broadcasted_iota(jnp.int32, (rows, rows), 0) + part * rows
        pick = jnp.where(wanted == slots, 1.0, 0.0).astype(jnp.bfloat16)
        send_ref[part * rows:(part + 1) * rows, :] = jnp.dot(
            pick, kv_buf[...], preferred_element_type=jnp.float32
        ).astype(jnp.bfloat16)
    scale = 1.0 / math.sqrt(HD)
    tile = PAGE
    for start in range(0, rows, tile):
        low = max(0, start - tile)
        high = start + tile
        seg_q = segc_ref[start:high, :]
        seg_k = segr_ref[:, low:high]
        row_at = lax.broadcasted_iota(jnp.int32, (tile, high - low), 0) + start
        col_at = lax.broadcasted_iota(jnp.int32, (tile, high - low), 1) + low
        allowed = (seg_q == seg_k) & (seg_k >= 0) & (col_at <= row_at)
        for head in range(q_heads):
            kv = head // group
            kv_cols = slice(kv * HD, (kv + 1) * HD)
            scores = lax.dot_general(
                q_buf[start:high, head * HD:(head + 1) * HD], k_buf[low:high, kv_cols], NT,
                preferred_element_type=jnp.float32,
            ) * scale
            row_max = jnp.max(jnp.where(allowed, scores, -1e30), axis=-1, keepdims=True)
            weights = jnp.where(allowed, jnp.exp(scores - row_max), 0.0)
            total = jnp.sum(weights, axis=-1, keepdims=True)
            probs = (weights / jnp.where(total > 0.0, total, 1.0)).astype(jnp.bfloat16)
            mixed = jnp.dot(
                probs, v_buf[low:high, kv_cols], preferred_element_type=jnp.float32
            ).astype(jnp.bfloat16)
            size = rows // len(order)
            for at in range(0, tile, size):
                to = order[(start + at) // size] * size
                out_ref[to:to + size, head * HD:(head + 1) * HD] = mixed[at:at + size]


def attention(q_pre, k_pre, v_pre, q_bias, k_bias, v_bias, cosine, sine, segs, slots, slot_count, order):
    rows, q_cols = q_pre.shape
    kv_cols = k_pre.shape[1]
    vmem = pl.BlockSpec(memory_space=pltpu.VMEM)
    return pl.pallas_call(
        lambda *refs: attention_kernel(order, *refs),
        out_shape=(
            jax.ShapeDtypeStruct((rows, q_cols), jnp.bfloat16),
            jax.ShapeDtypeStruct((slot_count, 2 * kv_cols), jnp.bfloat16),
        ),
        in_specs=[vmem] * 11,
        out_specs=(vmem, vmem),
        scratch_shapes=[
            pltpu.VMEM((rows, q_cols), jnp.bfloat16),
            pltpu.VMEM((rows, kv_cols), jnp.bfloat16),
            pltpu.VMEM((rows, kv_cols), jnp.bfloat16),
            pltpu.VMEM((rows, 2 * kv_cols), jnp.bfloat16),
        ],
        compiler_params=pltpu.CompilerParams(vmem_limit_bytes=32 * 2**20),
        cost_estimate=pl.CostEstimate(flops=10**8, bytes_accessed=2**16, transcendentals=0),
        name="attention",
    )(q_pre, k_pre, v_pre, q_bias[None], k_bias[None], v_bias[None], cosine, sine, segs[:, None], segs[None],
      slots[None])


def cache_kernel(source_ref, in_ref, out_ref):
    for page in range(out_ref.shape[0]):
        for head in range(out_ref.shape[1]):
            out_ref[page, head] = in_ref[source_ref[page], :, head * 2 * HD:(head + 1) * 2 * HD]


def write_cache(sources, pages_in, kv_heads):
    vmem = pl.BlockSpec(memory_space=pltpu.VMEM)
    return pl.pallas_call(
        cache_kernel,
        out_shape=jax.ShapeDtypeStruct((REQS, kv_heads, PAGE, 2 * HD), jnp.bfloat16),
        in_specs=[pl.BlockSpec(memory_space=pltpu.SMEM), vmem],
        out_specs=vmem,
        cost_estimate=pl.CostEstimate(flops=0, bytes_accessed=2**16, transcendentals=0),
        name="write_cache",
    )(sources, pages_in)


def mlp_kernel(count, pieces, halves, outs, ids_ref, *refs):
    weights = (refs[:count], refs[count:2 * count])
    rows_in = refs[2 * count:2 * count + pieces]
    out_refs = refs[2 * count + pieces:2 * count + pieces + outs]
    gate_buf, up_buf, row_buf, acc, weight_sems, row_sems = refs[2 * count + pieces + outs:]
    units, depth = weights[0][0].shape
    parts = weight_sems.shape[2]
    piece = rows_in[0].shape[0] // halves
    first, second = [], []
    for index in range(pieces):
        for half in range(halves):
            at = pl.multiple_of((half * pieces + ids_ref[count + index]) * piece, piece)
            first.append(
                pltpu.make_async_copy(
                    rows_in[index].at[pl.ds(half * piece, piece), :],
                    row_buf.at[pl.ds(at, piece), :],
                    row_sems.at[index, half],
                )
            )
    for index in range(count):
        for which, buf in ((0, gate_buf), (1, up_buf)):
            for part in range(parts):
                some = pl.ds(part * (units // parts), units // parts)
                second.append(
                    pltpu.make_async_copy(
                        weights[which][index].at[some, :], buf.at[index, some, :], weight_sems.at[which, index, part]
                    )
                )
    for copy in first + second:
        copy.start()
    for copy in first:
        copy.wait()
    tokens, span = row_buf.shape[0], out_refs[0].shape[1]
    tile = min(256, span)
    for index in range(count):
        for copy in second[2 * parts * index:2 * parts * (index + 1)]:
            copy.wait()
        at = pl.multiple_of(ids_ref[index] * depth, depth)
        for start in range(0, tokens, tile):
            block = row_buf[start:start + tile, pl.ds(at, depth)]
            for which, buf in ((0, gate_buf), (1, up_buf)):
                term = lax.dot_general(buf[index], block, NT, preferred_element_type=jnp.float32)
                if index:
                    term = acc[which, :, start:start + tile] + term
                acc[which, :, start:start + tile] = term
    for start in range(0, tokens, tile):
        gate = acc[0, :, start:start + tile]
        up = acc[1, :, start:start + tile]
        at = start % span
        out_refs[start // span][:, at:at + tile] = (gate / (1.0 + jnp.exp(-gate)) * up).astype(jnp.bfloat16)


def mlp_block(weights, weight_ids, rows_in, row_ids, halves, outs):
    count, pieces = len(weight_ids), len(row_ids)
    units, depth = weights[0].shape
    width = rows_in[0].shape[1]
    piece = rows_in[0].shape[0] // halves
    tokens = piece * pieces * halves
    if depth % 128 or units % 16 or piece % 16:
        both = jnp.zeros((2, units, width), jnp.bfloat16)
        for index in range(count):
            pair = jnp.stack([weights[index], weights[count + index]])
            both = lax.dynamic_update_slice(both, pair, (0, 0, weight_ids[index] * depth))
        rows = jnp.zeros((tokens, width), jnp.bfloat16)
        for index in range(pieces):
            for half in range(halves):
                at = (half * pieces + row_ids[index]) * piece
                rows = lax.dynamic_update_slice(rows, rows_in[index][half * piece:(half + 1) * piece], (at, 0))
        gate = lax.dot_general(both[0], rows, NT, preferred_element_type=jnp.float32)
        up = lax.dot_general(both[1], rows, NT, preferred_element_type=jnp.float32)
        return jnp.split((jax.nn.silu(gate) * up).astype(jnp.bfloat16), outs, axis=1)
    ids = jnp.stack([jnp.asarray(i, jnp.int32) for i in list(weight_ids) + list(row_ids)])
    anywhere = pl.BlockSpec(memory_space=pl.ANY)
    return pl.pallas_call(
        lambda *refs: mlp_kernel(count, pieces, halves, outs, *refs),
        out_shape=[jax.ShapeDtypeStruct((units, tokens // outs), jnp.bfloat16)] * outs,
        in_specs=[pl.BlockSpec(memory_space=pltpu.SMEM)] + [anywhere] * (2 * count + pieces),
        out_specs=[pl.BlockSpec(memory_space=pltpu.VMEM)] * outs,
        scratch_shapes=[
            pltpu.VMEM((count, units, depth), jnp.bfloat16),
            pltpu.VMEM((count, units, depth), jnp.bfloat16),
            pltpu.VMEM((tokens, width), jnp.bfloat16),
            pltpu.VMEM((2, units, tokens), jnp.float32),
            pltpu.SemaphoreType.DMA((2, count, 3 if units % 48 == 0 else 1)),
            pltpu.SemaphoreType.DMA((pieces, halves)),
        ],
        compiler_params=pltpu.CompilerParams(vmem_limit_bytes=60 * 2**20),
        cost_estimate=pl.CostEstimate(flops=10**8, bytes_accessed=2**16, transcendentals=0),
        name="mlp_block",
    )(ids, *weights, *rows_in)


def after(value, *before):
    return lax.optimization_barrier((value,) + before)[0]


def shards(q_pre, k_pre, v_pre, q_bias, k_bias, v_bias, segment_ids, lengths, page_table, w_out, residual,
           norm_gain, w_gate, w_up):
    me_req = lax.axis_index("req")
    me_mp = lax.axis_index("mp")
    n_req = lax.axis_size("req")
    n_mp = lax.axis_size("mp")
    n_y = n_req // N_Z
    n_x = n_mp // CORES
    z = me_req // n_y
    y = me_req % n_y
    x = me_mp // CORES
    core = me_mp % CORES

    def along_z(value, moves):
        return lax.ppermute(value, "req", [(a * n_y + c, b * n_y + c) for a, b in moves for c in range(n_y)])

    def turn_z(value, shift):
        return along_z(value, [(a, (a + shift) % N_Z) for a in range(N_Z)])

    def along_y(value):
        return [
            lax.ppermute(
                value, "req", [(a * n_y + b, a * n_y + (b + step) % n_y) for a in range(N_Z) for b in range(n_y)]
            )
            for step in range(1, n_y)
        ]

    def along_x(value):
        return [
            lax.ppermute(
                value,
                "mp",
                [(a * CORES + b, (a + step) % n_x * CORES + b) for a in range(n_x) for b in range(CORES)],
            )
            for step in range(1, n_x)
        ]

    def across_cores(value):
        return lax.ppermute(
            value, "mp", [(a * CORES + b, a * CORES + 1 - b) for a in range(n_x) for b in range(CORES)]
        )

    units_all, depth = w_gate.shape[1], w_gate.shape[0]
    units = units_all // N_Z

    def share(weight_t, shift):
        return lax.dynamic_slice(weight_t, ((z + shift) % N_Z * units, 0), (units, depth))

    def source_ids(shift):
        source_z = (z - shift) % N_Z
        return [source_z * n_y + (y - step) % n_y for step in range(n_y)]

    gate_t, up_t = w_gate.T, w_up.T
    gate_2 = share(gate_t, 2)
    gate_t, up_t, gate_2, q_pre, segment_ids = lax.optimization_barrier((gate_t, up_t, gate_2, q_pre, segment_ids))
    gate_2 = turn_z(gate_2, 2)

    rows = q_pre.shape[0]
    kv_heads = k_pre.shape[1] // HD
    own_lens = lax.dynamic_index_in_dim(lengths, me_req, 0, keepdims=False)
    own_pages = lax.dynamic_index_in_dim(page_table, me_req, 0, keepdims=False)
    own_owner = own_pages // REQS
    starts = jnp.cumsum(own_lens) - own_lens
    alive = segment_ids >= 0
    req_idx = jnp.clip(segment_ids - me_req * REQS, 0, REQS - 1)
    hit = req_idx[:, None] == jnp.arange(REQS)[None, :]
    row_start = jnp.sum(jnp.where(hit, starts[None, :], 0), axis=1)
    row_owner = jnp.sum(jnp.where(hit, own_owner[None, :], 0), axis=1)
    row_pos = jnp.arange(rows, dtype=jnp.int32) - row_start
    slots = jnp.where(alive, row_owner * PAGE + row_pos, -1)
    cosine, sine = rope_tables(row_pos.astype(jnp.float32))
    run = rows // n_mp // 2
    order = []
    for group in range(2 * n_mp):
        half, device = divmod(group, n_mp)
        order.append((device % CORES * n_x + device // CORES) * 2 + half)
    attended, kv_send = attention(
        q_pre, k_pre, v_pre, q_bias, k_bias, v_bias, cosine, sine, segment_ids, slots, n_req * PAGE, order
    )
    attended = attended.reshape(CORES, n_x * 2 * run, attended.shape[1])

    def project(which):
        picked = lax.dynamic_index_in_dim(attended, which, 0, keepdims=False)
        return jnp.dot(picked, w_out, preferred_element_type=jnp.float32).astype(jnp.bfloat16)

    kept, given = project(core), project(1 - core)
    up_2, gate_0, up_0, gate_2, kept, given = lax.optimization_barrier(
        (share(up_t, 2), share(gate_t, 0), share(up_t, 0), gate_2, kept, given)
    )
    up_2 = turn_z(up_2, 2)
    gate_0_y, up_0_y = along_y(gate_0), along_y(up_0)
    sibling = across_cores(given)
    width = sibling.shape[1]
    gate_1, up_2, gate_0_y, up_0_y, gate_2, sibling = lax.optimization_barrier(
        (share(gate_t, 1), up_2, gate_0_y, up_0_y, gate_2, sibling)
    )
    gate_1 = turn_z(gate_1, 1)
    gate_2_y = along_y(gate_2)
    pair = (kept.astype(jnp.float32) + sibling.astype(jnp.float32)).reshape(n_x, 2 * run, width)
    summed = lax.dynamic_index_in_dim(pair, x, 0, keepdims=False)
    outgoing = [
        lax.dynamic_index_in_dim(pair, (x + step) % n_x, 0, keepdims=False).astype(jnp.bfloat16)
        for step in range(1, n_x)
    ]
    gate_3, up_3, gate_1, up_2, gate_2_y, outgoing = lax.optimization_barrier(
        (share(gate_t, 3), share(up_t, 3), gate_1, up_2, gate_2_y, outgoing)
    )
    gate_3, up_3 = turn_z(gate_3, 3), turn_z(up_3, 3)
    up_2_y = along_y(up_2)
    gate_1_y = along_y(gate_1)
    incoming = [
        lax.ppermute(
            outgoing[step - 1],
            "mp",
            [(a * CORES + b, (a + step) % n_x * CORES + b) for a in range(n_x) for b in range(CORES)],
        )
        for step in range(1, n_x)
    ]
    up_1, gate_3, up_3, gate_1_y, up_2_y, incoming = lax.optimization_barrier(
        (share(up_t, 1), gate_3, up_3, gate_1_y, up_2_y, incoming)
    )
    up_1 = turn_z(up_1, 1)
    gate_3_y = along_y(gate_3)
    residual_rows = jnp.concatenate(
        [
            lax.dynamic_slice(residual, (me_mp * run, 0), (run, width)),
            lax.dynamic_slice(residual, (rows // 2 + me_mp * run, 0), (run, width)),
        ]
    )
    for other in incoming:
        summed = summed + other.astype(jnp.float32)
    state = residual_rows.astype(jnp.float32) + summed
    scale = lax.rsqrt(jnp.mean(state * state, axis=-1, keepdims=True) + EPS)
    normed = (state * scale * norm_gain).astype(jnp.bfloat16)
    near, up_1, gate_3_y = lax.optimization_barrier((normed, up_1, gate_3_y))

    row_ids = [(x - step) % n_x * CORES + core for step in range(n_x)]
    row_ids += [(x - step) % n_x * CORES + 1 - core for step in range(n_x)]
    flip = [[(a, a ^ by) for a in range(N_Z)] for by in range(N_Z)]
    middle = [(1, 2), (2, 1)]
    outward = [(1, 0), (2, 3)]
    at_end = (z == 0) | (z == N_Z - 1)
    up_1_y, up_3_y = along_y(up_1), along_y(up_3)
    near_x = along_x(near)
    next_1, middle_1 = along_z(near, flip[1]), along_z(near, middle)
    next_1, middle_1, up_1_y, up_3_y, near_x = lax.optimization_barrier((next_1, middle_1, up_1_y, up_3_y, near_x))
    next_2e, next_2m = along_z(middle_1, outward), along_z(next_1, middle)
    next_1_x = along_x(next_1)

    gates = [gate_0, *gate_0_y, gate_2, *gate_2_y, gate_1, *gate_1_y, gate_3, *gate_3_y]
    ups = [up_0, *up_0_y, up_2, *up_2_y, up_1, *up_1_y, up_3, *up_3_y]
    weights = gates + ups
    weight_ids = [i for shift in (0, 2, 1, 3) for i in source_ids(shift)]

    def shared(block, block_x):
        return [block, *block_x, *[across_cores(p) for p in (block, *block_x)]]

    def work(pieces, outs=1):
        done = mlp_block(weights, weight_ids, pieces, row_ids, pieces[0].shape[0] // run, outs)
        return done[0] if outs == 1 else list(done)

    pieces_0 = shared(near, near_x)
    next_2e, next_2m, next_1_x, pieces_0 = lax.optimization_barrier((next_2e, next_2m, next_1_x, pieces_0))
    next_3 = along_z(next_2m, outward)
    next_2 = jnp.where(at_end, next_2e, next_2m)
    next_2_x = along_x(next_2)
    hidden_0 = work(pieces_0)
    hidden_0, kv_send = lax.optimization_barrier((hidden_0, kv_send))
    kv_in = lax.all_to_all(
        kv_send.reshape(n_req, PAGE, 2 * kv_heads * HD), "req", split_axis=0, concat_axis=0, tiled=True
    )
    hidden_1 = work(shared(next_1, next_1_x))
    next_3, next_2_x, hidden_0, hidden_1 = lax.optimization_barrier((next_3, next_2_x, hidden_0, hidden_1))
    next_3a = jnp.where(at_end, next_3[:run], middle_1[:run])
    next_3a, next_3 = lax.optimization_barrier((next_3a, next_3))
    next_3a_x = along_x(next_3a)
    next_3b = jnp.where(at_end, next_3[run:], middle_1[run:])
    hidden_2 = work(shared(next_2, next_2_x), 2)
    back_1 = along_z(hidden_1, flip[1])
    next_3b, next_3a_x, hidden_2, back_1, kv_in = lax.optimization_barrier(
        (next_3b, next_3a_x, hidden_2, back_1, kv_in)
    )
    next_3b_x = along_x(next_3b)
    back_2 = [along_z(half, flip[2]) for half in hidden_2]
    hidden_3a = work(shared(next_3a, next_3a_x))
    next_3b_x, hidden_3a, back_2[0] = lax.optimization_barrier((next_3b_x, hidden_3a, back_2[0]))
    back_3a = along_z(hidden_3a, flip[3])
    hidden_3b, back_2[1], kv_in = lax.optimization_barrier((work(shared(next_3b, next_3b_x)), back_2[1], kv_in))
    back_3b = along_z(hidden_3b, flip[3])
    mine = page_table[None] == (me_req * REQS + jnp.arange(REQS, dtype=jnp.int32))[:, None, None]
    sources = jnp.sum(jnp.where(mine, jnp.arange(n_req, dtype=jnp.int32)[None, :, None], 0), axis=(1, 2))
    cache_out = write_cache(sources.astype(jnp.int32), kv_in, kv_heads)
    hidden_t = jnp.zeros((units_all, rows), jnp.bfloat16)
    for by, at, done in (
        (0, 0, hidden_0),
        (1, 0, back_1),
        (2, 0, back_2[0]),
        (2, rows // 2, back_2[1]),
        (3, 0, back_3a),
        (3, rows // 2, back_3b),
    ):
        hidden_t = lax.dynamic_update_slice(hidden_t, done, ((z ^ by) * units, at))
    return hidden_t.T, cache_out


def solution(mesh):
    in_specs = (
        P("req", "mp"),
        P("req", "mp"),
        P("req", "mp"),
        P("mp"),
        P("mp"),
        P("mp"),
        P("req"),
        P(),
        P(),
        P("mp", None),
        P("req", None),
        P(),
        P("req", "mp"),
        P("req", "mp"),
    )
    out_specs = (P("req", "mp"), P("req", "mp", None, None))
    return jax.shard_map(shards, mesh=mesh, in_specs=in_specs, out_specs=out_specs, check_vma=False)
```

```python
import math

import jax
import jax.numpy as jnp
from jax import lax
from jax.experimental import pallas as pl
from jax.experimental.pallas import tpu as pltpu
from jax.sharding import PartitionSpec as P

HD = 128
PAGE = 128
REQS = 4
CORES = 2
N_Z = 4
THETA = 1000000.0
EPS = 1e-06
NT = (((1,), (1,)), ((), ()))


def rope_tables(positions):
    half_dim = HD // 2
    frequencies = THETA ** (-jnp.arange(half_dim, dtype=jnp.float32) * (2.0 / HD))
    angles = positions[:, None] * frequencies[None, :]
    cosine = jnp.cos(angles)
    sine = jnp.sin(angles)
    return jnp.concatenate([cosine, cosine], axis=-1), jnp.concatenate([-sine, sine], axis=-1)


def attention_kernel(order, q_ref, k_ref, v_ref, qb_ref, kb_ref, vb_ref, cos_ref, sin_ref, segc_ref, segr_ref,
                     slot_ref, out_ref, send_ref, q_buf, k_buf, v_buf, kv_buf):
    rows = q_ref.shape[0]
    kv_heads = k_ref.shape[1] // HD
    q_heads = q_ref.shape[1] // HD
    group = q_heads // kv_heads
    live = segc_ref[...] >= 0
    cosine = cos_ref[...]
    sine = sin_ref[...]

    def turned(source, bias, head):
        cols = slice(head * HD, (head + 1) * HD)
        raw = source[:, cols].astype(jnp.float32) + bias[:, cols]
        return jnp.where(live, raw * cosine + pltpu.roll(raw, HD // 2, 1) * sine, 0.0).astype(jnp.bfloat16)

    for head in range(q_heads):
        q_buf[:, head * HD:(head + 1) * HD] = turned(q_ref, qb_ref, head)
    for head in range(kv_heads):
        cols = slice(head * HD, (head + 1) * HD)
        key = turned(k_ref, kb_ref, head)
        value = jnp.where(live, v_ref[:, cols].astype(jnp.float32) + vb_ref[:, cols], 0.0).astype(jnp.bfloat16)
        k_buf[:, cols] = key
        v_buf[:, cols] = value
        kv_buf[:, 2 * head * HD:(2 * head + 1) * HD] = key
        kv_buf[:, (2 * head + 1) * HD:(2 * head + 2) * HD] = value
    slots = slot_ref[...]
    for part in range(send_ref.shape[0] // rows):
        wanted = lax.broadcasted_iota(jnp.int32, (rows, rows), 0) + part * rows
        pick = jnp.where(wanted == slots, 1.0, 0.0).astype(jnp.bfloat16)
        send_ref[part * rows:(part + 1) * rows, :] = jnp.dot(
            pick, kv_buf[...], preferred_element_type=jnp.float32
        ).astype(jnp.bfloat16)
    scale = 1.0 / math.sqrt(HD)
    tile = PAGE
    for start in range(0, rows, tile):
        low = max(0, start - tile)
        high = start + tile
        seg_q = segc_ref[start:high, :]
        seg_k = segr_ref[:, low:high]
        row_at = lax.broadcasted_iota(jnp.int32, (tile, high - low), 0) + start
        col_at = lax.broadcasted_iota(jnp.int32, (tile, high - low), 1) + low
        allowed = (seg_q == seg_k) & (seg_k >= 0) & (col_at <= row_at)
        for head in range(q_heads):
            kv = head // group
            kv_cols = slice(kv * HD, (kv + 1) * HD)
            scores = lax.dot_general(
                q_buf[start:high, head * HD:(head + 1) * HD], k_buf[low:high, kv_cols], NT,
                preferred_element_type=jnp.float32,
            ) * scale
            row_max = jnp.max(jnp.where(allowed, scores, -1e30), axis=-1, keepdims=True)
            weights = jnp.where(allowed, jnp.exp(scores - row_max), 0.0)
            total = jnp.sum(weights, axis=-1, keepdims=True)
            probs = (weights / jnp.where(total > 0.0, total, 1.0)).astype(jnp.bfloat16)
            mixed = jnp.dot(
                probs, v_buf[low:high, kv_cols], preferred_element_type=jnp.float32
            ).astype(jnp.bfloat16)
            size = rows // len(order)
            for at in range(0, tile, size):
                to = order[(start + at) // size] * size
                out_ref[to:to + size, head * HD:(head + 1) * HD] = mixed[at:at + size]


def attention(q_pre, k_pre, v_pre, q_bias, k_bias, v_bias, cosine, sine, segs, slots, slot_count, order):
    rows, q_cols = q_pre.shape
    kv_cols = k_pre.shape[1]
    vmem = pl.BlockSpec(memory_space=pltpu.VMEM)
    return pl.pallas_call(
        lambda *refs: attention_kernel(order, *refs),
        out_shape=(
            jax.ShapeDtypeStruct((rows, q_cols), jnp.bfloat16),
            jax.ShapeDtypeStruct((slot_count, 2 * kv_cols), jnp.bfloat16),
        ),
        in_specs=[vmem] * 11,
        out_specs=(vmem, vmem),
        scratch_shapes=[
            pltpu.VMEM((rows, q_cols), jnp.bfloat16),
            pltpu.VMEM((rows, kv_cols), jnp.bfloat16),
            pltpu.VMEM((rows, kv_cols), jnp.bfloat16),
            pltpu.VMEM((rows, 2 * kv_cols), jnp.bfloat16),
        ],
        compiler_params=pltpu.CompilerParams(vmem_limit_bytes=32 * 2**20),
        cost_estimate=pl.CostEstimate(flops=10**8, bytes_accessed=2**16, transcendentals=0),
        name="attention",
    )(q_pre, k_pre, v_pre, q_bias[None], k_bias[None], v_bias[None], cosine, sine, segs[:, None], segs[None],
      slots[None])


def cache_kernel(source_ref, in_ref, out_ref):
    for page in range(out_ref.shape[0]):
        for head in range(out_ref.shape[1]):
            out_ref[page, head] = in_ref[source_ref[page], :, head * 2 * HD:(head + 1) * 2 * HD]


def write_cache(sources, pages_in, kv_heads):
    vmem = pl.BlockSpec(memory_space=pltpu.VMEM)
    return pl.pallas_call(
        cache_kernel,
        out_shape=jax.ShapeDtypeStruct((REQS, kv_heads, PAGE, 2 * HD), jnp.bfloat16),
        in_specs=[pl.BlockSpec(memory_space=pltpu.SMEM), vmem],
        out_specs=vmem,
        cost_estimate=pl.CostEstimate(flops=0, bytes_accessed=2**16, transcendentals=0),
        name="write_cache",
    )(sources, pages_in)


def mlp_kernel(count, pieces, halves, outs, ids_ref, *refs):
    weights = (refs[:count], refs[count:2 * count])
    rows_in = refs[2 * count:2 * count + pieces]
    out_refs = refs[2 * count + pieces:2 * count + pieces + outs]
    gate_buf, up_buf, row_buf, acc, weight_sems, row_sems = refs[2 * count + pieces + outs:]
    units, depth = weights[0][0].shape
    parts = weight_sems.shape[2]
    piece = rows_in[0].shape[0] // halves
    first, second = [], []
    for index in range(pieces):
        for half in range(halves):
            at = pl.multiple_of((half * pieces + ids_ref[count + index]) * piece, piece)
            first.append(
                pltpu.make_async_copy(
                    rows_in[index].at[pl.ds(half * piece, piece), :],
                    row_buf.at[pl.ds(at, piece), :],
                    row_sems.at[index, half],
                )
            )
    for index in range(count):
        for which, buf in ((0, gate_buf), (1, up_buf)):
            for part in range(parts):
                some = pl.ds(part * (units // parts), units // parts)
                second.append(
                    pltpu.make_async_copy(
                        weights[which][index].at[some, :], buf.at[index, some, :], weight_sems.at[which, index, part]
                    )
                )
    for copy in first + second:
        copy.start()
    for copy in first:
        copy.wait()
    tokens, span = row_buf.shape[0], out_refs[0].shape[1]
    tile = min(256, span)
    for index in range(count):
        for copy in second[2 * parts * index:2 * parts * (index + 1)]:
            copy.wait()
        at = pl.multiple_of(ids_ref[index] * depth, depth)
        for start in range(0, tokens, tile):
            block = row_buf[start:start + tile, pl.ds(at, depth)]
            for which, buf in ((0, gate_buf), (1, up_buf)):
                term = lax.dot_general(buf[index], block, NT, preferred_element_type=jnp.float32)
                if index:
                    term = acc[which, :, start:start + tile] + term
                acc[which, :, start:start + tile] = term
    for start in range(0, tokens, tile):
        gate = acc[0, :, start:start + tile]
        up = acc[1, :, start:start + tile]
        at = start % span
        out_refs[start // span][:, at:at + tile] = (gate / (1.0 + jnp.exp(-gate)) * up).astype(jnp.bfloat16)


def mlp_block(weights, weight_ids, rows_in, row_ids, halves, outs):
    count, pieces = len(weight_ids), len(row_ids)
    units, depth = weights[0].shape
    width = rows_in[0].shape[1]
    piece = rows_in[0].shape[0] // halves
    tokens = piece * pieces * halves
    if depth % 128 or units % 16 or piece % 16:
        both = jnp.zeros((2, units, width), jnp.bfloat16)
        for index in range(count):
            pair = jnp.stack([weights[index], weights[count + index]])
            both = lax.dynamic_update_slice(both, pair, (0, 0, weight_ids[index] * depth))
        rows = jnp.zeros((tokens, width), jnp.bfloat16)
        for index in range(pieces):
            for half in range(halves):
                at = (half * pieces + row_ids[index]) * piece
                rows = lax.dynamic_update_slice(rows, rows_in[index][half * piece:(half + 1) * piece], (at, 0))
        gate = lax.dot_general(both[0], rows, NT, preferred_element_type=jnp.float32)
        up = lax.dot_general(both[1], rows, NT, preferred_element_type=jnp.float32)
        return jnp.split((jax.nn.silu(gate) * up).astype(jnp.bfloat16), outs, axis=1)
    ids = jnp.stack([jnp.asarray(i, jnp.int32) for i in list(weight_ids) + list(row_ids)])
    anywhere = pl.BlockSpec(memory_space=pl.ANY)
    return pl.pallas_call(
        lambda *refs: mlp_kernel(count, pieces, halves, outs, *refs),
        out_shape=[jax.ShapeDtypeStruct((units, tokens // outs), jnp.bfloat16)] * outs,
        in_specs=[pl.BlockSpec(memory_space=pltpu.SMEM)] + [anywhere] * (2 * count + pieces),
        out_specs=[pl.BlockSpec(memory_space=pltpu.VMEM)] * outs,
        scratch_shapes=[
            pltpu.VMEM((count, units, depth), jnp.bfloat16),
            pltpu.VMEM((count, units, depth), jnp.bfloat16),
            pltpu.VMEM((tokens, width), jnp.bfloat16),
            pltpu.VMEM((2, units, tokens), jnp.float32),
            pltpu.SemaphoreType.DMA((2, count, 1)),
            pltpu.SemaphoreType.DMA((pieces, halves)),
        ],
        compiler_params=pltpu.CompilerParams(vmem_limit_bytes=60 * 2**20),
        cost_estimate=pl.CostEstimate(flops=10**8, bytes_accessed=2**16, transcendentals=0),
        name="mlp_block",
    )(ids, *weights, *rows_in)


def after(value, *before):
    return lax.optimization_barrier((value,) + before)[0]


def shards(q_pre, k_pre, v_pre, q_bias, k_bias, v_bias, segment_ids, lengths, page_table, w_out, residual,
           norm_gain, w_gate, w_up):
    me_req = lax.axis_index("req")
    me_mp = lax.axis_index("mp")
    n_req = lax.axis_size("req")
    n_mp = lax.axis_size("mp")
    n_y = n_req // N_Z
    n_x = n_mp // CORES
    z = me_req // n_y
    y = me_req % n_y
    x = me_mp // CORES
    core = me_mp % CORES

    def along_z(value, moves):
        return lax.ppermute(value, "req", [(a * n_y + c, b * n_y + c) for a, b in moves for c in range(n_y)])

    def turn_z(value, shift):
        return along_z(value, [(a, (a + shift) % N_Z) for a in range(N_Z)])

    def along_y(value):
        return [
            lax.ppermute(
                value, "req", [(a * n_y + b, a * n_y + (b + step) % n_y) for a in range(N_Z) for b in range(n_y)]
            )
            for step in range(1, n_y)
        ]

    def along_x(value):
        return [
            lax.ppermute(
                value,
                "mp",
                [(a * CORES + b, (a + step) % n_x * CORES + b) for a in range(n_x) for b in range(CORES)],
            )
            for step in range(1, n_x)
        ]

    def across_cores(value):
        return lax.ppermute(
            value, "mp", [(a * CORES + b, a * CORES + 1 - b) for a in range(n_x) for b in range(CORES)]
        )

    units_all, depth = w_gate.shape[1], w_gate.shape[0]
    units = units_all // N_Z

    def share(weight_t, shift):
        return lax.dynamic_slice(weight_t, ((z + shift) % N_Z * units, 0), (units, depth))

    def source_ids(shift):
        source_z = (z - shift) % N_Z
        return [source_z * n_y + (y - step) % n_y for step in range(n_y)]

    gate_t, up_t = w_gate.T, w_up.T
    gate_2 = share(gate_t, 2)
    gate_t, up_t, gate_2, q_pre, segment_ids = lax.optimization_barrier((gate_t, up_t, gate_2, q_pre, segment_ids))
    gate_2 = turn_z(gate_2, 2)

    rows = q_pre.shape[0]
    kv_heads = k_pre.shape[1] // HD
    own_lens = lax.dynamic_index_in_dim(lengths, me_req, 0, keepdims=False)
    own_pages = lax.dynamic_index_in_dim(page_table, me_req, 0, keepdims=False)
    own_owner = own_pages // REQS
    starts = jnp.cumsum(own_lens) - own_lens
    alive = segment_ids >= 0
    req_idx = jnp.clip(segment_ids - me_req * REQS, 0, REQS - 1)
    hit = req_idx[:, None] == jnp.arange(REQS)[None, :]
    row_start = jnp.sum(jnp.where(hit, starts[None, :], 0), axis=1)
    row_owner = jnp.sum(jnp.where(hit, own_owner[None, :], 0), axis=1)
    row_pos = jnp.arange(rows, dtype=jnp.int32) - row_start
    slots = jnp.where(alive, row_owner * PAGE + row_pos, -1)
    cosine, sine = rope_tables(row_pos.astype(jnp.float32))
    run = rows // n_mp // 2
    order = []
    for group in range(2 * n_mp):
        half, device = divmod(group, n_mp)
        order.append((device % CORES * n_x + device // CORES) * 2 + half)
    attended, kv_send = attention(
        q_pre, k_pre, v_pre, q_bias, k_bias, v_bias, cosine, sine, segment_ids, slots, n_req * PAGE, order
    )
    attended = attended.reshape(CORES, n_x * 2 * run, attended.shape[1])

    def project(which):
        picked = lax.dynamic_index_in_dim(attended, which, 0, keepdims=False)
        return jnp.dot(picked, w_out, preferred_element_type=jnp.float32).astype(jnp.bfloat16)

    mine = page_table[None] == (me_req * REQS + jnp.arange(REQS, dtype=jnp.int32))[:, None, None]
    sources = jnp.sum(jnp.where(mine, jnp.arange(n_req, dtype=jnp.int32)[None, :, None], 0), axis=(1, 2))
    kept, given = project(core), project(1 - core)
    up_2, gate_0, up_0, gate_2, kept, given, sources = lax.optimization_barrier(
        (share(up_t, 2), share(gate_t, 0), share(up_t, 0), gate_2, kept, given, sources)
    )
    up_2 = turn_z(up_2, 2)
    gate_0_y, up_0_y = along_y(gate_0), along_y(up_0)
    sibling = across_cores(given)
    width = sibling.shape[1]
    gate_1, up_2, gate_0_y, up_0_y, gate_2, sibling = lax.optimization_barrier(
        (share(gate_t, 1), up_2, gate_0_y, up_0_y, gate_2, sibling)
    )
    gate_1 = turn_z(gate_1, 1)
    gate_2_y = along_y(gate_2)
    pair = (kept.astype(jnp.float32) + sibling.astype(jnp.float32)).reshape(n_x, 2 * run, width)
    summed = lax.dynamic_index_in_dim(pair, x, 0, keepdims=False)
    outgoing = [
        lax.dynamic_index_in_dim(pair, (x + step) % n_x, 0, keepdims=False).astype(jnp.bfloat16)
        for step in range(1, n_x)
    ]
    gate_3, up_3, gate_1, up_2, gate_2_y = lax.optimization_barrier(
        (share(gate_t, 3), share(up_t, 3), gate_1, up_2, gate_2_y)
    )
    gate_3, up_3 = turn_z(gate_3, 3), turn_z(up_3, 3)
    up_2_y = along_y(up_2)
    gate_1_y = along_y(gate_1)
    incoming = [
        lax.ppermute(
            outgoing[step - 1],
            "mp",
            [(a * CORES + b, (a + step) % n_x * CORES + b) for a in range(n_x) for b in range(CORES)],
        )
        for step in range(1, n_x)
    ]
    up_1, gate_3, up_3, gate_1_y, up_2_y, incoming = lax.optimization_barrier(
        (share(up_t, 1), gate_3, up_3, gate_1_y, up_2_y, incoming)
    )
    up_1 = turn_z(up_1, 1)
    gate_3_y = along_y(gate_3)
    residual_rows = jnp.concatenate(
        [
            lax.dynamic_slice(residual, (me_mp * run, 0), (run, width)),
            lax.dynamic_slice(residual, (rows // 2 + me_mp * run, 0), (run, width)),
        ]
    )
    for other in incoming:
        summed = summed + other.astype(jnp.float32)
    state = residual_rows.astype(jnp.float32) + summed
    scale = lax.rsqrt(jnp.mean(state * state, axis=-1, keepdims=True) + EPS)
    normed = (state * scale * norm_gain).astype(jnp.bfloat16)
    near, up_1, gate_3_y = lax.optimization_barrier((normed, up_1, gate_3_y))

    row_ids = [(x - step) % n_x * CORES + core for step in range(n_x)]
    row_ids += [(x - step) % n_x * CORES + 1 - core for step in range(n_x)]
    flip = [[(a, a ^ by) for a in range(N_Z)] for by in range(N_Z)]
    middle = [(1, 2), (2, 1)]
    outward = [(1, 0), (2, 3)]
    at_end = (z == 0) | (z == N_Z - 1)
    up_1_y, up_3_y = along_y(up_1), along_y(up_3)
    near_x = along_x(near)
    next_1, middle_1 = along_z(near, flip[1]), along_z(near, middle)
    next_1, middle_1, up_1_y, up_3_y, near_x = lax.optimization_barrier((next_1, middle_1, up_1_y, up_3_y, near_x))
    next_2e, next_2m = along_z(middle_1, outward), along_z(next_1, middle)
    next_1_x = along_x(next_1)

    gates = [gate_0, *gate_0_y, gate_2, *gate_2_y, gate_1, *gate_1_y, gate_3, *gate_3_y]
    ups = [up_0, *up_0_y, up_2, *up_2_y, up_1, *up_1_y, up_3, *up_3_y]
    weights = gates + ups
    weight_ids = [i for shift in (0, 2, 1, 3) for i in source_ids(shift)]

    def shared(block, block_x):
        return [block, *block_x, *[across_cores(p) for p in (block, *block_x)]]

    def work(pieces, outs=1):
        done = mlp_block(weights, weight_ids, pieces, row_ids, pieces[0].shape[0] // run, outs)
        return done[0] if outs == 1 else list(done)

    pieces_0 = shared(near, near_x)
    next_2e, next_2m, next_1_x, pieces_0 = lax.optimization_barrier((next_2e, next_2m, next_1_x, pieces_0))
    next_3 = along_z(next_2m, outward)
    next_2 = jnp.where(at_end, next_2e, next_2m)
    next_2_x = along_x(next_2)
    hidden_0 = work(pieces_0)
    hidden_0, kv_send = lax.optimization_barrier((hidden_0, kv_send))
    kv_in = lax.all_to_all(
        kv_send.reshape(n_req, PAGE, 2 * kv_heads * HD), "req", split_axis=0, concat_axis=0, tiled=True
    )
    hidden_1 = work(shared(next_1, next_1_x))
    next_3, next_2_x, hidden_0, hidden_1 = lax.optimization_barrier((next_3, next_2_x, hidden_0, hidden_1))
    next_3a = jnp.where(at_end, next_3[:run], middle_1[:run])
    next_3a, next_3 = lax.optimization_barrier((next_3a, next_3))
    next_3a_x = along_x(next_3a)
    next_3b = jnp.where(at_end, next_3[run:], middle_1[run:])
    hidden_2 = work(shared(next_2, next_2_x), 2)
    back_1 = along_z(hidden_1, flip[1])
    next_3b, next_3a_x, hidden_2, back_1, kv_in = lax.optimization_barrier(
        (next_3b, next_3a_x, hidden_2, back_1, kv_in)
    )
    next_3b_x = along_x(next_3b)
    back_2 = [along_z(half, flip[2]) for half in hidden_2]
    hidden_3a = work(shared(next_3a, next_3a_x))
    next_3b_x, hidden_3a, back_2[0] = lax.optimization_barrier((next_3b_x, hidden_3a, back_2[0]))
    back_3a = along_z(hidden_3a, flip[3])
    hidden_3b, back_2[1], kv_in = lax.optimization_barrier((work(shared(next_3b, next_3b_x)), back_2[1], kv_in))
    back_3b = along_z(hidden_3b, flip[3])
    cache_out = write_cache(sources.astype(jnp.int32), kv_in, kv_heads)
    hidden_t = jnp.zeros((units_all, rows), jnp.bfloat16)
    for by, at, done in (
        (0, 0, hidden_0),
        (1, 0, back_1),
        (2, 0, back_2[0]),
        (2, rows // 2, back_2[1]),
        (3, 0, back_3a),
        (3, rows // 2, back_3b),
    ):
        hidden_t = lax.dynamic_update_slice(hidden_t, done, ((z ^ by) * units, at))
    return hidden_t.T, cache_out


def solution(mesh):
    in_specs = (
        P("req", "mp"),
        P("req", "mp"),
        P("req", "mp"),
        P("mp"),
        P("mp"),
        P("mp"),
        P("req"),
        P(),
        P(),
        P("mp", None),
        P("req", None),
        P(),
        P("req", "mp"),
        P("req", "mp"),
    )
    out_specs = (P("req", "mp"), P("req", "mp", None, None))
    return jax.shard_map(shards, mesh=mesh, in_specs=in_specs, out_specs=out_specs, check_vma=False)
```
